256 devices in a mesh: rows: 64 (over z, x, core), sub: 4 (over y).
Axes of the slice: x: 4, y: 4, z: 8, core: 2. Of those that a mesh axis runs over, the one named last changes fastest.
Arguments:
- embeddings: float32 [131072, 256], P('rows'), may hold values from -6 to 6
- start_vectors: float32 [131072, 64], P('rows'), may hold values from -6 to 6
- pairs: int32 [512, 2], P('rows'), may hold values from -1 to 127, as said below
Outputs:
- vectors: float32 [131072, 64], P('rows')
The draws below stay inside these ranges and needn't reach their ends.
Inputs may be any that keep to these rules, and one draw needn't show every extreme that they name: Slot s of row group g is entry g * 8 + s. A group's pairs have row block 2g or 2g+1 (owned by the group) and column block j with row block <= j <= 2g+3 and j < 128; no pair is listed twice; both diagonal pairs (2g, 2g) and (2g+1, 2g+1) are listed; used slots come first, empty slots hold -1 in both entries; at most 7 slots of a group are used and group 0 uses 7.
All inputs are finite; a program needn't handle non-finite values.
Results may differ from the reference program's by a relative error of at most 0.0003.
Values sent between devices are 32-bit elements; how exact they have to be, the bound alone decides.
No kernel may reach another device: no remote copies, remote signals or barrier semaphores. Data moves between devices by JAX's collectives and lax.ppermute only.
A program may use at most 64 MiB of HBM per device.

```python
import math
import jax
import jax.numpy as jnp
from jax import lax

E = 256
K = 64
BLOCK = 1024
BLK_DEV = 2
GSLOTS = 8
ITERS = 2
NBLK = 128
NROWS = 131072


def draw_embeddings(key, part):
    per_block = max(BLOCK // 48, 1)
    clusters = NBLK * per_block
    key_pick, key_centre, key_noise = jax.random.split(jax.random.fold_in(key, 23), 3)
    row_ids = jnp.arange(NROWS, dtype=jnp.int32)
    block_of = row_ids // BLOCK
    pick = jax.random.randint(key_pick, (NROWS,), 0, 2 * per_block)
    ident = ((block_of * per_block + pick) % clusters).astype(jnp.int32)
    centres = jax.random.normal(key_centre, (clusters, E), jnp.float32) * math.sqrt(160.0 / E)
    noise = jax.random.normal(key_noise, (NROWS, E), jnp.float32) * math.sqrt(32.0 / E)
    return jnp.clip(jnp.take(centres, ident, axis=0) + noise, -6.0, 6.0)


def draw_pairs(key, part):
    groups = NBLK // BLK_DEV
    base = jnp.arange(groups, dtype=jnp.int32) * BLK_DEV
    row_offsets = jnp.array([0, 0, 0, 0, 1, 1, 1], jnp.int32)
    col_offsets = jnp.array([0, 1, 2, 3, 1, 2, 3], jnp.int32)
    row_ids = base[:, None] + row_offsets[None, :]
    col_ids = base[:, None] + col_offsets[None, :]
    inside = col_ids < NBLK
    diagonal = (row_offsets == col_offsets)[None, :]
    key_level, key_coin = jax.random.split(jax.random.fold_in(key, 11))
    level = jax.random.randint(key_level, (groups, 1), 0, 5)
    coin = jax.random.randint(key_coin, (groups, 7), 0, 4)
    first = (jnp.arange(groups) == 0)[:, None]
    valid = ((coin < level) | diagonal | first) & inside
    score = (1 - valid.astype(jnp.int32)) * 8 + jnp.arange(7, dtype=jnp.int32)[None, :]
    order = jnp.argsort(score, axis=1)
    row_sorted = jnp.take_along_axis(jnp.where(valid, row_ids, -1), order, axis=1)
    col_sorted = jnp.take_along_axis(jnp.where(valid, col_ids, -1), order, axis=1)
    empty = -jnp.ones((groups, GSLOTS - 7), jnp.int32)
    row_full = jnp.concatenate([row_sorted, empty], axis=1)
    col_full = jnp.concatenate([col_sorted, empty], axis=1)
    return jnp.stack([row_full, col_full], axis=-1).reshape(groups * GSLOTS, 2).astype(jnp.int32)


def shard_levels(key, shape, cuts, smallest, high):
    factor_of = 1.0
    for position, blocks in cuts:
        draws = jax.random.uniform(jax.random.fold_in(jax.random.fold_in(key, 6), position), (blocks,), jnp.float32, smallest / len(cuts), high / len(cuts))
        factor_of = factor_of * jnp.repeat(jnp.exp(draws), shape[position] // blocks).reshape((-1,) + (1,) * (len(shape) - 1 - position))
    return factor_of


def gaussian(own_key, extent, width, most, cuts=(), kind=jnp.bfloat16):
    result = width * jax.random.normal(own_key, extent, jnp.float32)
    if cuts:
        result = result * shard_levels(own_key, extent, cuts, -0.22, 0.18)
    return jnp.clip(result, -most, most).astype(kind)


def setup_inputs(seed: int = 0) -> dict:
    arg_keys = jax.random.split(jax.random.key(seed), 4)
    return {
        "embeddings": draw_embeddings(jax.random.fold_in(arg_keys[3], 71), 0),
        "start_vectors": gaussian(arg_keys[1], (NROWS, K), 1.0, 6.0, ((0, 64),), jnp.float32),
        "pairs": draw_pairs(jax.random.fold_in(arg_keys[3], 71), 0),
    }


inverse_width = 1.0 / 64.0
highest = lax.Precision.HIGHEST

def tile_add(acc, embeddings, norms, vectors, row_start, col_start, same):
    xa = lax.dynamic_slice_in_dim(embeddings, row_start, BLOCK, 0)
    xb = lax.dynamic_slice_in_dim(embeddings, col_start, BLOCK, 0)
    na = lax.dynamic_slice_in_dim(norms, row_start, BLOCK, 0)
    nb = lax.dynamic_slice_in_dim(norms, col_start, BLOCK, 0)
    dots = lax.dot_general(xa.astype(jnp.float32), xb.astype(jnp.float32), (((1,), (1,)), ((), ())), precision=highest, preferred_element_type=jnp.float32)
    dist = jnp.maximum(na[:, None] + nb[None, :] - 2.0 * dots, 0.0)
    affinity = jnp.exp(-dist * inverse_width)
    va = lax.dynamic_slice_in_dim(vectors, row_start, BLOCK, 0)
    vb = lax.dynamic_slice_in_dim(vectors, col_start, BLOCK, 0)
    ahead = jnp.dot(affinity.astype(jnp.float32), vb.astype(jnp.float32), precision=highest, preferred_element_type=jnp.float32)
    behind = lax.dot_general(affinity.astype(jnp.float32), va.astype(jnp.float32), (((0,), (0,)), ((), ())), precision=highest, preferred_element_type=jnp.float32)
    behind = behind * (1.0 - same)
    current = lax.dynamic_slice_in_dim(acc, row_start, BLOCK, 0)
    acc = lax.dynamic_update_slice_in_dim(acc, current + ahead, row_start, 0)
    current = lax.dynamic_slice_in_dim(acc, col_start, BLOCK, 0)
    return lax.dynamic_update_slice_in_dim(acc, current + behind, col_start, 0)

def reference(embeddings, start_vectors, pairs):
    norms = jnp.sum(embeddings * embeddings, axis=1)
    vectors = start_vectors
    for step in range(ITERS):

        def visit(acc, pair):
            row_block = pair[0]
            col_block = pair[1]

            def work(inner):
                row_start = (jnp.maximum(row_block, 0) * BLOCK).astype(jnp.int32)
                col_start = (jnp.maximum(col_block, 0) * BLOCK).astype(jnp.int32)
                same = (row_block == col_block).astype(jnp.float32)
                return tile_add(inner, embeddings, norms, vectors, row_start, col_start, same)
            return (lax.cond(row_block >= 0, work, lambda inner: inner, acc), None)
        image, _ = lax.scan(visit, jnp.zeros((NROWS, K), jnp.float32), pairs)
        gram = lax.dot_general(image.astype(jnp.float32), image.astype(jnp.float32), (((0,), (0,)), ((), ())), precision=highest, preferred_element_type=jnp.float32) / NROWS
        lower = jnp.linalg.cholesky(gram)
        vectors = lax.linalg.triangular_solve(lower, image, left_side=False, lower=True, transpose_a=True)
    return vectors
```

```python
import functools
import jax
import jax.numpy as jnp
from jax import lax
from jax.experimental import pallas as pl
from jax.experimental.pallas import tpu as pltpu
from jax.sharding import PartitionSpec as P

BLK_DEV = 2
MB = 1024 * 1024
LOG2E = 1.4426950408889634
SCALE = LOG2E / 64.0

f32 = jnp.float32
bf16 = jnp.bfloat16
NN = (((1,), (0,)), ((), ()))
NT = (((1,), (1,)), ((), ()))


def dot(a, b, dims):
    return lax.dot_general(a, b, dims, preferred_element_type=f32)


def split2(x):
    hi = x.astype(bf16)
    return hi, (x - hi.astype(f32)).astype(bf16)


def split3(x):
    hi = x.astype(bf16)
    rest = x - hi.astype(f32)
    mid = rest.astype(bf16)
    return hi, mid, (rest - mid.astype(f32)).astype(bf16)


def listed(pairs_ref, row_block, col_block):
    hit = jnp.int32(0)
    for slot in range(pairs_ref.shape[0]):
        same = (pairs_ref[slot, 0] == row_block) & (pairs_ref[slot, 1] == col_block)
        hit = hit | same.astype(jnp.int32)
    return hit > 0


def place():
    group = lax.axis_index("rows")
    member = lax.axis_index("sub")
    return group, member


def want(pairs_ref, group, member, members, offset, j):
    mine = group * BLK_DEV + (member * BLK_DEV) // members
    other = (group + offset) * BLK_DEV + j
    return listed(pairs_ref, jnp.minimum(mine, other), jnp.maximum(mine, other))


def add_tiles(x_ref, xah, xal, na, v_ref, acc_ref, eh_ref, el_ref, start, rows, chunk):
    for c in range(rows // chunk):
        here = pl.ds(start + c * chunk, chunk)
        x = x_ref[here, :]
        nb = jnp.sum(x * x, axis=1, keepdims=True) * SCALE
        xh, xl = split2(x)
        d = dot(xh, xah, NT) + (dot(xh, xal, NT) + dot(xl, xah, NT))
        e = jnp.exp2(jnp.minimum(d - nb - na, 0.0))
        eh, el = split2(e)
        eh_ref[here, :] = eh
        el_ref[here, :] = el
        vh, vm, vl = split3(v_ref[:, here])
        k = vh.shape[0]
        first = dot(jnp.concatenate([vh, vm, vl], 0), eh, NN)
        second = dot(jnp.concatenate([vh, vm], 0), el, NN)
        acc_ref[...] += (first[:k] + second[:k]) + (first[k : 2 * k] + second[k:] + first[2 * k :])


def own_kernel(members, x_ref, v_ref, pairs_ref, xah_ref, xal_ref, na_ref, acc_ref, eh_ref, el_ref):
    group, member = place()
    rows = x_ref.shape[0]
    quarter = rows // members
    block = rows // BLK_DEV
    xa = x_ref[pl.ds(pl.multiple_of(member * quarter, quarter), quarter), :]
    ones = jnp.ones((8, xa.shape[1]), f32)
    na_ref[...] = lax.dot_general(ones, xa * xa, NT, precision=lax.Precision.HIGHEST, preferred_element_type=f32) * SCALE
    xah, xal = split2(xa * (2.0 * SCALE))
    xah_ref[...] = xah
    xal_ref[...] = xal
    acc_ref[...] = jnp.zeros_like(acc_ref)
    for j in range(BLK_DEV):
        @pl.when(want(pairs_ref, group, member, members, 0, j))
        def _():
            add_tiles(x_ref, xah_ref[...], xal_ref[...], na_ref[0:1, :], v_ref, acc_ref, eh_ref, el_ref, j * block, block, 256)


def other_kernel(members, offset, x_ref, v_ref, pairs_ref, xah_ref, xal_ref, na_ref, in_ref, acc_ref, eh_ref, el_ref):
    group, member = place()
    rows = x_ref.shape[0]
    block = rows // BLK_DEV
    acc_ref[...] = in_ref[...]
    for j in range(BLK_DEV):
        @pl.when(want(pairs_ref, group, member, members, offset, j))
        def _():
            add_tiles(x_ref, xah_ref[...], xal_ref[...], na_ref[0:1, :], v_ref, acc_ref, eh_ref, el_ref, j * block, block, 256)


def gram_sum(vh, vm, vl):
    s = jnp.concatenate([vh, vm, vl], 0)
    k = vh.shape[0]
    p = dot(s, s, NT)
    r = p[:k] + (p[k : 2 * k] + p[2 * k :])
    return r[:, :k] + (r[:, k : 2 * k] + r[:, 2 * k :])


def gather_into(full_ref, pieces, members):
    _, member = place()
    quarter = pieces[0].shape[1]
    for k, piece in enumerate(pieces):
        q = lax.rem(member - k + members, members)
        full_ref[:, pl.ds(pl.multiple_of(q * quarter, quarter), quarter)] = piece[...]


def join_kernel(members, total, *refs):
    pieces, full_ref, gram_ref = refs[:members], refs[members], refs[members + 1]
    gather_into(full_ref, pieces, members)
    gram_ref[...] = gram_sum(*split3(full_ref[...])) / total


def second_kernel(members, vo_ref, vp_ref, vn_ref, eho, elo, ehp, elp, ehn, eln, pairs_ref, prev_pairs_ref, out_ref):
    group, member = place()
    rows = vo_ref.shape[1]
    block = rows // BLK_DEV
    k = vo_ref.shape[0]
    out_ref[...] = jnp.zeros_like(out_ref)
    for v_ref, eh_ref, el_ref, plist, offset in (
        (vo_ref, eho, elo, pairs_ref, 0),
        (vp_ref, ehp, elp, prev_pairs_ref, -1),
        (vn_ref, ehn, eln, pairs_ref, 1),
    ):
        for j in range(BLK_DEV):
            @pl.when(want(plist, group, member, members, offset, j))
            def _():
                here = pl.ds(j * block, block)
                vh, vm, vl = split3(v_ref[:, here])
                first = dot(jnp.concatenate([vh, vm, vl], 0), eh_ref[here, :], NN)
                second = dot(jnp.concatenate([vh, vm], 0), el_ref[here, :], NN)
                out_ref[...] += (first[:k] + second[:k]) + (first[k : 2 * k] + second[k:] + first[2 * k :])


def factor_inverse(gram):
    k = gram.shape[0]
    rows = lax.broadcasted_iota(jnp.int32, (k, k), 0)
    cols = lax.broadcasted_iota(jnp.int32, (k, k), 1)
    eye = (rows == cols).astype(f32)
    aug = jnp.concatenate([gram, eye], 1)
    row_ids = lax.broadcasted_iota(jnp.int32, (k, 2 * k), 0)
    for i in range(k):
        pivot = aug[i : i + 1, :]
        scale = lax.rsqrt(aug[i : i + 1, i : i + 1])
        row = pivot * scale
        col = aug[:, i : i + 1] * scale
        new = aug - col * row
        aug = jnp.where(row_ids < i, aug, jnp.where(row_ids == i, row, new))
    return aug[:, k:]


def factor_kernel(ga_ref, gb_ref, inv_ref):
    inv_ref[...] = factor_inverse(ga_ref[...] + gb_ref[...])


def exact(a, b):
    return lax.dot_general(a, b, NN, precision=lax.Precision.HIGHEST, preferred_element_type=f32)


def image_kernel(members, total, inv_ref, *refs):
    pieces, image_ref, gram_ref = refs[:members], refs[members], refs[members + 1]
    gather_into(image_ref, pieces, members)
    image_ref[...] = exact(inv_ref[...], image_ref[...])
    gram_ref[...] = gram_sum(*split3(image_ref[...])) / total


def last_kernel(ga_ref, gb_ref, image_ref, out_ref):
    inv = factor_inverse(ga_ref[...] + gb_ref[...])
    out_ref[...] = exact(inv, image_ref[...])


VM = pl.BlockSpec(memory_space=pltpu.VMEM)
SM = pl.BlockSpec(memory_space=pltpu.SMEM)


def call(body, specs, outs, name, limit=40, flops=10**9):
    return pl.pallas_call(
        body,
        in_specs=specs,
        out_specs=[VM] * len(outs),
        out_shape=[jax.ShapeDtypeStruct(s, t) for s, t in outs],
        compiler_params=pltpu.CompilerParams(vmem_limit_bytes=limit * MB),
        cost_estimate=pl.CostEstimate(flops=flops, bytes_accessed=MB, transcendentals=0),
        name=name,
    )


def shifted(x, axis, by):
    n = lax.axis_size(axis)
    return lax.ppermute(x, axis, [(i, i + by) for i in range(n) if 0 <= i + by < n])


def swapped(x, axis, mask):
    n = lax.axis_size(axis)
    return lax.ppermute(x, axis, [(i, i ^ mask) for i in range(n)])


def rotated(x, axis, by):
    n = lax.axis_size(axis)
    return lax.ppermute(x, axis, [(i, (i + by) % n) for i in range(n)])


MASKS = (1, 2, 6, 8, 16, 48)


def pair_sums(gram):
    for mask in MASKS[:-1]:
        gram = gram + swapped(gram, "rows", mask)
    return gram, swapped(gram, "rows", MASKS[-1])


def on_device(embeddings, start_vectors, pairs):
    members = lax.axis_size("sub")
    rows, width = embeddings.shape
    k = start_vectors.shape[1]
    quarter = rows // members
    total = rows * lax.axis_size("rows")
    vt = start_vectors.T
    prev_e = shifted(embeddings, "rows", 1)
    next_e = shifted(embeddings, "rows", -1)
    prev_v = shifted(vt, "rows", 1)
    next_v = shifted(vt, "rows", -1)
    prev_pairs = shifted(pairs, "rows", 1)
    part = ((k, quarter), f32)
    tiles = [((rows, quarter), bf16)] * 2
    xah, xal, na, acc, eho, elo = call(
        functools.partial(own_kernel, members), [VM, VM, SM],
        [((quarter, width), bf16)] * 2 + [((8, quarter), f32), part] + tiles, "own_tiles",
        flops=5 * 10**9)(embeddings, vt, pairs)
    other = lambda offset, name: call(
        functools.partial(other_kernel, members, offset), [VM, VM, SM, VM, VM, VM, VM],
        [part] + tiles, name, flops=5 * 10**9)
    acc, ehp, elp = other(-1, "prev_tiles")(prev_e, prev_v, prev_pairs, xah, xal, na, acc)
    acc, ehn, eln = other(1, "next_tiles")(next_e, next_v, pairs, xah, xal, na, acc)
    pieces = [acc] + [rotated(acc, "sub", s) for s in range(1, members)]
    whole = ((k, rows), f32)
    small = ((k, k), f32)
    image, gram = call(functools.partial(join_kernel, members, total), [VM] * members, [whole, small], "join")(*pieces)
    prev_i = shifted(image, "rows", 1)
    next_i = shifted(image, "rows", -1)
    ga, gb = pair_sums(gram)
    (acc2,) = call(
        functools.partial(second_kernel, members), [VM] * 9 + [SM, SM], [part], "second_product")(
        image, prev_i, next_i, eho, elo, ehp, elp, ehn, eln, pairs, prev_pairs)
    pieces = [acc2] + [rotated(acc2, "sub", s) for s in range(1, members)]
    (inv,) = call(factor_kernel, [VM, VM], [small], "factor")(ga, gb)
    image, gram = call(functools.partial(image_kernel, members, total), [VM] * (1 + members), [whole, small], "image")(inv, *pieces)
    ga, gb = pair_sums(gram)
    (out,) = call(last_kernel, [VM, VM, VM], [whole], "last")(ga, gb, image)
    return out.T


def solution(mesh):
    return jax.shard_map(
        on_device,
        mesh=mesh,
        in_specs=(P("rows", None), P("rows", None), P("rows", None)),
        out_specs=P("rows", None),
        check_vma=False,
    )
```

```python
import functools
import jax
import jax.numpy as jnp
from jax import lax
from jax.experimental import pallas as pl
from jax.experimental.pallas import tpu as pltpu
from jax.sharding import PartitionSpec as P

BLK_DEV = 2
OWN, SIB, CROSS = 0, 1, -1
MB = 1024 * 1024
LOG2E = 1.4426950408889634
SCALE = LOG2E / 64.0

f32 = jnp.float32
bf16 = jnp.bfloat16
NN = (((1,), (0,)), ((), ()))
NT = (((1,), (1,)), ((), ()))


def dot(a, b, dims):
    return lax.dot_general(a, b, dims, preferred_element_type=f32)


def split2(x):
    hi = x.astype(bf16)
    return hi, (x - hi.astype(f32)).astype(bf16)


def split3(x):
    hi = x.astype(bf16)
    rest = x - hi.astype(f32)
    mid = rest.astype(bf16)
    return hi, mid, (rest - mid.astype(f32)).astype(bf16)


def listed(pairs_ref, row_block, col_block):
    hit = jnp.int32(0)
    for slot in range(pairs_ref.shape[0]):
        same = (pairs_ref[slot, 0] == row_block) & (pairs_ref[slot, 1] == col_block)
        hit = hit | same.astype(jnp.int32)
    return hit > 0


def place():
    group = lax.axis_index("rows")
    member = lax.axis_index("sub")
    return group, member


def want(lists, group, member, members, side, j):
    mine = group * BLK_DEV + (member * BLK_DEV) // members
    other = (group + side * (1 - 2 * (group % 2))) * BLK_DEV + j
    low, high = jnp.minimum(mine, other), jnp.maximum(mine, other)
    hit = listed(lists[0], low, high)
    for pairs_ref in lists[1:]:
        hit = hit | listed(pairs_ref, low, high)
    return hit


def add_tiles(x_ref, xah, xal, na, v_ref, acc_ref, eh_ref, el_ref, start, first, rows, chunk):
    for c in range(rows // chunk):
        here = pl.ds(start + c * chunk, chunk)
        x = x_ref[here, :]
        nb = jnp.sum(x * x, axis=1, keepdims=True) * SCALE
        xh, xl = split2(x)
        d = dot(xh, xah, NT) + (dot(xh, xal, NT) + dot(xl, xah, NT))
        e = jnp.exp2(jnp.minimum(d - nb - na, 0.0))
        eh, el = split2(e)
        eh_ref[here, :] = eh
        el_ref[here, :] = el
        vh, vm, vl = split3(v_ref[:, pl.ds(first + start + c * chunk, chunk)])
        k = vh.shape[0]
        one = dot(jnp.concatenate([vh, vm, vl], 0), eh, NN)
        two = dot(jnp.concatenate([vh, vm], 0), el, NN)
        acc_ref[...] += (one[:k] + two[:k]) + (one[k : 2 * k] + two[k:] + one[2 * k :])


def own_kernel(members, x_ref, v_ref, pairs_ref, xah_ref, xal_ref, na_ref, acc_ref, eh_ref, el_ref):
    group, member = place()
    rows = x_ref.shape[0]
    quarter = rows // members
    block = rows // BLK_DEV
    xa = x_ref[pl.ds(pl.multiple_of(member * quarter, quarter), quarter), :]
    ones = jnp.ones((8, xa.shape[1]), f32)
    na_ref[...] = lax.dot_general(ones, xa * xa, NT, precision=lax.Precision.HIGHEST, preferred_element_type=f32) * SCALE
    xah, xal = split2(xa * (2.0 * SCALE))
    xah_ref[...] = xah
    xal_ref[...] = xal
    acc_ref[...] = jnp.zeros_like(acc_ref)
    for j in range(BLK_DEV):
        @pl.when(want((pairs_ref,), group, member, members, OWN, j))
        def _():
            add_tiles(x_ref, xah_ref[...], xal_ref[...], na_ref[0:1, :], v_ref, acc_ref, eh_ref, el_ref, j * block, 0, block, 256)


def other_kernel(members, side, first, x_ref, v_ref, pairs_ref, prev_pairs_ref, xah_ref, xal_ref, na_ref, in_ref, acc_ref, eh_ref, el_ref):
    group, member = place()
    rows = x_ref.shape[0]
    block = v_ref.shape[1] // BLK_DEV
    acc_ref[...] = in_ref[...]
    step = min(rows, block)
    for start in range(0, rows, step):
        @pl.when(want((pairs_ref, prev_pairs_ref), group, member, members, side, (first + start) // block))
        def _():
            add_tiles(x_ref, xah_ref[...], xal_ref[...], na_ref[0:1, :], v_ref, acc_ref, eh_ref, el_ref, start, first, step, 256)


def gram_sum(vh, vm, vl):
    s = jnp.concatenate([vh, vm, vl], 0)
    k = vh.shape[0]
    p = dot(s, s, NT)
    r = p[:k] + (p[k : 2 * k] + p[2 * k :])
    return r[:, :k] + (r[:, k : 2 * k] + r[:, 2 * k :])


def gather_into(full_ref, pieces, members):
    _, member = place()
    quarter = pieces[0].shape[1]
    for k, piece in enumerate(pieces):
        q = lax.rem(member - k + members, members)
        full_ref[:, pl.ds(pl.multiple_of(q * quarter, quarter), quarter)] = piece[...]


def join_kernel(members, total, *refs):
    pieces, full_ref, gram_ref = refs[:members], refs[members], refs[members + 1]
    gather_into(full_ref, pieces, members)
    gram_ref[...] = gram_sum(*split3(full_ref[...])) / total


def second_kernel(members, sources, pairs_ref, prev_pairs_ref, *refs):
    group, member = place()
    vectors, kept, out_ref = refs[:3], refs[3:-1], refs[-1]
    k, rows = vectors[0].shape
    block = rows // BLK_DEV
    out_ref[...] = jnp.zeros_like(out_ref)
    for n, (which, first, count) in enumerate(sources):
        eh_ref, el_ref = kept[2 * n : 2 * n + 2]
        step = min(count, block)
        for start in range(0, count, step):
            @pl.when(want((pairs_ref, prev_pairs_ref), group, member, members, (OWN, SIB, CROSS)[which], (first + start) // block))
            def _():
                here = pl.ds(start, step)
                vh, vm, vl = split3(vectors[which][:, pl.ds(first + start, step)])
                one = dot(jnp.concatenate([vh, vm, vl], 0), eh_ref[here, :], NN)
                two = dot(jnp.concatenate([vh, vm], 0), el_ref[here, :], NN)
                out_ref[...] += (one[:k] + two[:k]) + (one[k : 2 * k] + two[k:] + one[2 * k :])


def factor_inverse(gram, w=8):
    k = gram.shape[0]
    rows = lax.broadcasted_iota(jnp.int32, (k, k), 0)
    cols = lax.broadcasted_iota(jnp.int32, (k, k), 1)
    aug = jnp.concatenate([gram, (rows == cols).astype(f32)], 1)
    tall, wide = 8, 2 * k
    a = [aug[t * tall : (t + 1) * tall, :] for t in range(k // tall)]
    sub = lax.broadcasted_iota(jnp.int32, (tall, wide), 0)
    spread = lambda x: jnp.broadcast_to(x, (tall, wide))
    for start in range(0, k, w):
        t, s = start // tall, start % tall
        r = [spread(a[t][s + i : s + i + 1, :]) for i in range(w)]
        d = [[spread(a[t][s + i : s + i + 1, start + j : start + j + 1]) if j >= i else None for j in range(w)] for i in range(w)]
        later = range(t if s + w < tall else t + 1, len(a))
        c = {u: [spread(a[u][:, start + i : start + i + 1]) for i in range(w)] for u in later}
        l = [[None] * w for _ in range(w)]
        inv = [None] * w
        for i in range(w):
            p = d[i][i]
            for m in range(i):
                p = p - l[i][m] * l[i][m]
            inv[i] = lax.rsqrt(p)
            for j in range(i + 1, w):
                q = d[i][j]
                for m in range(i):
                    q = q - l[i][m] * l[j][m]
                l[j][i] = q * inv[i]
        for i in range(w):
            for m in range(i):
                r[i] = r[i] - l[i][m] * r[m]
            r[i] = r[i] * inv[i]
        for u in later:
            x = c[u]
            for i in range(w):
                for m in range(i):
                    x[i] = x[i] - l[i][m] * x[m]
                x[i] = x[i] * inv[i]
            new = a[u]
            for i in range(w):
                new = new - x[i] * r[i]
            a[u] = new if u > t else jnp.where(sub < s + w, a[u], new)
        for i in range(w):
            a[t] = jnp.where(sub == s + i, r[i], a[t])
    return jnp.concatenate(a, 0)[:, k:]


def factor_kernel(ga_ref, gb_ref, inv_ref):
    inv_ref[...] = factor_inverse(ga_ref[...] + gb_ref[...])


def exact(a, b):
    return lax.dot_general(a, b, NN, precision=lax.Precision.HIGHEST, preferred_element_type=f32)


def image_kernel(members, total, inv_ref, *refs):
    pieces, image_ref, gram_ref = refs[:members], refs[members], refs[members + 1]
    gather_into(image_ref, pieces, members)
    image_ref[...] = exact(inv_ref[...], image_ref[...])
    gram_ref[...] = gram_sum(*split3(image_ref[...])) / total


def last_kernel(ga_ref, gb_ref, image_ref, out_ref):
    inv = factor_inverse(ga_ref[...] + gb_ref[...])
    out_ref[...] = exact(inv, image_ref[...])


VM = pl.BlockSpec(memory_space=pltpu.VMEM)
SM = pl.BlockSpec(memory_space=pltpu.SMEM)


def call(body, specs, outs, name, limit=40, flops=10**9):
    return pl.pallas_call(
        body,
        in_specs=specs,
        out_specs=[VM] * len(outs),
        out_shape=[jax.ShapeDtypeStruct(s, t) for s, t in outs],
        compiler_params=pltpu.CompilerParams(vmem_limit_bytes=limit * MB),
        cost_estimate=pl.CostEstimate(flops=flops, bytes_accessed=MB, transcendentals=0),
        name=name,
    )


def shifted(x, axis, by):
    n = lax.axis_size(axis)
    return lax.ppermute(x, axis, [(i, (i + by) % n) for i in range(n)])


def crossed(x):
    n = lax.axis_size("rows")
    return lax.ppermute(x, "rows", [(i, (i + 2 * (i % 2) - 1) % n) for i in range(n)])


def swapped(x, axis, mask):
    n = lax.axis_size(axis)
    return lax.ppermute(x, axis, [(i, i ^ mask) for i in range(n)])


MASKS = (1, 2, 6, 8, 16, 48)


def pair_sums(gram):
    for mask in MASKS[:-1]:
        gram = gram + swapped(gram, "rows", mask)
    return gram, swapped(gram, "rows", MASKS[-1])


def on_device(embeddings, start_vectors, pairs):
    members = lax.axis_size("sub")
    rows, width = embeddings.shape
    k = start_vectors.shape[1]
    quarter = rows // members
    total = rows * lax.axis_size("rows")
    vt = start_vectors.T
    chunks = 2
    piece = rows // chunks
    cross_e = [crossed(embeddings[c * piece : (c + 1) * piece]) for c in range(chunks)]
    sib_e = swapped(embeddings, "rows", 1)
    cross_v = crossed(vt)
    sib_v = swapped(vt, "rows", 1)
    prev_pairs = shifted(pairs, "rows", 1)
    part = ((k, quarter), f32)
    tiles = lambda n: [((n, quarter), bf16)] * 2
    xah, xal, na, acc, *own_t = call(
        functools.partial(own_kernel, members), [VM, VM, SM],
        [((quarter, width), bf16)] * 2 + [((8, quarter), f32), part] + tiles(rows), "own_tiles",
        flops=5 * 10**9)(embeddings, vt, pairs)
    other = lambda side, first, n, name: call(
        functools.partial(other_kernel, members, side, first), [VM, VM, SM, SM, VM, VM, VM, VM],
        [part] + tiles(n), name, flops=5 * 10**9)
    acc, *sib_t = other(SIB, 0, rows, "sib_tiles")(sib_e, sib_v, pairs, prev_pairs, xah, xal, na, acc)
    kept = own_t + sib_t
    sources = [(0, 0, rows), (1, 0, rows)]
    for c in range(chunks):
        acc, *t = other(CROSS, c * piece, piece, "cross_tiles")(cross_e[c], cross_v, pairs, prev_pairs, xah, xal, na, acc)
        kept += t
        sources.append((2, c * piece, piece))
    pieces = [acc] + [shifted(acc, "sub", s) for s in range(1, members)]
    whole = ((k, rows), f32)
    small = ((k, k), f32)
    image, gram = call(functools.partial(join_kernel, members, total), [VM] * members, [whole, small], "join")(*pieces)
    cross_i = crossed(image)
    sib_i = swapped(image, "rows", 1)
    ga, gb = pair_sums(gram)
    (acc2,) = call(
        functools.partial(second_kernel, members, sources), [SM, SM] + [VM] * (3 + len(kept)), [part], "second_product")(
        pairs, prev_pairs, image, sib_i, cross_i, *kept)
    pieces = [acc2] + [shifted(acc2, "sub", s) for s in range(1, members)]
    (inv,) = call(factor_kernel, [VM, VM], [small], "factor")(ga, gb)
    image, gram = call(functools.partial(image_kernel, members, total), [VM] * (1 + members), [whole, small], "image")(inv, *pieces)
    ga, gb = pair_sums(gram)
    (out,) = call(last_kernel, [VM, VM, VM], [whole], "last")(ga, gb, image)
    return out.T


def solution(mesh):
    return jax.shard_map(
        on_device,
        mesh=mesh,
        in_specs=(P("rows", None), P("rows", None), P("rows", None)),
        out_specs=P("rows", None),
        check_vma=False,
    )
```

```python
import functools
import jax
import jax.numpy as jnp
from jax import lax
from jax.experimental import pallas as pl
from jax.experimental.pallas import tpu as pltpu
from jax.sharding import PartitionSpec as P

BLK_DEV = 2
OWN, SIB, CROSS = 0, 1, -1
NOTE = 8
MB = 1024 * 1024
LOG2E = 1.4426950408889634
SCALE = LOG2E / 64.0

f32 = jnp.float32
bf16 = jnp.bfloat16
NN = (((1,), (0,)), ((), ()))
NT = (((1,), (1,)), ((), ()))


def dot(a, b, dims):
    return lax.dot_general(a, b, dims, preferred_element_type=f32)


def split2(x):
    hi = x.astype(bf16)
    return hi, (x - hi.astype(f32)).astype(bf16)


def split3(x):
    hi = x.astype(bf16)
    rest = x - hi.astype(f32)
    mid = rest.astype(bf16)
    return hi, mid, (rest - mid.astype(f32)).astype(bf16)


def listed(pairs_ref, row_block, col_block):
    hit = jnp.int32(0)
    for slot in range(pairs_ref.shape[0]):
        same = (pairs_ref[slot, 0] == row_block) & (pairs_ref[slot, 1] == col_block)
        hit = hit | same.astype(jnp.int32)
    return hit > 0


def place():
    group = lax.axis_index("rows")
    member = lax.axis_index("sub")
    return group, member


def want(pairs_ref, note_ref, group, member, members, side, j):
    mine = group * BLK_DEV + (member * BLK_DEV) // members
    other = (group + side * (1 - 2 * (group % 2))) * BLK_DEV + j
    low, high = jnp.minimum(mine, other), jnp.maximum(mine, other)
    hit = listed(pairs_ref, low, high)
    if note_ref is not None:
        note = note_ref[note_ref.shape[0] - NOTE :, 0:128]
        slot = lax.broadcasted_iota(jnp.int32, (1, 128), 1) < pairs_ref.shape[0]
        same = slot & (note[0:1, :] == low.astype(f32)) & (note[1:2, :] == high.astype(f32))
        hit = hit | (jnp.max(same.astype(f32)) > 0.5)
    return hit


def quarter_at(members, step, group, member):
    return (member + step * (1 - 2 * (group & 1))) & (members - 1)


def add_product(acc_ref, v, eh, el):
    vh, vm, vl = split3(v)
    k = vh.shape[0]
    one = dot(jnp.concatenate([vh, vm, vl], 0), eh, NN)
    two = dot(jnp.concatenate([vh, vm], 0), el, NN)
    acc_ref[...] += (one[:k] + two[:k]) + (one[k : 2 * k] + two[k:] + one[2 * k :])


def tiles_or_zeros(hit, x_ref, xah_ref, xal_ref, na_ref, v_ref, acc_ref, eh_ref, el_ref, start, rows, v_start, chunk=256):
    @pl.when(hit)
    def _():
        k = acc_ref.shape[0]
        xah, xal, na = xah_ref[...], xal_ref[...], na_ref[0:1, :]
        for c in range(rows // chunk):
            here = pl.ds(start + c * chunk, chunk)
            x = x_ref[here, :]
            nb = jnp.sum(x * x, axis=1, keepdims=True) * SCALE
            xh, xl = split2(x)
            d = dot(xh, xah, NT) + (dot(xh, xal, NT) + dot(xl, xah, NT))
            e = jnp.exp2(jnp.minimum(d - nb - na, 0.0))
            eh, el = split2(e)
            eh_ref[here, :] = eh
            el_ref[here, :] = el
            add_product(acc_ref, v_ref[:k, pl.ds(v_start + c * chunk, chunk)], eh, el)

    @pl.when(jnp.logical_not(hit))
    def _():
        here = pl.ds(start, rows)
        eh_ref[here, :] = jnp.zeros((rows, eh_ref.shape[1]), bf16)
        el_ref[here, :] = jnp.zeros((rows, el_ref.shape[1]), bf16)


def own_kernel(members, x_ref, v_ref, pairs_ref, xah_ref, xal_ref, na_ref, acc_ref, eh_ref, el_ref):
    group, member = place()
    rows = x_ref.shape[0]
    quarter = rows // members
    block = rows // BLK_DEV
    xa = x_ref[pl.ds(pl.multiple_of(member * quarter, quarter), quarter), :]
    ones = jnp.ones((8, xa.shape[1]), f32)
    na_ref[...] = lax.dot_general(ones, xa * xa, NT, precision=lax.Precision.HIGHEST, preferred_element_type=f32) * SCALE
    xah, xal = split2(xa * (2.0 * SCALE))
    xah_ref[...] = xah
    xal_ref[...] = xal
    acc_ref[...] = jnp.zeros_like(acc_ref)
    for j in range(BLK_DEV):
        hit = want(pairs_ref, None, group, member, members, OWN, j)
        tiles_or_zeros(hit, x_ref, xah_ref, xal_ref, na_ref, v_ref, acc_ref, eh_ref, el_ref, j * block, block, j * block)


def sib_kernel(members, x_ref, v_ref, pairs_ref, xah_ref, xal_ref, na_ref, in_ref, acc_ref, eh_ref, el_ref):
    group, member = place()
    block = x_ref.shape[0] // BLK_DEV
    acc_ref[...] = in_ref[...]
    for j in range(BLK_DEV):
        hit = want(pairs_ref, v_ref, group, member, members, SIB, j)
        tiles_or_zeros(hit, x_ref, xah_ref, xal_ref, na_ref, v_ref, acc_ref, eh_ref, el_ref, j * block, block, j * block)


def cross_kernel(members, step, x_ref, v_ref, pairs_ref, xah_ref, xal_ref, na_ref, in_ref, acc_ref, eh_ref, el_ref):
    group, member = place()
    rows = x_ref.shape[0]
    q = quarter_at(members, step, group, member)
    acc_ref[...] = in_ref[...]
    hit = want(pairs_ref, v_ref, group, member, members, CROSS, (q * BLK_DEV) // members)
    tiles_or_zeros(hit, x_ref, xah_ref, xal_ref, na_ref, v_ref, acc_ref, eh_ref, el_ref, 0, rows, pl.multiple_of(q * rows, rows))


def gram_sum(vh, vm, vl):
    s = jnp.concatenate([vh, vm, vl], 0)
    k = vh.shape[0]
    p = dot(s, s, NT)
    r = p[:k] + (p[k : 2 * k] + p[2 * k :])
    return r[:, :k] + (r[:, k : 2 * k] + r[:, 2 * k :])


def gather_into(full_ref, pieces, members):
    _, member = place()
    quarter = pieces[0].shape[1]
    for k, piece in enumerate(pieces):
        q = lax.rem(member - k + members, members)
        full_ref[:, pl.ds(pl.multiple_of(q * quarter, quarter), quarter)] = piece[...]


def put_gram(gram_ref, image, total):
    gram = gram_sum(*split3(image)) / total
    half = gram.shape[0] // 2
    packed = jnp.concatenate([gram[:half], gram[half:]], 1)
    for n in range(gram_ref.shape[0]):
        gram_ref[n] = packed


def take_gram(gram_ref):
    packed = gram_ref[0]
    for n in range(1, gram_ref.shape[0]):
        packed = packed + gram_ref[n]
    k = packed.shape[1] // 2
    return jnp.concatenate([packed[:, :k], packed[:, k:]], 0)


def join_kernel(members, total, *refs):
    pieces, full_ref, gram_ref = refs[:members], refs[members], refs[members + 1]
    gather_into(full_ref, pieces, members)
    put_gram(gram_ref, full_ref[...], total)


def second_kernel(members, vo_ref, vs_ref, vc_ref, *refs):
    group, member = place()
    kept, out_ref = refs[:-1], refs[-1]
    out_ref[...] = jnp.zeros_like(out_ref)
    for v_ref, eh_ref, el_ref in ((vo_ref, kept[0], kept[1]), (vs_ref, kept[2], kept[3])):
        block = v_ref.shape[1] // BLK_DEV
        for j in range(BLK_DEV):
            here = pl.ds(j * block, block)
            add_product(out_ref, v_ref[:, here], eh_ref[here, :], el_ref[here, :])
    for step in range(members):
        eh_ref, el_ref = kept[4 + 2 * step : 6 + 2 * step]
        rows = eh_ref.shape[0]
        q = quarter_at(members, step, group, member)
        add_product(out_ref, vc_ref[:, pl.ds(pl.multiple_of(q * rows, rows), rows)], eh_ref[...], el_ref[...])


def factor_inverse(gram, w=8):
    k = gram.shape[0]
    rows = lax.broadcasted_iota(jnp.int32, (k, k), 0)
    cols = lax.broadcasted_iota(jnp.int32, (k, k), 1)
    aug = jnp.concatenate([gram, (rows == cols).astype(f32)], 1)
    tall, wide = 8, 2 * k
    a = [aug[t * tall : (t + 1) * tall, :] for t in range(k // tall)]
    sub = lax.broadcasted_iota(jnp.int32, (tall, wide), 0)
    spread = lambda x: jnp.broadcast_to(x, (tall, wide))
    for start in range(0, k, w):
        t, s = start // tall, start % tall
        r = [spread(a[t][s + i : s + i + 1, :]) for i in range(w)]
        d = [[spread(a[t][s + i : s + i + 1, start + j : start + j + 1]) if j >= i else None for j in range(w)] for i in range(w)]
        later = range(t if s + w < tall else t + 1, len(a))
        c = {u: [spread(a[u][:, start + i : start + i + 1]) for i in range(w)] for u in later}
        l = [[None] * w for _ in range(w)]
        inv = [None] * w
        for i in range(w):
            p = d[i][i]
            for m in range(i):
                p = p - l[i][m] * l[i][m]
            inv[i] = lax.rsqrt(p)
            for j in range(i + 1, w):
                q = d[i][j]
                for m in range(i):
                    q = q - l[i][m] * l[j][m]
                l[j][i] = q * inv[i]
        for i in range(w):
            for m in range(i):
                r[i] = r[i] - l[i][m] * r[m]
            r[i] = r[i] * inv[i]
        for u in later:
            x = c[u]
            for i in range(w):
                for m in range(i):
                    x[i] = x[i] - l[i][m] * x[m]
                x[i] = x[i] * inv[i]
            new = a[u]
            for i in range(w):
                new = new - x[i] * r[i]
            a[u] = new if u > t else jnp.where(sub < s + w, a[u], new)
        for i in range(w):
            a[t] = jnp.where(sub == s + i, r[i], a[t])
    return jnp.concatenate(a, 0)[:, k:]


def factor_kernel(a_ref, b_ref, inv_ref):
    inv_ref[...] = factor_inverse(take_gram(a_ref) + take_gram(b_ref))


def exact(a, b):
    return lax.dot_general(a, b, NN, precision=lax.Precision.HIGHEST, preferred_element_type=f32)


def image_kernel(members, total, inv_ref, *refs):
    pieces, image_ref, gram_ref = refs[:members], refs[members], refs[members + 1]
    gather_into(image_ref, pieces, members)
    image_ref[...] = exact(inv_ref[...], image_ref[...])
    put_gram(gram_ref, image_ref[...], total)


def last_kernel(gram_ref, image_ref, out_ref):
    out_ref[...] = exact(factor_inverse(take_gram(gram_ref)), image_ref[...])


VM = pl.BlockSpec(memory_space=pltpu.VMEM)
SM = pl.BlockSpec(memory_space=pltpu.SMEM)


def call(body, specs, outs, name, limit=24, flops=10**9):
    return pl.pallas_call(
        body,
        in_specs=specs,
        out_specs=[VM] * len(outs),
        out_shape=[jax.ShapeDtypeStruct(s, t) for s, t in outs],
        compiler_params=pltpu.CompilerParams(vmem_limit_bytes=limit * MB),
        cost_estimate=pl.CostEstimate(flops=flops, bytes_accessed=MB, transcendentals=0),
        name=name,
    )


def shifted(x, axis, by):
    n = lax.axis_size(axis)
    return lax.ppermute(x, axis, [(i, (i + by) % n) for i in range(n)])


def crossed(x):
    n = lax.axis_size("rows")
    return lax.ppermute(x, "rows", [(i, (i + 2 * (i % 2) - 1) % n) for i in range(n)])


def swapped(x):
    return lax.ppermute(x, "rows", [(i, i ^ 1) for i in range(lax.axis_size("rows"))])


def passed_on(x):
    groups, members = lax.axis_size("rows"), lax.axis_size("sub")
    at = lambda g, m: g * members + m % members
    return lax.ppermute(x, ("rows", "sub"), [(at(g, m), at(g, m + 1 - 2 * (g % 2))) for g in range(groups) for m in range(members)])


NEAR = 8


def far_sets():
    groups, members = lax.axis_size("rows"), lax.axis_size("sub")
    return [[g * members + m for g in range(low, groups, NEAR)] for low in range(NEAR) for m in range(members)]


def near_sets():
    groups, members = lax.axis_size("rows"), lax.axis_size("sub")
    return [[g * members + m for g in range(base, base + NEAR)] for base in range(0, groups, NEAR) for m in range(members)]


def exchanged(x, sets):
    return lax.all_to_all(x, ("rows", "sub"), 0, 0, axis_index_groups=sets)


MASKS = (1, 2, 6, 8, 16, 48)


def pair_sums(gram):
    for mask in MASKS:
        pairs = [(i, i ^ mask) for i in range(lax.axis_size("rows"))]
        other = lax.ppermute(gram, "rows", pairs)
        gram = gram + other if mask != MASKS[-1] else (gram, other)
    return gram


def tie(x, *others):
    return lax.optimization_barrier((x, *others))[0]


def on_device(embeddings, start_vectors, pairs):
    members = lax.axis_size("sub")
    groups = lax.axis_size("rows")
    group, member = place()
    rows, width = embeddings.shape
    k = start_vectors.shape[1]
    quarter = rows // members
    total = rows * groups
    vt = start_vectors.T
    turn = 1 - 2 * (group & 1)

    def to_send(step, *after):
        q = (member - step * turn) & (members - 1)
        return lax.dynamic_slice(tie(embeddings, *after), (q * quarter, 0), (quarter, width), allow_negative_indices=False)

    first = to_send(0)
    note = jnp.pad(tie(pairs, first).T.astype(f32), ((0, NOTE - 2), (0, rows - pairs.shape[0])))
    message = jnp.concatenate([vt, note], 0)
    second = to_send(1, message)
    arrived = [crossed(first)]
    cross_v = crossed(message)
    arrived.append(crossed(second))
    sib_v = swapped(tie(message, second))
    sib_e = swapped(tie(embeddings, second))
    part = ((k, quarter), f32)
    tiles = lambda n: [((n, quarter), bf16)] * 2
    xah, xal, na, acc, *kept = call(
        functools.partial(own_kernel, members), [VM, VM, SM],
        [((quarter, width), bf16)] * 2 + [((8, quarter), f32), part] + tiles(rows), "own_tiles",
        flops=5 * 10**9)(embeddings, vt, pairs)
    acc, *t = call(
        functools.partial(sib_kernel, members), [VM, VM, SM, VM, VM, VM, VM], [part] + tiles(rows), "sib_tiles",
        flops=5 * 10**9)(sib_e, sib_v, pairs, xah, xal, na, acc)
    kept += t
    arrived.append(crossed(to_send(2, acc)))
    arrived.append(passed_on(arrived[0]))
    for step in (0, 3, 1, 2):
        acc, *t = call(
            functools.partial(cross_kernel, members, step), [VM, VM, SM, VM, VM, VM, VM], [part] + tiles(quarter), "cross_tiles",
            flops=2 * 10**9)(arrived[step], cross_v, pairs, xah, xal, na, acc)
        arrived[step] = t
    for t in arrived:
        kept += t
    pieces = [acc] + [shifted(acc, "sub", s) for s in range(1, members)]
    whole = ((k, rows), f32)
    far, near = far_sets(), near_sets()
    grams = lambda sets: ((len(sets[0]), k // 2, 2 * k), f32)
    image, gram = call(functools.partial(join_kernel, members, total), [VM] * members, [whole, ((1, k // 2, 2 * k), f32)], "join")(*pieces)
    cross_i = crossed(image)
    sib_i = swapped(image)
    grams_1 = pair_sums(gram)
    (acc2,) = call(functools.partial(second_kernel, members), [VM] * (3 + len(kept)), [part], "second_product")(
        image, sib_i, cross_i, *kept)
    pieces = [acc2] + [shifted(acc2, "sub", s) for s in range(1, members)]
    (inv,) = call(factor_kernel, [VM, VM], [((k, k), f32)], "factor")(*grams_1)
    image, gram = call(functools.partial(image_kernel, members, total), [VM] * (1 + members), [whole, grams(far)], "image")(inv, *pieces)
    gram = exchanged(gram, far)
    gram = exchanged(jnp.broadcast_to(gram.sum(0)[None], grams(near)[0]), near)
    (out,) = call(last_kernel, [VM, VM], [whole], "last")(gram, image)
    return out.T


def solution(mesh):
    return jax.shard_map(
        on_device,
        mesh=mesh,
        in_specs=(P("rows", None), P("rows", None), P("rows", None)),
        out_specs=P("rows", None),
        check_vma=False,
    )
```

```python
import functools
import jax
import jax.numpy as jnp
from jax import lax
from jax.experimental import pallas as pl
from jax.experimental.pallas import tpu as pltpu
from jax.sharding import PartitionSpec as P

BLK_DEV = 2
OWN, SIB, CROSS = 0, 1, -1
NOTE = 8
MB = 1024 * 1024
LOG2E = 1.4426950408889634
SCALE = LOG2E / 64.0

f32 = jnp.float32
bf16 = jnp.bfloat16
NN = (((1,), (0,)), ((), ()))
NT = (((1,), (1,)), ((), ()))


def dot(a, b, dims):
    return lax.dot_general(a, b, dims, preferred_element_type=f32)


def split2(x):
    hi = x.astype(bf16)
    return hi, (x - hi.astype(f32)).astype(bf16)


def split3(x):
    hi = x.astype(bf16)
    rest = x - hi.astype(f32)
    mid = rest.astype(bf16)
    return hi, mid, (rest - mid.astype(f32)).astype(bf16)


def listed(pairs_ref, row_block, col_block):
    hit = jnp.int32(0)
    for slot in range(pairs_ref.shape[0]):
        same = (pairs_ref[slot, 0] == row_block) & (pairs_ref[slot, 1] == col_block)
        hit = hit | same.astype(jnp.int32)
    return hit > 0


def place():
    group = lax.axis_index("rows")
    member = lax.axis_index("sub")
    return group, member


def want(pairs_ref, note_ref, group, member, members, side, j):
    mine = group * BLK_DEV + (member * BLK_DEV) // members
    other = (group + side * (1 - 2 * (group & 1))) * BLK_DEV + j
    low, high = jnp.minimum(mine, other), jnp.maximum(mine, other)
    hit = listed(pairs_ref, low, high)
    if note_ref is not None:
        slot = lax.broadcasted_iota(jnp.int32, (1, note_ref.shape[1]), 1) < pairs_ref.shape[0]
        same = slot & (note_ref[0:1, :] == low.astype(f32)) & (note_ref[1:2, :] == high.astype(f32))
        hit = hit | (jnp.max(same.astype(f32)) > 0.5)
    return hit


def quarter_at(members, step, group, member):
    return (member + step * (1 - 2 * (group & 1))) & (members - 1)


def add_product(acc_ref, v, eh, el):
    vh, vm, vl = split3(v)
    k = vh.shape[0]
    one = dot(jnp.concatenate([vh, vm, vl], 0), eh, NN)
    two = dot(jnp.concatenate([vh, vm], 0), el, NN)
    acc_ref[...] += (one[:k] + two[:k]) + (one[k : 2 * k] + two[k:] + one[2 * k :])


def tiles_or_zeros(hit, x_ref, xah_ref, xal_ref, na_ref, v_ref, acc_ref, eh_ref, el_ref, start, rows, v_start, chunk=256):
    @pl.when(hit)
    def _():
        xah, xal, na = xah_ref[...], xal_ref[...], na_ref[0:1, :]
        for c in range(rows // chunk):
            here = pl.ds(start + c * chunk, chunk)
            x = x_ref[here, :]
            nb = jnp.sum(x * x, axis=1, keepdims=True) * SCALE
            xh, xl = split2(x)
            d = dot(xh, xah, NT) + (dot(xh, xal, NT) + dot(xl, xah, NT))
            e = jnp.exp2(jnp.minimum(d - nb - na, 0.0))
            eh, el = split2(e)
            eh_ref[here, :] = eh
            el_ref[here, :] = el
        here = pl.ds(start, rows)
        add_product(acc_ref, v_ref[:, pl.ds(v_start, rows)], eh_ref[here, :], el_ref[here, :])

    @pl.when(jnp.logical_not(hit))
    def _():
        here = pl.ds(start, rows)
        eh_ref[here, :] = jnp.zeros((rows, eh_ref.shape[1]), bf16)
        el_ref[here, :] = jnp.zeros((rows, el_ref.shape[1]), bf16)


def cut_kernel(members, x_ref, v_ref, pairs_ref, *refs):
    group, member = place()
    outs, sib_ref = refs[:-1], refs[-1]
    quarter, width = outs[1].shape
    lane = lax.broadcasted_iota(jnp.int32, (NOTE, width), 1)
    row = lax.broadcasted_iota(jnp.int32, (NOTE, width), 0)
    note = jnp.zeros((NOTE, width), f32)
    for slot in range(pairs_ref.shape[0]):
        for c in range(2):
            note = jnp.where((lane == slot) & (row == c), pairs_ref[slot, c].astype(f32), note)
    k = v_ref.shape[0]
    sib_ref[:k, :] = v_ref[...]
    sib_ref[k:, :width] = note
    sib_ref[k:, width:] = jnp.zeros((NOTE, sib_ref.shape[1] - width), f32)
    outs[0][quarter:, :] = note
    for step, out_ref in enumerate(outs):
        q = quarter_at(members, -step, group, member)
        out_ref[:quarter, :] = x_ref[pl.ds(pl.multiple_of(q * quarter, quarter), quarter), :]


def chip_kernel(members, x_ref, v_ref, sib_x_ref, sib_v_ref, pairs_ref, xah_ref, xal_ref, na_ref, acc_ref, *kept):
    group, member = place()
    rows = x_ref.shape[0]
    quarter = rows // members
    block = rows // BLK_DEV
    xa = x_ref[pl.ds(pl.multiple_of(member * quarter, quarter), quarter), :]
    ones = jnp.ones((8, xa.shape[1]), f32)
    na_ref[...] = lax.dot_general(ones, xa * xa, NT, precision=lax.Precision.HIGHEST, preferred_element_type=f32) * SCALE
    xah, xal = split2(xa * (2.0 * SCALE))
    xah_ref[...] = xah
    xal_ref[...] = xal
    acc_ref[...] = jnp.zeros_like(acc_ref)
    k = v_ref.shape[0]
    for x, v, note, side, (eh_ref, el_ref) in (
        (x_ref, v_ref, None, OWN, kept[:2]),
        (sib_x_ref, sib_v_ref.at[:k], sib_v_ref.at[k:], SIB, kept[2:]),
    ):
        for j in range(BLK_DEV):
            hit = want(pairs_ref, note, group, member, members, side, j)
            tiles_or_zeros(hit, x, xah_ref, xal_ref, na_ref, v, acc_ref, eh_ref, el_ref, j * block, block, j * block)


def cross_kernel(members, step, x_ref, v_ref, note_ref, pairs_ref, xah_ref, xal_ref, na_ref, in_ref, acc_ref, eh_ref, el_ref):
    group, member = place()
    rows = eh_ref.shape[0]
    q = quarter_at(members, step, group, member)
    acc_ref[...] = in_ref[...]
    hit = want(pairs_ref, note_ref, group, member, members, CROSS, (q * BLK_DEV) // members)
    tiles_or_zeros(hit, x_ref, xah_ref, xal_ref, na_ref, v_ref, acc_ref, eh_ref, el_ref, 0, rows, pl.multiple_of(q * rows, rows))


def gram_sum(vh, vm, vl):
    s = jnp.concatenate([vh, vm, vl], 0)
    k = vh.shape[0]
    p = dot(s, s, NT)
    r = p[:k] + (p[k : 2 * k] + p[2 * k :])
    return r[:, :k] + (r[:, k : 2 * k] + r[:, 2 * k :])


def gather_into(full_ref, pieces, members):
    _, member = place()
    quarter = pieces[0].shape[1]
    for k, piece in enumerate(pieces):
        q = lax.rem(member - k + members, members)
        full_ref[:, pl.ds(pl.multiple_of(q * quarter, quarter), quarter)] = piece[...]


def put_gram(gram_ref, image, total):
    gram = gram_sum(*split3(image)) / total
    half = gram.shape[0] // 2
    packed = jnp.concatenate([gram[:half], gram[half:]], 1)
    for n in range(gram_ref.shape[0]):
        gram_ref[n] = packed


def take_gram(gram_ref):
    packed = gram_ref[0]
    for n in range(1, gram_ref.shape[0]):
        packed = packed + gram_ref[n]
    k = packed.shape[1] // 2
    return jnp.concatenate([packed[:, :k], packed[:, k:]], 0)


def join_kernel(members, total, *refs):
    pieces, full_ref, gram_ref = refs[:members], refs[members], refs[members + 1]
    gather_into(full_ref, pieces, members)
    put_gram(gram_ref, full_ref[...], total)


def second_kernel(members, vo_ref, vs_ref, vc_ref, *refs):
    group, member = place()
    kept, out_ref = refs[:-1], refs[-1]
    out_ref[...] = jnp.zeros_like(out_ref)
    for v_ref, eh_ref, el_ref in ((vo_ref, kept[0], kept[1]), (vs_ref, kept[2], kept[3])):
        block = v_ref.shape[1] // BLK_DEV
        for j in range(BLK_DEV):
            here = pl.ds(j * block, block)
            add_product(out_ref, v_ref[:, here], eh_ref[here, :], el_ref[here, :])
    for step in range(members):
        eh_ref, el_ref = kept[4 + 2 * step : 6 + 2 * step]
        rows = eh_ref.shape[0]
        q = quarter_at(members, step, group, member)
        add_product(out_ref, vc_ref[:, pl.ds(pl.multiple_of(q * rows, rows), rows)], eh_ref[...], el_ref[...])


def factor_inverse(gram, w=8):
    k = gram.shape[0]
    rows = lax.broadcasted_iota(jnp.int32, (k, k), 0)
    cols = lax.broadcasted_iota(jnp.int32, (k, k), 1)
    aug = jnp.concatenate([gram, (rows == cols).astype(f32)], 1)
    tall, wide = 8, 2 * k
    a = [aug[t * tall : (t + 1) * tall, :] for t in range(k // tall)]
    sub = lax.broadcasted_iota(jnp.int32, (tall, wide), 0)
    spread = lambda x: jnp.broadcast_to(x, (tall, wide))
    for start in range(0, k, w):
        t, s = start // tall, start % tall
        r = [spread(a[t][s + i : s + i + 1, :]) for i in range(w)]
        d = [[spread(a[t][s + i : s + i + 1, start + j : start + j + 1]) if j >= i else None for j in range(w)] for i in range(w)]
        later = range(t if s + w < tall else t + 1, len(a))
        c = {u: [spread(a[u][:, start + i : start + i + 1]) for i in range(w)] for u in later}
        l = [[None] * w for _ in range(w)]
        inv = [None] * w
        for i in range(w):
            p = d[i][i]
            for m in range(i):
                p = p - l[i][m] * l[i][m]
            inv[i] = lax.rsqrt(p)
            for j in range(i + 1, w):
                q = d[i][j]
                for m in range(i):
                    q = q - l[i][m] * l[j][m]
                l[j][i] = q * inv[i]
        for i in range(w):
            for m in range(i):
                r[i] = r[i] - l[i][m] * r[m]
            r[i] = r[i] * inv[i]
        for u in later:
            x = c[u]
            for i in range(w):
                for m in range(i):
                    x[i] = x[i] - l[i][m] * x[m]
                x[i] = x[i] * inv[i]
            new = a[u]
            for i in range(w):
                new = new - x[i] * r[i]
            a[u] = new if u > t else jnp.where(sub < s + w, a[u], new)
        for i in range(w):
            a[t] = jnp.where(sub == s + i, r[i], a[t])
    return jnp.concatenate(a, 0)[:, k:]


def factor_kernel(a_ref, b_ref, inv_ref):
    inv_ref[...] = factor_inverse(take_gram(a_ref) + take_gram(b_ref))


def exact(a, b):
    return lax.dot_general(a, b, NN, precision=lax.Precision.HIGHEST, preferred_element_type=f32)


def image_kernel(members, total, inv_ref, *refs):
    pieces, image_ref, gram_ref = refs[:members], refs[members], refs[members + 1]
    gather_into(image_ref, pieces, members)
    image_ref[...] = exact(inv_ref[...], image_ref[...])
    put_gram(gram_ref, image_ref[...], total)


def last_kernel(gram_ref, image_ref, out_ref):
    out_ref[...] = exact(factor_inverse(take_gram(gram_ref)), image_ref[...])


VM = pl.BlockSpec(memory_space=pltpu.VMEM)
SM = pl.BlockSpec(memory_space=pltpu.SMEM)


def call(body, specs, outs, name, limit=16, flops=10**9):
    return pl.pallas_call(
        body,
        in_specs=specs,
        out_specs=[VM] * len(outs),
        out_shape=[jax.ShapeDtypeStruct(s, t) for s, t in outs],
        compiler_params=pltpu.CompilerParams(vmem_limit_bytes=limit * MB),
        cost_estimate=pl.CostEstimate(flops=flops, bytes_accessed=MB, transcendentals=0),
        name=name,
    )


def shifted(x, axis, by):
    n = lax.axis_size(axis)
    return lax.ppermute(x, axis, [(i, (i + by) % n) for i in range(n)])


def crossed(x):
    n = lax.axis_size("rows")
    return lax.ppermute(x, "rows", [(i, (i + 2 * (i % 2) - 1) % n) for i in range(n)])


def swapped(x):
    return lax.ppermute(x, "rows", [(i, i ^ 1) for i in range(lax.axis_size("rows"))])


def passed_on(x):
    groups, members = lax.axis_size("rows"), lax.axis_size("sub")
    at = lambda g, m: g * members + m % members
    return lax.ppermute(x, ("rows", "sub"), [(at(g, m), at(g, m + 1 - 2 * (g % 2))) for g in range(groups) for m in range(members)])


NEAR = 8


def far_sets():
    groups, members = lax.axis_size("rows"), lax.axis_size("sub")
    return [[g * members + m for g in range(low, groups, NEAR)] for low in range(NEAR) for m in range(members)]


def near_sets():
    groups, members = lax.axis_size("rows"), lax.axis_size("sub")
    return [[g * members + m for g in range(base, base + NEAR)] for base in range(0, groups, NEAR) for m in range(members)]


def exchanged(x, sets):
    return lax.all_to_all(x, ("rows", "sub"), 0, 0, axis_index_groups=sets)


MASKS = (1, 2, 6, 8, 16, 48)


def pair_sums(gram):
    for mask in MASKS:
        pairs = [(i, i ^ mask) for i in range(lax.axis_size("rows"))]
        other = lax.ppermute(gram, "rows", pairs)
        gram = gram + other if mask != MASKS[-1] else (gram, other)
    return gram


def tie(x, *others):
    return lax.optimization_barrier((x, *others))[0]


def on_device(embeddings, start_vectors, pairs):
    members = lax.axis_size("sub")
    groups = lax.axis_size("rows")
    rows, width = embeddings.shape
    k = start_vectors.shape[1]
    quarter = rows // members
    total = rows * groups
    vt = start_vectors.T
    cross_v = crossed(vt)
    piece = ((quarter, width), f32)
    first, second, third, sib_v = call(
        functools.partial(cut_kernel, members), [VM, VM, SM],
        [((quarter + NOTE, width), f32), piece, piece, ((k + NOTE, rows), f32)], "cut", flops=10**6)(embeddings, vt, pairs)
    arrived = [crossed(first)]
    sib_e = swapped(embeddings)
    sib_v = swapped(sib_v)
    arrived.append(crossed(second))
    arrived.append(crossed(third))
    cross_note = arrived[0][quarter:]
    part = ((k, quarter), f32)
    tiles = lambda n: [((n, quarter), bf16)] * 2
    xah, xal, na, acc, *kept = call(
        functools.partial(chip_kernel, members), [VM, VM, VM, VM, SM],
        [((quarter, width), bf16)] * 2 + [((8, quarter), f32), part] + tiles(rows) + tiles(rows), "chip_tiles",
        flops=10**10)(embeddings, vt, sib_e, sib_v, pairs)
    arrived.append(passed_on(arrived[0]))
    for step in (0, 3, 1, 2):
        acc, *t = call(
            functools.partial(cross_kernel, members, step), [VM, VM, VM, SM, VM, VM, VM, VM], [part] + tiles(quarter), "cross_tiles",
            flops=2 * 10**9)(arrived[step], cross_v, cross_note, pairs, xah, xal, na, acc)
        arrived[step] = t
    for t in arrived:
        kept += t
    pieces = [acc] + [shifted(acc, "sub", s) for s in range(1, members)]
    whole = ((k, rows), f32)
    far, near = far_sets(), near_sets()
    grams = lambda sets: ((len(sets[0]), k // 2, 2 * k), f32)
    image, gram = call(functools.partial(join_kernel, members, total), [VM] * members, [whole, ((1, k // 2, 2 * k), f32)], "join")(*pieces)
    cross_i = crossed(image)
    sib_i = swapped(image)
    grams_1 = pair_sums(gram)
    (acc2,) = call(functools.partial(second_kernel, members), [VM] * (3 + len(kept)), [part], "second_product")(
        image, sib_i, cross_i, *kept)
    pieces = [acc2] + [shifted(acc2, "sub", s) for s in range(1, members)]
    (inv,) = call(factor_kernel, [VM, VM], [((k, k), f32)], "factor")(*grams_1)
    image, gram = call(functools.partial(image_kernel, members, total), [VM] * (1 + members), [whole, grams(far)], "image")(inv, *pieces)
    gram = exchanged(gram, far)
    gram = exchanged(jnp.broadcast_to(gram.sum(0)[None], grams(near)[0]), near)
    (out,) = call(last_kernel, [VM, VM], [whole], "last")(gram, image)
    return out.T


def solution(mesh):
    return jax.shard_map(
        on_device,
        mesh=mesh,
        in_specs=(P("rows", None), P("rows", None), P("rows", None)),
        out_specs=P("rows", None),
        check_vma=False,
    )
```

```python
import functools
import jax
import jax.numpy as jnp
from jax import lax
from jax.experimental import pallas as pl
from jax.experimental.pallas import tpu as pltpu
from jax.sharding import PartitionSpec as P

BLK_DEV = 2
OWN, SIB, CROSS = 0, 1, -1
NOTE = 8
MB = 1024 * 1024
LOG2E = 1.4426950408889634
SCALE = LOG2E / 64.0

f32 = jnp.float32
bf16 = jnp.bfloat16
NN = (((1,), (0,)), ((), ()))
NT = (((1,), (1,)), ((), ()))


def dot(a, b, dims):
    return lax.dot_general(a, b, dims, preferred_element_type=f32)


def split2(x):
    hi = x.astype(bf16)
    return hi, (x - hi.astype(f32)).astype(bf16)


def split3(x):
    hi = x.astype(bf16)
    rest = x - hi.astype(f32)
    mid = rest.astype(bf16)
    return hi, mid, (rest - mid.astype(f32)).astype(bf16)


def listed(pairs_ref, row_block, col_block):
    hit = jnp.int32(0)
    for slot in range(pairs_ref.shape[1]):
        same = (pairs_ref[0, slot] == row_block) & (pairs_ref[1, slot] == col_block)
        hit = hit | same.astype(jnp.int32)
    return hit > 0


def place():
    group = lax.axis_index("rows")
    member = lax.axis_index("sub")
    return group, member


def want(pairs_ref, note_ref, group, member, members, side, j):
    mine = group * BLK_DEV + (member * BLK_DEV) // members
    other = (group + side * (1 - 2 * (group & 1))) * BLK_DEV + j
    low, high = jnp.minimum(mine, other), jnp.maximum(mine, other)
    hit = listed(pairs_ref, low, high)
    if note_ref is not None:
        slot = lax.broadcasted_iota(jnp.int32, (1, note_ref.shape[1]), 1) < pairs_ref.shape[1]
        same = slot & (note_ref[0:1, :] == low.astype(f32)) & (note_ref[1:2, :] == high.astype(f32))
        hit = hit | (jnp.max(same.astype(f32)) > 0.5)
    return hit


def quarter_at(members, step, group, member):
    return (member + step * (1 - 2 * (group & 1))) & (members - 1)


def add_product(acc_ref, v, eh, el):
    vh, vm, vl = split3(v)
    k = vh.shape[0]
    one = dot(jnp.concatenate([vh, vm, vl], 0), eh, NN)
    two = dot(jnp.concatenate([vh, vm], 0), el, NN)
    acc_ref[...] += (one[:k] + two[:k]) + (one[k : 2 * k] + two[k:] + one[2 * k :])


def tiles_or_zeros(hit, x_ref, xah_ref, xal_ref, na_ref, v_ref, acc_ref, eh_ref, el_ref, start, rows, v_start, chunk=256):
    @pl.when(hit)
    def _():
        xah, xal, na = xah_ref[...], xal_ref[...], na_ref[0:1, :]
        for c in range(rows // chunk):
            here = pl.ds(start + c * chunk, chunk)
            x = x_ref[here, :]
            nb = jnp.sum(x * x, axis=1, keepdims=True) * SCALE
            xh, xl = split2(x)
            d = dot(xh, xah, NT) + (dot(xh, xal, NT) + dot(xl, xah, NT))
            e = jnp.exp2(jnp.minimum(d - nb - na, 0.0))
            eh, el = split2(e)
            eh_ref[here, :] = eh
            el_ref[here, :] = el
        here = pl.ds(start, rows)
        add_product(acc_ref, v_ref[:, pl.ds(v_start, rows)], eh_ref[here, :], el_ref[here, :])

    @pl.when(jnp.logical_not(hit))
    def _():
        here = pl.ds(start, rows)
        eh_ref[here, :] = jnp.zeros((rows, eh_ref.shape[1]), bf16)
        el_ref[here, :] = jnp.zeros((rows, el_ref.shape[1]), bf16)


def cut_kernel(members, x_ref, v_ref, pairs_ref, *refs):
    group, member = place()
    outs, sib_ref, sems = refs[:-2], refs[-2], refs[-1]
    quarter, width = outs[1].shape
    k = v_ref.shape[0]
    copies = [pltpu.make_async_copy(v_ref, sib_ref.at[pl.ds(0, k)], sems.at[len(outs)])]
    for step, out_ref in enumerate(outs):
        q = quarter_at(members, -step, group, member)
        source = x_ref.at[pl.ds(pl.multiple_of(q * quarter, quarter), quarter)]
        copies.append(pltpu.make_async_copy(source, out_ref.at[pl.ds(0, quarter)], sems.at[step]))
    for copy in copies:
        copy.start()
    lane = lax.broadcasted_iota(jnp.int32, (NOTE, width), 1)
    row = lax.broadcasted_iota(jnp.int32, (NOTE, width), 0)
    note = jnp.zeros((NOTE, width), f32)
    for slot in range(pairs_ref.shape[1]):
        for c in range(2):
            note = jnp.where((lane == slot) & (row == c), pairs_ref[c, slot].astype(f32), note)
    sib_ref[k:, :width] = note
    sib_ref[k:, width:] = jnp.zeros((NOTE, sib_ref.shape[1] - width), f32)
    outs[0][quarter:, :] = note
    for copy in copies:
        copy.wait()


def chip_kernel(members, x_ref, v_ref, sib_x_ref, sib_v_ref, pairs_ref, xah_ref, xal_ref, na_ref, acc_ref, *kept):
    group, member = place()
    rows = x_ref.shape[0]
    quarter = rows // members
    block = rows // BLK_DEV
    xa = x_ref[pl.ds(pl.multiple_of(member * quarter, quarter), quarter), :]
    ones = jnp.ones((8, xa.shape[1]), f32)
    na_ref[...] = lax.dot_general(ones, xa * xa, NT, precision=lax.Precision.HIGHEST, preferred_element_type=f32) * SCALE
    xah, xal = split2(xa * (2.0 * SCALE))
    xah_ref[...] = xah
    xal_ref[...] = xal
    acc_ref[...] = jnp.zeros_like(acc_ref)
    k = v_ref.shape[0]
    for x, v, note, side, (eh_ref, el_ref) in (
        (x_ref, v_ref, None, OWN, kept[:2]),
        (sib_x_ref, sib_v_ref.at[:k], sib_v_ref.at[k:], SIB, kept[2:]),
    ):
        for j in range(BLK_DEV):
            hit = want(pairs_ref, note, group, member, members, side, j)
            tiles_or_zeros(hit, x, xah_ref, xal_ref, na_ref, v, acc_ref, eh_ref, el_ref, j * block, block, j * block)


def cross_kernel(members, step, x_ref, v_ref, note_ref, pairs_ref, xah_ref, xal_ref, na_ref, in_ref, acc_ref, eh_ref, el_ref):
    group, member = place()
    rows = eh_ref.shape[0]
    q = quarter_at(members, step, group, member)
    acc_ref[...] = in_ref[...]
    hit = want(pairs_ref, note_ref, group, member, members, CROSS, (q * BLK_DEV) // members)
    tiles_or_zeros(hit, x_ref, xah_ref, xal_ref, na_ref, v_ref, acc_ref, eh_ref, el_ref, 0, rows, pl.multiple_of(q * rows, rows))


def gram_sum(vh, vm, vl):
    s = jnp.concatenate([vh, vm, vl], 0)
    k = vh.shape[0]
    p = dot(s, s, NT)
    r = p[:k] + (p[k : 2 * k] + p[2 * k :])
    return r[:, :k] + (r[:, k : 2 * k] + r[:, 2 * k :])


def gather_into(full_ref, pieces, members):
    _, member = place()
    quarter = pieces[0].shape[1]
    for k, piece in enumerate(pieces):
        q = lax.rem(member - k + members, members)
        full_ref[:, pl.ds(pl.multiple_of(q * quarter, quarter), quarter)] = piece[...]


def put_gram(gram_ref, image, total):
    gram = gram_sum(*split3(image)) / total
    half = gram.shape[0] // 2
    packed = jnp.concatenate([gram[:half], gram[half:]], 1)
    for n in range(gram_ref.shape[0]):
        gram_ref[n] = packed


def take_gram(gram_ref):
    packed = gram_ref[0]
    for n in range(1, gram_ref.shape[0]):
        packed = packed + gram_ref[n]
    k = packed.shape[1] // 2
    return jnp.concatenate([packed[:, :k], packed[:, k:]], 0)


def join_kernel(members, total, *refs):
    pieces, full_ref, gram_ref = refs[:members], refs[members], refs[members + 1]
    gather_into(full_ref, pieces, members)
    put_gram(gram_ref, full_ref[...], total)


def second_kernel(members, vo_ref, vs_ref, vc_ref, *refs):
    group, member = place()
    kept, out_ref = refs[:-1], refs[-1]
    out_ref[...] = jnp.zeros_like(out_ref)
    for v_ref, eh_ref, el_ref in ((vo_ref, kept[0], kept[1]), (vs_ref, kept[2], kept[3])):
        block = v_ref.shape[1] // BLK_DEV
        for j in range(BLK_DEV):
            here = pl.ds(j * block, block)
            add_product(out_ref, v_ref[:, here], eh_ref[here, :], el_ref[here, :])
    for step in range(members):
        eh_ref, el_ref = kept[4 + 2 * step : 6 + 2 * step]
        rows = eh_ref.shape[0]
        q = quarter_at(members, step, group, member)
        add_product(out_ref, vc_ref[:, pl.ds(pl.multiple_of(q * rows, rows), rows)], eh_ref[...], el_ref[...])


def factor_inverse(gram, w=8):
    k = gram.shape[0]
    rows = lax.broadcasted_iota(jnp.int32, (k, k), 0)
    cols = lax.broadcasted_iota(jnp.int32, (k, k), 1)
    aug = jnp.concatenate([gram, (rows == cols).astype(f32)], 1)
    tall, wide = 8, 2 * k
    a = [aug[t * tall : (t + 1) * tall, :] for t in range(k // tall)]
    sub = lax.broadcasted_iota(jnp.int32, (tall, wide), 0)
    spread = lambda x: jnp.broadcast_to(x, (tall, wide))
    for start in range(0, k, w):
        t, s = start // tall, start % tall
        r = [spread(a[t][s + i : s + i + 1, :]) for i in range(w)]
        d = [[spread(a[t][s + i : s + i + 1, start + j : start + j + 1]) if j >= i else None for j in range(w)] for i in range(w)]
        later = range(t if s + w < tall else t + 1, len(a))
        c = {u: [spread(a[u][:, start + i : start + i + 1]) for i in range(w)] for u in later}
        l = [[None] * w for _ in range(w)]
        inv = [None] * w
        for i in range(w):
            p = d[i][i]
            for m in range(i):
                p = p - l[i][m] * l[i][m]
            inv[i] = lax.rsqrt(p)
            for j in range(i + 1, w):
                q = d[i][j]
                for m in range(i):
                    q = q - l[i][m] * l[j][m]
                l[j][i] = q * inv[i]
        for i in range(w):
            for m in range(i):
                r[i] = r[i] - l[i][m] * r[m]
            r[i] = r[i] * inv[i]
        for u in later:
            x = c[u]
            for i in range(w):
                for m in range(i):
                    x[i] = x[i] - l[i][m] * x[m]
                x[i] = x[i] * inv[i]
            new = a[u]
            for i in range(w):
                new = new - x[i] * r[i]
            a[u] = new if u > t else jnp.where(sub < s + w, a[u], new)
        for i in range(w):
            a[t] = jnp.where(sub == s + i, r[i], a[t])
    return jnp.concatenate(a, 0)[:, k:]


def factor_kernel(a_ref, b_ref, inv_ref):
    inv_ref[...] = factor_inverse(take_gram(a_ref) + take_gram(b_ref))


def exact(a, b):
    return lax.dot_general(a, b, NN, precision=lax.Precision.HIGHEST, preferred_element_type=f32)


def image_kernel(members, total, inv_ref, *refs):
    pieces, image_ref, gram_ref = refs[:members], refs[members], refs[members + 1]
    gather_into(image_ref, pieces, members)
    image_ref[...] = exact(inv_ref[...], image_ref[...])
    put_gram(gram_ref, image_ref[...], total)


def last_kernel(gram_ref, image_ref, out_ref):
    out_ref[...] = exact(factor_inverse(take_gram(gram_ref)), image_ref[...])


VM = pl.BlockSpec(memory_space=pltpu.VMEM)
SM = pl.BlockSpec(memory_space=pltpu.SMEM)
HB = pl.BlockSpec(memory_space=pltpu.HBM)


def call(body, specs, outs, name, limit=16, flops=10**9, scratch=()):
    return pl.pallas_call(
        body,
        in_specs=specs,
        out_specs=[VM] * len(outs),
        scratch_shapes=scratch,
        out_shape=[jax.ShapeDtypeStruct(s, t) for s, t in outs],
        compiler_params=pltpu.CompilerParams(vmem_limit_bytes=limit * MB),
        cost_estimate=pl.CostEstimate(flops=flops, bytes_accessed=MB, transcendentals=0),
        name=name,
    )


def shifted(x, axis, by):
    n = lax.axis_size(axis)
    return lax.ppermute(x, axis, [(i, (i + by) % n) for i in range(n)])


def crossed(x):
    n = lax.axis_size("rows")
    return lax.ppermute(x, "rows", [(i, (i + 2 * (i % 2) - 1) % n) for i in range(n)])


def swapped(x):
    return lax.ppermute(x, "rows", [(i, i ^ 1) for i in range(lax.axis_size("rows"))])


def passed_on(x):
    groups, members = lax.axis_size("rows"), lax.axis_size("sub")
    at = lambda g, m: g * members + m % members
    return lax.ppermute(x, ("rows", "sub"), [(at(g, m), at(g, m + 1 - 2 * (g % 2))) for g in range(groups) for m in range(members)])


NEAR = 8


def far_sets():
    groups, members = lax.axis_size("rows"), lax.axis_size("sub")
    return [[g * members + m for g in range(low, groups, NEAR)] for low in range(NEAR) for m in range(members)]


def near_sets():
    groups, members = lax.axis_size("rows"), lax.axis_size("sub")
    return [[g * members + m for g in range(base, base + NEAR)] for base in range(0, groups, NEAR) for m in range(members)]


def exchanged(x, sets):
    return lax.all_to_all(x, ("rows", "sub"), 0, 0, axis_index_groups=sets)


MASKS = (1, 2, 6, 8, 16, 48)


def pair_sums(gram):
    for mask in MASKS:
        pairs = [(i, i ^ mask) for i in range(lax.axis_size("rows"))]
        other = lax.ppermute(gram, "rows", pairs)
        gram = gram + other if mask != MASKS[-1] else (gram, other)
    return gram


def tie(x, *others):
    return lax.optimization_barrier((x, *others))[0]


def on_device(embeddings, start_vectors, pairs):
    members = lax.axis_size("sub")
    groups = lax.axis_size("rows")
    rows, width = embeddings.shape
    k = start_vectors.shape[1]
    quarter = rows // members
    total = rows * groups
    vt = start_vectors.T
    pairs = pairs.T
    cross_v = crossed(vt)
    piece = ((quarter, width), f32)
    first, second, third, sib_v = call(
        functools.partial(cut_kernel, members), [HB, HB, SM],
        [((quarter + NOTE, width), f32), piece, piece, ((k + NOTE, rows), f32)], "cut", flops=10**6,
        scratch=[pltpu.SemaphoreType.DMA((4,))])(
        *(pltpu.with_memory_space_constraint(a, pltpu.HBM) for a in (embeddings, vt)), pairs)
    arrived = [crossed(first)]
    sib_e = swapped(embeddings)
    sib_v = swapped(sib_v)
    arrived.append(crossed(second))
    arrived.append(crossed(third))
    cross_note = arrived[0][quarter:]
    part = ((k, quarter), f32)
    tiles = lambda n: [((n, quarter), bf16)] * 2
    xah, xal, na, acc, *kept = call(
        functools.partial(chip_kernel, members), [VM, VM, VM, VM, SM],
        [((quarter, width), bf16)] * 2 + [((8, quarter), f32), part] + tiles(rows) + tiles(rows), "chip_tiles",
        flops=10**10)(embeddings, vt, sib_e, sib_v, pairs)
    arrived.append(passed_on(arrived[0]))
    for step in (0, 3, 1, 2):
        acc, *t = call(
            functools.partial(cross_kernel, members, step), [VM, VM, VM, SM, VM, VM, VM, VM], [part] + tiles(quarter), "cross_tiles",
            flops=2 * 10**9)(arrived[step], cross_v, cross_note, pairs, xah, xal, na, acc)
        arrived[step] = t
    for t in arrived:
        kept += t
    pieces = [acc] + [shifted(acc, "sub", s) for s in range(1, members)]
    whole = ((k, rows), f32)
    far, near = far_sets(), near_sets()
    grams = lambda sets: ((len(sets[0]), k // 2, 2 * k), f32)
    image, gram = call(functools.partial(join_kernel, members, total), [VM] * members, [whole, ((1, k // 2, 2 * k), f32)], "join")(*pieces)
    cross_i = crossed(image)
    sib_i = swapped(image)
    grams_1 = pair_sums(gram)
    (acc2,) = call(functools.partial(second_kernel, members), [VM] * (3 + len(kept)), [part], "second_product")(
        image, sib_i, cross_i, *kept)
    pieces = [acc2] + [shifted(acc2, "sub", s) for s in range(1, members)]
    (inv,) = call(factor_kernel, [VM, VM], [((k, k), f32)], "factor")(*grams_1)
    image, gram = call(functools.partial(image_kernel, members, total), [VM] * (1 + members), [whole, grams(far)], "image")(inv, *pieces)
    gram = exchanged(gram, far)
    gram = exchanged(jnp.broadcast_to(gram.sum(0)[None], grams(near)[0]), near)
    (out,) = call(last_kernel, [VM, VM], [whole], "last")(gram, image)
    return out.T


def solution(mesh):
    return jax.shard_map(
        on_device,
        mesh=mesh,
        in_specs=(P("rows", None), P("rows", None), P("rows", None)),
        out_specs=P("rows", None),
        check_vma=False,
    )
```

```python
import functools
import jax
import jax.numpy as jnp
from jax import lax
from jax.experimental import pallas as pl
from jax.experimental.pallas import tpu as pltpu
from jax.sharding import PartitionSpec as P

BLK_DEV = 2
OWN, SIB, CROSS = 0, 1, -1
NOTE = 8
MB = 1024 * 1024
LOG2E = 1.4426950408889634
SCALE = LOG2E / 64.0

f32 = jnp.float32
bf16 = jnp.bfloat16
NN = (((1,), (0,)), ((), ()))
NT = (((1,), (1,)), ((), ()))


def dot(a, b, dims):
    return lax.dot_general(a, b, dims, preferred_element_type=f32)


def split2(x):
    hi = x.astype(bf16)
    return hi, (x - hi.astype(f32)).astype(bf16)


def split3(x):
    hi = x.astype(bf16)
    rest = x - hi.astype(f32)
    mid = rest.astype(bf16)
    return hi, mid, (rest - mid.astype(f32)).astype(bf16)


def listed(pairs_ref, row_block, col_block):
    hit = jnp.int32(0)
    for slot in range(pairs_ref.shape[1]):
        same = (pairs_ref[0, slot] == row_block) & (pairs_ref[1, slot] == col_block)
        hit = hit | same.astype(jnp.int32)
    return hit > 0


def place():
    group = lax.axis_index("rows")
    member = lax.axis_index("sub")
    return group, member


def want(pairs_ref, note_ref, group, member, members, side, j):
    mine = group * BLK_DEV + (member * BLK_DEV) // members
    other = (group + side * (1 - 2 * (group & 1))) * BLK_DEV + j
    low, high = jnp.minimum(mine, other), jnp.maximum(mine, other)
    hit = listed(pairs_ref, low, high)
    if note_ref is not None:
        slot = lax.broadcasted_iota(jnp.int32, (1, note_ref.shape[1]), 1) < pairs_ref.shape[1]
        same = slot & (note_ref[0:1, :] == low.astype(f32)) & (note_ref[1:2, :] == high.astype(f32))
        hit = hit | (jnp.max(same.astype(f32)) > 0.5)
    return hit


def quarter_at(members, step, group, member):
    return (member + step * (1 - 2 * (group & 1))) & (members - 1)


def add_product(acc_ref, v, eh, el):
    vh, vm, vl = split3(v)
    k = vh.shape[0]
    one = dot(jnp.concatenate([vh, vm, vl], 0), eh, NN)
    two = dot(jnp.concatenate([vh, vm], 0), el, NN)
    acc_ref[...] += (one[:k] + two[:k]) + (one[k : 2 * k] + two[k:] + one[2 * k :])


def tiles_or_zeros(hit, x_ref, xah_ref, xal_ref, na_ref, v_ref, acc_ref, eh_ref, el_ref, start, rows, v_start, chunk=256):
    @pl.when(hit)
    def _():
        xah, xal, na = xah_ref[...], xal_ref[...], na_ref[0:1, :]
        for c in range(rows // chunk):
            here = pl.ds(start + c * chunk, chunk)
            x = x_ref[here, :]
            nb = jnp.sum(x * x, axis=1, keepdims=True) * SCALE
            xh, xl = split2(x)
            d = dot(xh, xah, NT) + (dot(xh, xal, NT) + dot(xl, xah, NT))
            e = jnp.exp2(jnp.minimum(d - nb - na, 0.0))
            eh, el = split2(e)
            eh_ref[here, :] = eh
            el_ref[here, :] = el
        here = pl.ds(start, rows)
        add_product(acc_ref, v_ref[:, pl.ds(v_start, rows)], eh_ref[here, :], el_ref[here, :])

    @pl.when(jnp.logical_not(hit))
    def _():
        here = pl.ds(start, rows)
        eh_ref[here, :] = jnp.zeros((rows, eh_ref.shape[1]), bf16)
        el_ref[here, :] = jnp.zeros((rows, el_ref.shape[1]), bf16)


def cut_kernel(members, x_ref, v_ref, pairs_ref, *refs):
    group, member = place()
    outs, sib_ref, sems = refs[:-2], refs[-2], refs[-1]
    quarter, width = outs[1].shape
    k = v_ref.shape[0]
    copies = [pltpu.make_async_copy(v_ref, sib_ref.at[pl.ds(0, k)], sems.at[len(outs)])]
    for step, out_ref in enumerate(outs):
        q = quarter_at(members, -step, group, member)
        source = x_ref.at[pl.ds(pl.multiple_of(q * quarter, quarter), quarter)]
        copies.append(pltpu.make_async_copy(source, out_ref.at[pl.ds(0, quarter)], sems.at[step]))
    for copy in copies:
        copy.start()
    lane = lax.broadcasted_iota(jnp.int32, (NOTE, width), 1)
    row = lax.broadcasted_iota(jnp.int32, (NOTE, width), 0)
    note = jnp.zeros((NOTE, width), f32)
    for slot in range(pairs_ref.shape[1]):
        for c in range(2):
            note = jnp.where((lane == slot) & (row == c), pairs_ref[c, slot].astype(f32), note)
    sib_ref[k:, :width] = note
    sib_ref[k:, width:] = jnp.zeros((NOTE, sib_ref.shape[1] - width), f32)
    outs[0][quarter:, :] = note
    for copy in copies:
        copy.wait()


def chip_kernel(members, x_ref, v_ref, sib_x_ref, sib_v_ref, pairs_ref, xah_ref, xal_ref, na_ref, acc_ref, *kept):
    group, member = place()
    rows = x_ref.shape[0]
    quarter = rows // members
    block = rows // BLK_DEV
    xa = x_ref[pl.ds(pl.multiple_of(member * quarter, quarter), quarter), :]
    ones = jnp.ones((8, xa.shape[1]), f32)
    na_ref[...] = lax.dot_general(ones, xa * xa, NT, precision=lax.Precision.HIGHEST, preferred_element_type=f32) * SCALE
    xah, xal = split2(xa * (2.0 * SCALE))
    xah_ref[...] = xah
    xal_ref[...] = xal
    acc_ref[...] = jnp.zeros_like(acc_ref)
    k = v_ref.shape[0]
    for x, v, note, side, (eh_ref, el_ref) in (
        (x_ref, v_ref, None, OWN, kept[:2]),
        (sib_x_ref, sib_v_ref.at[:k], sib_v_ref.at[k:], SIB, kept[2:]),
    ):
        for j in range(BLK_DEV):
            hit = want(pairs_ref, note, group, member, members, side, j)
            tiles_or_zeros(hit, x, xah_ref, xal_ref, na_ref, v, acc_ref, eh_ref, el_ref, j * block, block, j * block)


def cross_kernel(members, steps, *refs):
    n = len(steps)
    x_refs, (v_ref, note_ref, pairs_ref, xah_ref, xal_ref, na_ref, in_ref, acc_ref), kept = refs[:n], refs[n : n + 8], refs[n + 8 :]
    group, member = place()
    rows = kept[0].shape[0]
    acc_ref[...] = in_ref[...]
    for i, step in enumerate(steps):
        eh_ref, el_ref = kept[2 * i : 2 * i + 2]
        q = quarter_at(members, step, group, member)
        hit = want(pairs_ref, note_ref, group, member, members, CROSS, (q * BLK_DEV) // members)
        tiles_or_zeros(hit, x_refs[i], xah_ref, xal_ref, na_ref, v_ref, acc_ref, eh_ref, el_ref, 0, rows, pl.multiple_of(q * rows, rows))


def gram_sum(vh, vm, vl):
    s = jnp.concatenate([vh, vm, vl], 0)
    k = vh.shape[0]
    p = dot(s, s, NT)
    r = p[:k] + (p[k : 2 * k] + p[2 * k :])
    return r[:, :k] + (r[:, k : 2 * k] + r[:, 2 * k :])


def gather_into(full_ref, pieces, members):
    _, member = place()
    quarter = pieces[0].shape[1]
    for k, piece in enumerate(pieces):
        q = lax.rem(member - k + members, members)
        full_ref[:, pl.ds(pl.multiple_of(q * quarter, quarter), quarter)] = piece[...]


def put_gram(gram_ref, image, total):
    gram = gram_sum(*split3(image)) / total
    half = gram.shape[0] // 2
    packed = jnp.concatenate([gram[:half], gram[half:]], 1)
    for n in range(gram_ref.shape[0]):
        gram_ref[n] = packed


def take_gram(terms):
    me, opposite, left, right = (ref[...] for ref in terms)
    packed = (me + opposite) + (left + right)
    k = packed.shape[1] // 2
    return jnp.concatenate([packed[:, :k], packed[:, k:]], 0)


def join_kernel(members, total, *refs):
    pieces, full_ref, gram_ref = refs[:members], refs[members], refs[members + 1]
    gather_into(full_ref, pieces, members)
    put_gram(gram_ref, full_ref[...], total)


def second_kernel(members, vo_ref, vs_ref, vc_ref, *refs):
    group, member = place()
    kept, out_ref = refs[:-1], refs[-1]
    out_ref[...] = jnp.zeros_like(out_ref)
    for v_ref, eh_ref, el_ref in ((vo_ref, kept[0], kept[1]), (vs_ref, kept[2], kept[3])):
        block = v_ref.shape[1] // BLK_DEV
        for j in range(BLK_DEV):
            here = pl.ds(j * block, block)
            add_product(out_ref, v_ref[:, here], eh_ref[here, :], el_ref[here, :])
    for step in range(members):
        eh_ref, el_ref = kept[4 + 2 * step : 6 + 2 * step]
        rows = eh_ref.shape[0]
        q = quarter_at(members, step, group, member)
        add_product(out_ref, vc_ref[:, pl.ds(pl.multiple_of(q * rows, rows), rows)], eh_ref[...], el_ref[...])


def factor_inverse(gram, w=8):
    k = gram.shape[0]
    rows = lax.broadcasted_iota(jnp.int32, (k, k), 0)
    cols = lax.broadcasted_iota(jnp.int32, (k, k), 1)
    aug = jnp.concatenate([gram, (rows == cols).astype(f32)], 1)
    tall, wide = 8, 2 * k
    a = [aug[t * tall : (t + 1) * tall, :] for t in range(k // tall)]
    sub = lax.broadcasted_iota(jnp.int32, (tall, wide), 0)
    spread = lambda x: jnp.broadcast_to(x, (tall, wide))
    for start in range(0, k, w):
        t, s = start // tall, start % tall
        r = [spread(a[t][s + i : s + i + 1, :]) for i in range(w)]
        d = [[spread(a[t][s + i : s + i + 1, start + j : start + j + 1]) if j >= i else None for j in range(w)] for i in range(w)]
        later = range(t if s + w < tall else t + 1, len(a))
        c = {u: [spread(a[u][:, start + i : start + i + 1]) for i in range(w)] for u in later}
        l = [[None] * w for _ in range(w)]
        inv = [None] * w
        for i in range(w):
            p = d[i][i]
            for m in range(i):
                p = p - l[i][m] * l[i][m]
            inv[i] = lax.rsqrt(p)
            for j in range(i + 1, w):
                q = d[i][j]
                for m in range(i):
                    q = q - l[i][m] * l[j][m]
                l[j][i] = q * inv[i]
        for i in range(w):
            for m in range(i):
                r[i] = r[i] - l[i][m] * r[m]
            r[i] = r[i] * inv[i]
        for u in later:
            x = c[u]
            for i in range(w):
                for m in range(i):
                    x[i] = x[i] - l[i][m] * x[m]
                x[i] = x[i] * inv[i]
            new = a[u]
            for i in range(w):
                new = new - x[i] * r[i]
            a[u] = new if u > t else jnp.where(sub < s + w, a[u], new)
        for i in range(w):
            a[t] = jnp.where(sub == s + i, r[i], a[t])
    return jnp.concatenate(a, 0)[:, k:]


def factor_kernel(*refs):
    inv_ref = refs[-1]
    inv_ref[...] = factor_inverse(take_gram(refs[:-1]))


def exact(a, b):
    return lax.dot_general(a, b, NN, precision=lax.Precision.HIGHEST, preferred_element_type=f32)


def image_kernel(members, total, inv_ref, *refs):
    pieces, image_ref, gram_ref = refs[:members], refs[members], refs[members + 1]
    gather_into(image_ref, pieces, members)
    image_ref[...] = exact(inv_ref[...], image_ref[...])
    put_gram(gram_ref, image_ref[...], total)


def last_kernel(image_ref, *refs):
    out_ref = refs[-1]
    out_ref[...] = exact(factor_inverse(take_gram(refs[:-1])), image_ref[...])


VM = pl.BlockSpec(memory_space=pltpu.VMEM)
SM = pl.BlockSpec(memory_space=pltpu.SMEM)
HB = pl.BlockSpec(memory_space=pltpu.HBM)


def call(body, specs, outs, name, limit=16, flops=10**9, scratch=()):
    return pl.pallas_call(
        body,
        in_specs=specs,
        out_specs=[VM] * len(outs),
        scratch_shapes=scratch,
        out_shape=[jax.ShapeDtypeStruct(s, t) for s, t in outs],
        compiler_params=pltpu.CompilerParams(vmem_limit_bytes=limit * MB),
        cost_estimate=pl.CostEstimate(flops=flops, bytes_accessed=MB, transcendentals=0),
        name=name,
    )


def shifted(x, axis, by):
    n = lax.axis_size(axis)
    return lax.ppermute(x, axis, [(i, (i + by) % n) for i in range(n)])


def crossed(x):
    n = lax.axis_size("rows")
    return lax.ppermute(x, "rows", [(i, (i + 2 * (i % 2) - 1) % n) for i in range(n)])


def swapped(x):
    return lax.ppermute(x, "rows", [(i, i ^ 1) for i in range(lax.axis_size("rows"))])


def passed_on(x):
    groups, members = lax.axis_size("rows"), lax.axis_size("sub")
    at = lambda g, m: g * members + m % members
    return lax.ppermute(x, ("rows", "sub"), [(at(g, m), at(g, m + 1 - 2 * (g % 2))) for g in range(groups) for m in range(members)])


NEAR = 8


def far_sets():
    groups, members = lax.axis_size("rows"), lax.axis_size("sub")
    return [[g * members + m for g in range(low, groups, NEAR)] for low in range(NEAR) for m in range(members)]


def exchanged(x, sets):
    return lax.all_to_all(x, ("rows", "sub"), 0, 0, axis_index_groups=sets)


def sum_kernel(gram_ref, out_ref):
    packed = gram_ref[0]
    for n in range(1, gram_ref.shape[0]):
        packed = packed + gram_ref[n]
    out_ref[...] = packed


RING = (4, 2, 6)


def row_sums(gram):
    (total,) = call(sum_kernel, [VM], [(gram.shape[1:], f32)], "sum_z", flops=10**6)(exchanged(gram, far_sets()))
    total = total + swapped(total)
    groups = lax.axis_size("rows")
    return [total] + [lax.ppermute(total, "rows", [(i, i ^ mask) for i in range(groups)]) for mask in RING]


def tie(x, *others):
    return lax.optimization_barrier((x, *others))[0]


def on_device(embeddings, start_vectors, pairs):
    members = lax.axis_size("sub")
    groups = lax.axis_size("rows")
    rows, width = embeddings.shape
    k = start_vectors.shape[1]
    quarter = rows // members
    total = rows * groups
    vt = start_vectors.T
    pairs = pairs.T
    cross_v = crossed(vt)
    piece = ((quarter, width), f32)
    first, second, third, sib_v = call(
        functools.partial(cut_kernel, members), [HB, HB, SM],
        [((quarter + NOTE, width), f32), piece, piece, ((k + NOTE, rows), f32)], "cut", flops=10**6,
        scratch=[pltpu.SemaphoreType.DMA((4,))])(
        *(pltpu.with_memory_space_constraint(a, pltpu.HBM) for a in (embeddings, vt)), pairs)
    arrived = [crossed(first)]
    sib_e = swapped(embeddings)
    sib_v = swapped(sib_v)
    arrived.append(crossed(second))
    arrived.append(crossed(third))
    cross_note = arrived[0][quarter:]
    part = ((k, quarter), f32)
    tiles = lambda n: [((n, quarter), bf16)] * 2
    xah, xal, na, acc, *kept = call(
        functools.partial(chip_kernel, members), [VM, VM, VM, VM, SM],
        [((quarter, width), bf16)] * 2 + [((8, quarter), f32), part] + tiles(rows) + tiles(rows), "chip_tiles",
        flops=10**10)(embeddings, vt, sib_e, sib_v, pairs)
    arrived.append(passed_on(arrived[0]))
    far_tiles = {}
    for steps in ((0,), (3,), (1, 2)):
        n = len(steps)
        acc, *t = call(
            functools.partial(cross_kernel, members, steps), [VM] * (n + 2) + [SM, VM, VM, VM, VM], [part] + tiles(quarter) * n,
            "cross_tiles", flops=2 * 10**9)(*(arrived[step] for step in steps), cross_v, cross_note, pairs, xah, xal, na, acc)
        for i, step in enumerate(steps):
            far_tiles[step] = t[2 * i : 2 * i + 2]
    for step in range(members):
        kept += far_tiles[step]
    pieces = [acc] + [shifted(acc, "sub", s) for s in range(1, members)]
    whole = ((k, rows), f32)
    copies = ((groups // NEAR, k // 2, 2 * k), f32)
    image, gram = call(functools.partial(join_kernel, members, total), [VM] * members, [whole, copies], "join")(*pieces)
    cross_i = crossed(image)
    sib_i = swapped(image)
    terms = row_sums(gram)
    (acc2,) = call(functools.partial(second_kernel, members), [VM] * (3 + len(kept)), [part], "second_product")(
        image, sib_i, cross_i, *kept)
    pieces = [acc2] + [shifted(acc2, "sub", s) for s in range(1, members)]
    (inv,) = call(factor_kernel, [VM] * len(terms), [((k, k), f32)], "factor")(*terms)
    image, gram = call(functools.partial(image_kernel, members, total), [VM] * (1 + members), [whole, copies], "image")(inv, *pieces)
    terms = row_sums(gram)
    (out,) = call(last_kernel, [VM] * (1 + len(terms)), [whole], "last")(image, *terms)
    return out.T


def solution(mesh):
    return jax.shard_map(
        on_device,
        mesh=mesh,
        in_specs=(P("rows", None), P("rows", None), P("rows", None)),
        out_specs=P("rows", None),
        check_vma=False,
    )
```

```python
import functools
import jax
import jax.numpy as jnp
from jax import lax
from jax.experimental import pallas as pl
from jax.experimental.pallas import tpu as pltpu
from jax.sharding import PartitionSpec as P

BLK_DEV = 2
OWN, SIB, CROSS = 0, 1, -1
NOTE = 8
MB = 1024 * 1024
LOG2E = 1.4426950408889634
SCALE = LOG2E / 64.0

f32 = jnp.float32
bf16 = jnp.bfloat16
NN = (((1,), (0,)), ((), ()))
NT = (((1,), (1,)), ((), ()))


def dot(a, b, dims):
    return lax.dot_general(a, b, dims, preferred_element_type=f32)


def split2(x):
    hi = x.astype(bf16)
    return hi, (x - hi.astype(f32)).astype(bf16)


def split3(x):
    hi = x.astype(bf16)
    rest = x - hi.astype(f32)
    mid = rest.astype(bf16)
    return hi, mid, (rest - mid.astype(f32)).astype(bf16)


def listed(pairs_ref, row_block, col_block):
    hit = jnp.int32(0)
    for slot in range(pairs_ref.shape[1]):
        same = (pairs_ref[0, slot] == row_block) & (pairs_ref[1, slot] == col_block)
        hit = hit | same.astype(jnp.int32)
    return hit > 0


def place():
    group = lax.axis_index("rows")
    member = lax.axis_index("sub")
    return group, member


def want(pairs_ref, note_ref, group, member, members, side, j):
    mine = group * BLK_DEV + (member * BLK_DEV) // members
    other = (group + side * (1 - 2 * (group & 1))) * BLK_DEV + j
    low, high = jnp.minimum(mine, other), jnp.maximum(mine, other)
    hit = listed(pairs_ref, low, high)
    if note_ref is not None:
        slot = lax.broadcasted_iota(jnp.int32, (1, note_ref.shape[1]), 1) < pairs_ref.shape[1]
        same = slot & (note_ref[0:1, :] == low.astype(f32)) & (note_ref[1:2, :] == high.astype(f32))
        hit = hit | (jnp.max(same.astype(f32)) > 0.5)
    return hit


def quarter_at(members, step, group, member):
    return (member + step * (1 - 2 * (group & 1))) & (members - 1)


def add_product(acc_ref, v, eh, el):
    vh, vm, vl = split3(v)
    k = vh.shape[0]
    one = dot(jnp.concatenate([vh, vm, vl], 0), eh, NN)
    two = dot(jnp.concatenate([vh, vm], 0), el, NN)
    acc_ref[...] += (one[:k] + two[:k]) + (one[k : 2 * k] + two[k:] + one[2 * k :])


def tiles_or_zeros(hit, x_ref, xah_ref, xal_ref, na_ref, vectors, acc_ref, eh_ref, el_ref, start, rows, chunk=256):
    @pl.when(hit)
    def _():
        xah, xal, na = xah_ref[...], xal_ref[...], na_ref[0:1, :]
        for c in range(rows // chunk):
            here = pl.ds(start + c * chunk, chunk)
            x = x_ref[here, :]
            nb = jnp.sum(x * x, axis=1, keepdims=True) * SCALE
            xh, xl = split2(x)
            d = dot(xh, xah, NT) + (dot(xh, xal, NT) + dot(xl, xah, NT))
            e = jnp.exp2(jnp.minimum(d - nb - na, 0.0))
            eh, el = split2(e)
            eh_ref[here, :] = eh
            el_ref[here, :] = el
        here = pl.ds(start, rows)
        add_product(acc_ref, vectors(), eh_ref[here, :], el_ref[here, :])

    @pl.when(jnp.logical_not(hit))
    def _():
        here = pl.ds(start, rows)
        eh_ref[here, :] = jnp.zeros((rows, eh_ref.shape[1]), bf16)
        el_ref[here, :] = jnp.zeros((rows, el_ref.shape[1]), bf16)


def cut_kernel(members, x_ref, v_ref, pairs_ref, *refs):
    group, member = place()
    outs, sib_ref, sems = refs[:-2], refs[-2], refs[-1]
    quarter, width = outs[1].shape
    k = v_ref.shape[0]
    copies = [pltpu.make_async_copy(v_ref, sib_ref.at[pl.ds(0, k)], sems.at[len(outs)])]
    for h in range(2):
        source = v_ref.at[:, pl.ds(pl.multiple_of(member * quarter + h * width, width), width)]
        copies.append(pltpu.make_async_copy(source, outs[0].at[pl.ds(quarter + h * k, k)], sems.at[len(outs) + 1 + h]))
    for step, out_ref in enumerate(outs):
        q = quarter_at(members, -step, group, member)
        source = x_ref.at[pl.ds(pl.multiple_of(q * quarter, quarter), quarter)]
        copies.append(pltpu.make_async_copy(source, out_ref.at[pl.ds(0, quarter)], sems.at[step]))
    for copy in copies:
        copy.start()
    lane = lax.broadcasted_iota(jnp.int32, (NOTE, width), 1)
    row = lax.broadcasted_iota(jnp.int32, (NOTE, width), 0)
    note = jnp.zeros((NOTE, width), f32)
    for slot in range(pairs_ref.shape[1]):
        for c in range(2):
            note = jnp.where((lane == slot) & (row == c), pairs_ref[c, slot].astype(f32), note)
    sib_ref[k:, :width] = note
    sib_ref[k:, width:] = jnp.zeros((NOTE, sib_ref.shape[1] - width), f32)
    outs[0][quarter + 2 * k :, :] = note
    for copy in copies:
        copy.wait()


def chip_kernel(members, x_ref, v_ref, sib_x_ref, sib_v_ref, pairs_ref, xah_ref, xal_ref, na_ref, acc_ref, *kept):
    group, member = place()
    rows = x_ref.shape[0]
    quarter = rows // members
    block = rows // BLK_DEV
    xa = x_ref[pl.ds(pl.multiple_of(member * quarter, quarter), quarter), :]
    ones = jnp.ones((8, xa.shape[1]), f32)
    na_ref[...] = lax.dot_general(ones, xa * xa, NT, precision=lax.Precision.HIGHEST, preferred_element_type=f32) * SCALE
    xah, xal = split2(xa * (2.0 * SCALE))
    xah_ref[...] = xah
    xal_ref[...] = xal
    acc_ref[...] = jnp.zeros_like(acc_ref)
    k = v_ref.shape[0]
    for x, v, note, side, (eh_ref, el_ref) in (
        (x_ref, v_ref, None, OWN, kept[:2]),
        (sib_x_ref, sib_v_ref.at[:k], sib_v_ref.at[k:], SIB, kept[2:]),
    ):
        for j in range(BLK_DEV):
            hit = want(pairs_ref, note, group, member, members, side, j)
            vectors = functools.partial(lambda v, j: v[:, pl.ds(j * block, block)], v, j)
            tiles_or_zeros(hit, x, xah_ref, xal_ref, na_ref, vectors, acc_ref, eh_ref, el_ref, j * block, block)


def cross_kernel(members, steps, *refs):
    n = len(steps)
    pairs_ref, xah_ref, xal_ref, na_ref, in_ref, acc_ref = refs[:6]
    rows = xah_ref.shape[0]
    kept = refs[6 : 6 + 2 * n]
    x_refs, tails = refs[6 + 2 * n : 6 + 3 * n], refs[6 + 3 * n :]
    group, member = place()
    k = acc_ref.shape[0]
    acc_ref[...] = in_ref[...]
    for i, step in enumerate(steps):
        eh_ref, el_ref = kept[2 * i : 2 * i + 2]
        tail = tails[i] if tails else x_refs[i].at[rows:]
        q = quarter_at(members, step, group, member)
        hit = want(pairs_ref, tail.at[2 * k :], group, member, members, CROSS, (q * BLK_DEV) // members)
        vectors = functools.partial(lambda tail: jnp.concatenate([tail[:k, :], tail[k : 2 * k, :]], 1), tail)
        tiles_or_zeros(hit, x_refs[i], xah_ref, xal_ref, na_ref, vectors, acc_ref, eh_ref, el_ref, 0, rows)


def cross_first(members, steps, n_in, *refs):
    far, rest = refs[:n_in], refs[n_in:]
    cross_kernel(members, steps, *rest, *far)


def gram_sum(vh, vm, vl):
    s = jnp.concatenate([vh, vm, vl], 0)
    k = vh.shape[0]
    p = dot(s, s, NT)
    r = p[:k] + (p[k : 2 * k] + p[2 * k :])
    return r[:, :k] + (r[:, k : 2 * k] + r[:, 2 * k :])


def gather_into(full_ref, pieces, members):
    _, member = place()
    quarter = pieces[0].shape[1]
    for k, piece in enumerate(pieces):
        q = lax.rem(member - k + members, members)
        full_ref[:, pl.ds(pl.multiple_of(q * quarter, quarter), quarter)] = piece[...]


def put_gram(gram_ref, image, total):
    gram = gram_sum(*split3(image)) / total
    half = gram.shape[0] // 2
    packed = jnp.concatenate([gram[:half], gram[half:]], 1)
    for n in range(gram_ref.shape[0]):
        gram_ref[n] = packed


def take_gram(terms):
    me, opposite, left, right = (ref[...] for ref in terms)
    packed = (me + opposite) + (left + right)
    k = packed.shape[1] // 2
    return jnp.concatenate([packed[:, :k], packed[:, k:]], 0)


def join_kernel(members, total, *refs):
    pieces, full_ref, gram_ref = refs[:members], refs[members], refs[members + 1]
    gather_into(full_ref, pieces, members)
    put_gram(gram_ref, full_ref[...], total)


def second_kernel(members, vo_ref, vs_ref, vc_ref, *refs):
    group, member = place()
    kept, out_ref = refs[:-1], refs[-1]
    out_ref[...] = jnp.zeros_like(out_ref)
    for v_ref, eh_ref, el_ref in ((vo_ref, kept[0], kept[1]), (vs_ref, kept[2], kept[3])):
        block = v_ref.shape[1] // BLK_DEV
        for j in range(BLK_DEV):
            here = pl.ds(j * block, block)
            add_product(out_ref, v_ref[:, here], eh_ref[here, :], el_ref[here, :])
    for step in range(members):
        eh_ref, el_ref = kept[4 + 2 * step : 6 + 2 * step]
        rows = eh_ref.shape[0]
        q = quarter_at(members, step, group, member)
        add_product(out_ref, vc_ref[:, pl.ds(pl.multiple_of(q * rows, rows), rows)], eh_ref[...], el_ref[...])


def factor_inverse(gram, w=8):
    k = gram.shape[0]
    rows = lax.broadcasted_iota(jnp.int32, (k, k), 0)
    cols = lax.broadcasted_iota(jnp.int32, (k, k), 1)
    aug = jnp.concatenate([gram, (rows == cols).astype(f32)], 1)
    tall, wide = 8, 2 * k
    a = [aug[t * tall : (t + 1) * tall, :] for t in range(k // tall)]
    sub = lax.broadcasted_iota(jnp.int32, (tall, wide), 0)
    spread = lambda x: jnp.broadcast_to(x, (tall, wide))
    for start in range(0, k, w):
        t, s = start // tall, start % tall
        r = [spread(a[t][s + i : s + i + 1, :]) for i in range(w)]
        d = [[spread(a[t][s + i : s + i + 1, start + j : start + j + 1]) if j >= i else None for j in range(w)] for i in range(w)]
        later = range(t if s + w < tall else t + 1, len(a))
        c = {u: [spread(a[u][:, start + i : start + i + 1]) for i in range(w)] for u in later}
        l = [[None] * w for _ in range(w)]
        inv = [None] * w
        for i in range(w):
            p = d[i][i]
            for m in range(i):
                p = p - l[i][m] * l[i][m]
            inv[i] = lax.rsqrt(p)
            for j in range(i + 1, w):
                q = d[i][j]
                for m in range(i):
                    q = q - l[i][m] * l[j][m]
                l[j][i] = q * inv[i]
        for i in range(w):
            for m in range(i):
                r[i] = r[i] - l[i][m] * r[m]
            r[i] = r[i] * inv[i]
        for u in later:
            x = c[u]
            for i in range(w):
                for m in range(i):
                    x[i] = x[i] - l[i][m] * x[m]
                x[i] = x[i] * inv[i]
            new = a[u]
            for i in range(w):
                new = new - x[i] * r[i]
            a[u] = new if u > t else jnp.where(sub < s + w, a[u], new)
        for i in range(w):
            a[t] = jnp.where(sub == s + i, r[i], a[t])
    return jnp.concatenate(a, 0)[:, k:]


def factor_kernel(*refs):
    inv_ref = refs[-1]
    inv_ref[...] = factor_inverse(take_gram(refs[:-1]))


def exact(a, b):
    return lax.dot_general(a, b, NN, precision=lax.Precision.HIGHEST, preferred_element_type=f32)


def image_kernel(members, total, inv_ref, *refs):
    pieces, image_ref, gram_ref = refs[:members], refs[members], refs[members + 1]
    gather_into(image_ref, pieces, members)
    image_ref[...] = exact(inv_ref[...], image_ref[...])
    put_gram(gram_ref, image_ref[...], total)


def last_kernel(image_ref, *refs):
    out_ref = refs[-1]
    out_ref[...] = exact(factor_inverse(take_gram(refs[:-1])), image_ref[...])


VM = pl.BlockSpec(memory_space=pltpu.VMEM)
SM = pl.BlockSpec(memory_space=pltpu.SMEM)
HB = pl.BlockSpec(memory_space=pltpu.HBM)


def call(body, specs, outs, name, limit=16, flops=10**9, scratch=()):
    return pl.pallas_call(
        body,
        in_specs=specs,
        out_specs=[VM] * len(outs),
        scratch_shapes=scratch,
        out_shape=[jax.ShapeDtypeStruct(s, t) for s, t in outs],
        compiler_params=pltpu.CompilerParams(vmem_limit_bytes=limit * MB),
        cost_estimate=pl.CostEstimate(flops=flops, bytes_accessed=MB, transcendentals=0),
        name=name,
    )


def shifted(x, axis, by):
    n = lax.axis_size(axis)
    return lax.ppermute(x, axis, [(i, (i + by) % n) for i in range(n)])


def crossed(x):
    n = lax.axis_size("rows")
    return lax.ppermute(x, "rows", [(i, (i + 2 * (i % 2) - 1) % n) for i in range(n)])


def swapped(x):
    return lax.ppermute(x, "rows", [(i, i ^ 1) for i in range(lax.axis_size("rows"))])


def passed_on(x, by):
    groups, members = lax.axis_size("rows"), lax.axis_size("sub")
    at = lambda g, m: g * members + m % members
    return lax.ppermute(x, ("rows", "sub"), [(at(g, m), at(g, m + by * (1 - 2 * (g % 2)))) for g in range(groups) for m in range(members)])


NEAR = 8


def far_sets():
    groups, members = lax.axis_size("rows"), lax.axis_size("sub")
    return [[g * members + m for g in range(low, groups, NEAR)] for low in range(NEAR) for m in range(members)]


def exchanged(x, sets):
    return lax.all_to_all(x, ("rows", "sub"), 0, 0, axis_index_groups=sets)


def sum_kernel(gram_ref, out_ref):
    packed = gram_ref[0]
    for n in range(1, gram_ref.shape[0]):
        packed = packed + gram_ref[n]
    out_ref[...] = packed


RING = (4, 2, 6)


def row_sums(gram):
    (total,) = call(sum_kernel, [VM], [(gram.shape[1:], f32)], "sum_z", flops=10**6)(exchanged(gram, far_sets()))
    total = total + swapped(total)
    groups = lax.axis_size("rows")
    return [total] + [lax.ppermute(total, "rows", [(i, i ^ mask) for i in range(groups)]) for mask in RING]


def tie(x, *others):
    return lax.optimization_barrier((x, *others))[0]


def on_device(embeddings, start_vectors, pairs):
    members = lax.axis_size("sub")
    groups = lax.axis_size("rows")
    rows, width = embeddings.shape
    k = start_vectors.shape[1]
    quarter = rows // members
    total = rows * groups
    vt = start_vectors.T
    pairs = pairs.T
    piece = ((quarter, width), f32)
    first, second, third, sib_v = call(
        functools.partial(cut_kernel, members), [HB, HB, SM],
        [((quarter + 2 * k + NOTE, width), f32), piece, piece, ((k + NOTE, rows), f32)], "cut", flops=10**6,
        scratch=[pltpu.SemaphoreType.DMA((6,))])(
        *(pltpu.with_memory_space_constraint(a, pltpu.HBM) for a in (embeddings, vt)), pairs)
    arrived = [crossed(first)]
    sib_e = swapped(embeddings)
    sib_v = swapped(sib_v)
    arrived.append(crossed(second))
    arrived.append(crossed(third))
    tail = arrived[0][quarter:]
    part = ((k, quarter), f32)
    tiles = lambda n: [((n, quarter), bf16)] * 2
    xah, xal, na, acc, *kept = call(
        functools.partial(chip_kernel, members), [VM, VM, VM, VM, SM],
        [((quarter, width), bf16)] * 2 + [((8, quarter), f32), part] + tiles(rows) + tiles(rows), "chip_tiles",
        flops=10**10)(embeddings, vt, sib_e, sib_v, pairs)
    arrived.append(passed_on(arrived[0], 1))
    tails = {1: passed_on(tail, -1), 2: passed_on(tail, 2)}
    far_tiles = {}
    for steps in ((0,), (3,), (1, 2)):
        n = len(steps)
        far = [arrived[step] for step in steps] + [tails[step] for step in steps if step in tails]
        acc, *t = call(
            functools.partial(cross_first, members, steps, len(far)), [VM] * len(far) + [SM, VM, VM, VM, VM], [part] + tiles(quarter) * n,
            "cross_tiles", flops=2 * 10**9)(*far, pairs, xah, xal, na, acc)
        for i, step in enumerate(steps):
            far_tiles[step] = t[2 * i : 2 * i + 2]
    for step in range(members):
        kept += far_tiles[step]
    pieces = [acc] + [shifted(acc, "sub", s) for s in range(1, members)]
    whole = ((k, rows), f32)
    copies = ((groups // NEAR, k // 2, 2 * k), f32)
    image, gram = call(functools.partial(join_kernel, members, total), [VM] * members, [whole, copies], "join")(*pieces)
    cross_i = crossed(image)
    sib_i = swapped(image)
    terms = row_sums(gram)
    (acc2,) = call(functools.partial(second_kernel, members), [VM] * (3 + len(kept)), [part], "second_product")(
        image, sib_i, cross_i, *kept)
    pieces = [acc2] + [shifted(acc2, "sub", s) for s in range(1, members)]
    (inv,) = call(factor_kernel, [VM] * len(terms), [((k, k), f32)], "factor")(*terms)
    image, gram = call(functools.partial(image_kernel, members, total), [VM] * (1 + members), [whole, copies], "image")(inv, *pieces)
    terms = row_sums(gram)
    (out,) = call(last_kernel, [VM] * (1 + len(terms)), [whole], "last")(image, *terms)
    return out.T


def solution(mesh):
    return jax.shard_map(
        on_device,
        mesh=mesh,
        in_specs=(P("rows", None), P("rows", None), P("rows", None)),
        out_specs=P("rows", None),
        check_vma=False,
    )
```

```python
import functools
import jax
import jax.numpy as jnp
from jax import lax
from jax.experimental import pallas as pl
from jax.experimental.pallas import tpu as pltpu
from jax.sharding import PartitionSpec as P

BLK_DEV = 2
OWN, SIB, CROSS = 0, 1, -1
NOTE = 8
MB = 1024 * 1024
LOG2E = 1.4426950408889634
SCALE = LOG2E / 64.0

f32 = jnp.float32
bf16 = jnp.bfloat16
NN = (((1,), (0,)), ((), ()))
NT = (((1,), (1,)), ((), ()))


def dot(a, b, dims):
    return lax.dot_general(a, b, dims, preferred_element_type=f32)


def split2(x):
    hi = x.astype(bf16)
    return hi, (x - hi.astype(f32)).astype(bf16)


def split3(x):
    hi = x.astype(bf16)
    rest = x - hi.astype(f32)
    mid = rest.astype(bf16)
    return hi, mid, (rest - mid.astype(f32)).astype(bf16)


def listed(pairs_ref, row_block, col_block):
    hit = jnp.int32(0)
    for slot in range(pairs_ref.shape[1]):
        same = (pairs_ref[0, slot] == row_block) & (pairs_ref[1, slot] == col_block)
        hit = hit | same.astype(jnp.int32)
    return hit > 0


def place():
    group = lax.axis_index("rows")
    member = lax.axis_index("sub")
    return group, member


def want(pairs_ref, note_ref, members, side, j):
    group, member = place()
    mine = group * BLK_DEV + j
    other = (group + side * (1 - 2 * (group & 1))) * BLK_DEV + (member * BLK_DEV) // members
    low, high = jnp.minimum(mine, other), jnp.maximum(mine, other)
    slot = lax.broadcasted_iota(jnp.int32, (1, note_ref.shape[1]), 1) < pairs_ref.shape[1]
    same = slot & (note_ref[0:1, :] == low.astype(f32)) & (note_ref[1:2, :] == high.astype(f32))
    return listed(pairs_ref, low, high) | (jnp.max(same.astype(f32)) > 0.5)


def add_product(acc_ref, v, eh, el):
    vh, vm, vl = split3(v)
    k = vh.shape[0]
    one = dot(jnp.concatenate([vh, vm, vl], 0), eh, NN)
    two = dot(jnp.concatenate([vh, vm], 0), el, NN)
    acc_ref[...] += (one[:k] + two[:k]) + (one[k : 2 * k] + two[k:] + one[2 * k :])


def cut_kernel(x_ref, pairs_ref, out_ref, sem):
    _, member = place()
    quarter, width = out_ref.shape[0] - NOTE, out_ref.shape[1]
    source = x_ref.at[pl.ds(pl.multiple_of(member * quarter, quarter), quarter)]
    copy = pltpu.make_async_copy(source, out_ref.at[pl.ds(0, quarter)], sem)
    copy.start()
    lane = lax.broadcasted_iota(jnp.int32, (NOTE, width), 1)
    row = lax.broadcasted_iota(jnp.int32, (NOTE, width), 0)
    note = jnp.zeros((NOTE, width), f32)
    for slot in range(pairs_ref.shape[1]):
        for c in range(2):
            note = jnp.where((lane == slot) & (row == c), pairs_ref[c, slot].astype(f32), note)
    out_ref[quarter:, :] = note
    copy.wait()


def tiles_kernel(members, side, x_ref, v_ref, message_ref, pairs_ref, acc_ref, eh_ref, el_ref, xah_ref, xal_ref, chunk=256):
    quarter = message_ref.shape[0] - NOTE
    block = x_ref.shape[0] // BLK_DEV
    xa = message_ref[:quarter, :]
    ones = jnp.ones((8, xa.shape[1]), f32)
    na = lax.dot_general(ones, xa * xa, NT, precision=lax.Precision.HIGHEST, preferred_element_type=f32)[0:1, :] * SCALE
    xah_ref[...], xal_ref[...] = split2(xa * (2.0 * SCALE))
    acc_ref[...] = jnp.zeros_like(acc_ref)
    for j in range(BLK_DEV):
        hit = want(pairs_ref, message_ref.at[quarter:], members, side, j)
        all_rows = pl.ds(j * block, block)

        @pl.when(hit)
        def _():
            xah, xal = xah_ref[...], xal_ref[...]
            for c in range(block // chunk):
                here = pl.ds(j * block + c * chunk, chunk)
                x = x_ref[here, :]
                nb = jnp.sum(x * x, axis=1, keepdims=True) * SCALE
                xh, xl = split2(x)
                d = dot(xh, xah, NT) + (dot(xh, xal, NT) + dot(xl, xah, NT))
                e = jnp.exp2(jnp.minimum(d - nb - na, 0.0))
                eh_ref[here, :], el_ref[here, :] = split2(e)
            add_product(acc_ref, v_ref[:, all_rows], eh_ref[all_rows, :], el_ref[all_rows, :])

        @pl.when(jnp.logical_not(hit))
        def _():
            eh_ref[all_rows, :] = jnp.zeros((block, quarter), bf16)
            el_ref[all_rows, :] = jnp.zeros((block, quarter), bf16)


def gram_sum(vh, vm, vl):
    s = jnp.concatenate([vh, vm, vl], 0)
    k = vh.shape[0]
    p = dot(s, s, NT)
    r = p[:k] + (p[k : 2 * k] + p[2 * k :])
    return r[:, :k] + (r[:, k : 2 * k] + r[:, 2 * k :])


def gather_into(full_ref, pieces, members):
    _, member = place()
    quarter = pieces[0].shape[1]
    for k, piece in enumerate(pieces):
        q = lax.rem(member - k + members, members)
        full_ref[:, pl.ds(pl.multiple_of(q * quarter, quarter), quarter)] = piece[...]


def put_gram(gram_ref, image, total):
    gram = gram_sum(*split3(image)) / total
    half = gram.shape[0] // 2
    packed = jnp.concatenate([gram[:half], gram[half:]], 1)
    for n in range(gram_ref.shape[0]):
        gram_ref[n] = packed


def take_gram(terms):
    me, opposite, left, right = (ref[...] for ref in terms)
    packed = (me + opposite) + (left + right)
    k = packed.shape[1] // 2
    return jnp.concatenate([packed[:, :k], packed[:, k:]], 0)


def join_kernel(members, total, *refs):
    pieces, full_ref, gram_ref = refs[:members], refs[members], refs[members + 1]
    gather_into(full_ref, pieces, members)
    put_gram(gram_ref, full_ref[...], total)


def second_kernel(v_ref, *refs):
    n = len(refs) // 3
    kept, outs = refs[: 2 * n], refs[2 * n :]
    block = v_ref.shape[1] // BLK_DEV
    for i, out_ref in enumerate(outs):
        out_ref[...] = jnp.zeros_like(out_ref)
        for j in range(BLK_DEV):
            here = pl.ds(j * block, block)
            add_product(out_ref, v_ref[:, here], kept[2 * i][here, :], kept[2 * i + 1][here, :])


def factor_inverse(gram, w=8):
    k = gram.shape[0]
    rows = lax.broadcasted_iota(jnp.int32, (k, k), 0)
    cols = lax.broadcasted_iota(jnp.int32, (k, k), 1)
    aug = jnp.concatenate([gram, (rows == cols).astype(f32)], 1)
    tall, wide = 8, 2 * k
    a = [aug[t * tall : (t + 1) * tall, :] for t in range(k // tall)]
    sub = lax.broadcasted_iota(jnp.int32, (tall, wide), 0)
    spread = lambda x: jnp.broadcast_to(x, (tall, wide))
    for start in range(0, k, w):
        t, s = start // tall, start % tall
        r = [spread(a[t][s + i : s + i + 1, :]) for i in range(w)]
        d = [[spread(a[t][s + i : s + i + 1, start + j : start + j + 1]) if j >= i else None for j in range(w)] for i in range(w)]
        later = range(t if s + w < tall else t + 1, len(a))
        c = {u: [spread(a[u][:, start + i : start + i + 1]) for i in range(w)] for u in later}
        l = [[None] * w for _ in range(w)]
        inv = [None] * w
        for i in range(w):
            p = d[i][i]
            for m in range(i):
                p = p - l[i][m] * l[i][m]
            inv[i] = lax.rsqrt(p)
            for j in range(i + 1, w):
                q = d[i][j]
                for m in range(i):
                    q = q - l[i][m] * l[j][m]
                l[j][i] = q * inv[i]
        for i in range(w):
            for m in range(i):
                r[i] = r[i] - l[i][m] * r[m]
            r[i] = r[i] * inv[i]
        for u in later:
            x = c[u]
            for i in range(w):
                for m in range(i):
                    x[i] = x[i] - l[i][m] * x[m]
                x[i] = x[i] * inv[i]
            new = a[u]
            for i in range(w):
                new = new - x[i] * r[i]
            a[u] = new if u > t else jnp.where(sub < s + w, a[u], new)
        for i in range(w):
            a[t] = jnp.where(sub == s + i, r[i], a[t])
    return jnp.concatenate(a, 0)[:, k:]


def factor_kernel(*refs):
    inv_ref = refs[-1]
    inv_ref[...] = factor_inverse(take_gram(refs[:-1]))


def exact(a, b):
    return lax.dot_general(a, b, NN, precision=lax.Precision.HIGHEST, preferred_element_type=f32)


def image_kernel(members, total, inv_ref, *refs):
    pieces, image_ref, gram_ref = refs[:members], refs[members], refs[members + 1]
    gather_into(image_ref, pieces, members)
    image_ref[...] = exact(inv_ref[...], image_ref[...])
    put_gram(gram_ref, image_ref[...], total)


def last_kernel(image_ref, *refs):
    out_ref = refs[-1]
    out_ref[...] = exact(factor_inverse(take_gram(refs[:-1])), image_ref[...])


VM = pl.BlockSpec(memory_space=pltpu.VMEM)
SM = pl.BlockSpec(memory_space=pltpu.SMEM)
HB = pl.BlockSpec(memory_space=pltpu.HBM)


def call(body, specs, outs, name, limit=16, flops=10**9, scratch=()):
    return pl.pallas_call(
        body,
        in_specs=specs,
        out_specs=[VM] * len(outs),
        scratch_shapes=scratch,
        out_shape=[jax.ShapeDtypeStruct(s, t) for s, t in outs],
        compiler_params=pltpu.CompilerParams(vmem_limit_bytes=limit * MB),
        cost_estimate=pl.CostEstimate(flops=flops, bytes_accessed=MB, transcendentals=0),
        name=name,
    )


def shifted(x, axis, by):
    n = lax.axis_size(axis)
    return lax.ppermute(x, axis, [(i, (i + by) % n) for i in range(n)])


def crossed(x):
    n = lax.axis_size("rows")
    return lax.ppermute(x, "rows", [(i, (i + 2 * (i % 2) - 1) % n) for i in range(n)])


def swapped(x):
    return lax.ppermute(x, "rows", [(i, i ^ 1) for i in range(lax.axis_size("rows"))])


NEAR = 8


def far_sets():
    groups, members = lax.axis_size("rows"), lax.axis_size("sub")
    return [[g * members + m for g in range(low, groups, NEAR)] for low in range(NEAR) for m in range(members)]


def exchanged(x, sets):
    return lax.all_to_all(x, ("rows", "sub"), 0, 0, axis_index_groups=sets)


def sum_kernel(gram_ref, out_ref):
    packed = gram_ref[0]
    for n in range(1, gram_ref.shape[0]):
        packed = packed + gram_ref[n]
    out_ref[...] = packed


RING = (4, 2, 6)


def row_sums(gram):
    (total,) = call(sum_kernel, [VM], [(gram.shape[1:], f32)], "sum_z", flops=10**6)(exchanged(gram, far_sets()))
    total = total + swapped(total)
    groups = lax.axis_size("rows")
    return [total] + [lax.ppermute(total, "rows", [(i, i ^ mask) for i in range(groups)]) for mask in RING]


def tie(x, *others):
    return lax.optimization_barrier((x, *others))[0]


def on_device(embeddings, start_vectors, pairs):
    members = lax.axis_size("sub")
    groups = lax.axis_size("rows")
    rows, width = embeddings.shape
    k = start_vectors.shape[1]
    quarter = rows // members
    total = rows * groups
    vt = start_vectors.T
    pairs = pairs.T
    part = ((k, quarter), f32)
    kept = [((rows, quarter), bf16)] * 2
    (mine,) = call(
        cut_kernel, [HB, SM], [((quarter + NOTE, width), f32)], "cut", flops=10**6, scratch=[pltpu.SemaphoreType.DMA])(
        pltpu.with_memory_space_constraint(embeddings, pltpu.HBM), pairs)
    cross = crossed(mine)
    sib = swapped(mine)

    def make(side, message, name):
        acc, *t = call(
            functools.partial(tiles_kernel, members, side), [VM, VM, VM, SM], [part] + kept, name, flops=5 * 10**9,
            scratch=[pltpu.VMEM((quarter, width), bf16)] * 2)(embeddings, vt, message, pairs)
        return acc, t

    acc, own_t = make(OWN, mine, "own_tiles")
    sib_acc, sib_t = make(SIB, sib, "sib_tiles")
    cross_acc, cross_t = make(CROSS, tie(cross, sib_acc), "cross_tiles")
    acc = (acc + swapped(sib_acc)) + crossed(cross_acc)
    pieces = [acc] + [shifted(acc, "sub", s) for s in range(1, members)]
    whole = ((k, rows), f32)
    copies = ((groups // NEAR, k // 2, 2 * k), f32)
    image, gram = call(functools.partial(join_kernel, members, total), [VM] * members, [whole, copies], "join")(*pieces)
    sib_acc, cross_acc = call(second_kernel, [VM] * 5, [part] * 2, "second_far")(image, *sib_t, *cross_t)
    (acc2,) = call(second_kernel, [VM] * 3, [part], "second_own")(image, *own_t)
    terms = row_sums(tie(gram, acc2, sib_acc, cross_acc))
    acc2 = (acc2 + swapped(sib_acc)) + crossed(cross_acc)
    pieces = [acc2] + [shifted(acc2, "sub", s) for s in range(1, members)]
    (inv,) = call(factor_kernel, [VM] * len(terms), [((k, k), f32)], "factor")(*terms)
    image, gram = call(functools.partial(image_kernel, members, total), [VM] * (1 + members), [whole, copies], "image")(inv, *pieces)
    terms = row_sums(gram)
    (out,) = call(last_kernel, [VM] * (1 + len(terms)), [whole], "last")(image, *terms)
    return out.T


def solution(mesh):
    return jax.shard_map(
        on_device,
        mesh=mesh,
        in_specs=(P("rows", None), P("rows", None), P("rows", None)),
        out_specs=P("rows", None),
        check_vma=False,
    )
```

```python
import functools
import jax
import jax.numpy as jnp
from jax import lax
from jax.experimental import pallas as pl
from jax.experimental.pallas import tpu as pltpu
from jax.sharding import PartitionSpec as P

BLK_DEV = 2
OWN, SIB, CROSS = 0, 1, -1
NOTE = 8
MB = 1024 * 1024
LOG2E = 1.4426950408889634
SCALE = LOG2E / 64.0

f32 = jnp.float32
bf16 = jnp.bfloat16
NN = (((1,), (0,)), ((), ()))
NT = (((1,), (1,)), ((), ()))


def dot(a, b, dims):
    return lax.dot_general(a, b, dims, preferred_element_type=f32)


def split2(x):
    hi = x.astype(bf16)
    return hi, (x - hi.astype(f32)).astype(bf16)


def split3(x):
    hi = x.astype(bf16)
    rest = x - hi.astype(f32)
    mid = rest.astype(bf16)
    return hi, mid, (rest - mid.astype(f32)).astype(bf16)


def listed(pairs_ref, row_block, col_block):
    hit = jnp.int32(0)
    for slot in range(pairs_ref.shape[1]):
        same = (pairs_ref[0, slot] == row_block) & (pairs_ref[1, slot] == col_block)
        hit = hit | same.astype(jnp.int32)
    return hit > 0


def place():
    group = lax.axis_index("rows")
    member = lax.axis_index("sub")
    return group, member


def want(pairs_ref, note_ref, members, side, j):
    group, member = place()
    mine = group * BLK_DEV + j
    other = (group + side * (1 - 2 * (group & 1))) * BLK_DEV + (member * BLK_DEV) // members
    low, high = jnp.minimum(mine, other), jnp.maximum(mine, other)
    slot = lax.broadcasted_iota(jnp.int32, (1, note_ref.shape[1]), 1) < pairs_ref.shape[1]
    same = slot & (note_ref[0:1, :] == low.astype(f32)) & (note_ref[1:2, :] == high.astype(f32))
    return listed(pairs_ref, low, high) | (jnp.max(same.astype(f32)) > 0.5)


def add_product(acc_ref, v, eh, el):
    vh, vm, vl = split3(v)
    k = vh.shape[0]
    one = dot(jnp.concatenate([vh, vm, vl], 0), eh, NN)
    two = dot(jnp.concatenate([vh, vm], 0), el, NN)
    acc_ref[...] += (one[:k] + two[:k]) + (one[k : 2 * k] + two[k:] + one[2 * k :])


def cut_kernel(x_ref, pairs_ref, out_ref, sem):
    _, member = place()
    quarter, width = out_ref.shape[0] - NOTE, out_ref.shape[1]
    source = x_ref.at[pl.ds(pl.multiple_of(member * quarter, quarter), quarter)]
    copy = pltpu.make_async_copy(source, out_ref.at[pl.ds(0, quarter)], sem)
    copy.start()
    lane = lax.broadcasted_iota(jnp.int32, (NOTE, width), 1)
    row = lax.broadcasted_iota(jnp.int32, (NOTE, width), 0)
    note = jnp.zeros((NOTE, width), f32)
    for slot in range(pairs_ref.shape[1]):
        for c in range(2):
            note = jnp.where((lane == slot) & (row == c), pairs_ref[c, slot].astype(f32), note)
    out_ref[quarter:, :] = note
    copy.wait()


def tiles_kernel(members, side, x_ref, v_ref, message_ref, pairs_ref, acc_ref, eh_ref, el_ref, xah_ref, xal_ref, chunk=256):
    quarter = message_ref.shape[0] - NOTE
    block = x_ref.shape[0] // BLK_DEV
    xa = message_ref[:quarter, :]
    ones = jnp.ones((8, xa.shape[1]), f32)
    na = lax.dot_general(ones, xa * xa, NT, precision=lax.Precision.HIGHEST, preferred_element_type=f32)[0:1, :] * SCALE
    xah_ref[...], xal_ref[...] = split2(xa * (2.0 * SCALE))
    acc_ref[...] = jnp.zeros_like(acc_ref)
    for j in range(BLK_DEV):
        hit = want(pairs_ref, message_ref.at[quarter:], members, side, j)
        all_rows = pl.ds(j * block, block)

        @pl.when(hit)
        def _():
            xah, xal = xah_ref[...], xal_ref[...]
            for c in range(block // chunk):
                here = pl.ds(j * block + c * chunk, chunk)
                x = x_ref[here, :]
                nb = jnp.sum(x * x, axis=1, keepdims=True) * SCALE
                xh, xl = split2(x)
                d = dot(xh, xah, NT) + (dot(xh, xal, NT) + dot(xl, xah, NT))
                e = jnp.exp2(jnp.minimum(d - nb - na, 0.0))
                eh_ref[here, :], el_ref[here, :] = split2(e)
            add_product(acc_ref, v_ref[:, all_rows], eh_ref[all_rows, :], el_ref[all_rows, :])

        @pl.when(jnp.logical_not(hit))
        def _():
            eh_ref[all_rows, :] = jnp.zeros((block, quarter), bf16)
            el_ref[all_rows, :] = jnp.zeros((block, quarter), bf16)


def gram_sum(vh, vm, vl):
    s = jnp.concatenate([vh, vm, vl], 0)
    k = vh.shape[0]
    p = dot(s, s, NT)
    r = p[:k] + (p[k : 2 * k] + p[2 * k :])
    return r[:, :k] + (r[:, k : 2 * k] + r[:, 2 * k :])


def gather_into(full_ref, pieces, members):
    _, member = place()
    quarter = pieces[0].shape[1]
    for k, piece in enumerate(pieces):
        q = lax.rem(member - k + members, members)
        full_ref[:, pl.ds(pl.multiple_of(q * quarter, quarter), quarter)] = piece[...]


def put_gram(gram_ref, image, total):
    gram = gram_sum(*split3(image)) / total
    half = gram.shape[0] // 2
    packed = jnp.concatenate([gram[:half], gram[half:]], 1)
    if len(gram_ref.shape) == 2:
        gram_ref[...] = packed
        return
    for n in range(gram_ref.shape[0]):
        gram_ref[n] = packed


def take_gram(terms):
    packed = terms[0][...] + terms[1][...]
    if len(terms) > 2:
        packed = packed + (terms[2][...] + terms[3][...])
    k = packed.shape[1] // 2
    return jnp.concatenate([packed[:, :k], packed[:, k:]], 0)


def join_kernel(members, total, *refs):
    pieces, full_ref, gram_ref = refs[:members], refs[members], refs[members + 1]
    gather_into(full_ref, pieces, members)
    put_gram(gram_ref, full_ref[...], total)


def second_kernel(v_ref, *refs):
    n = len(refs) // 3
    kept, outs = refs[: 2 * n], refs[2 * n :]
    block = v_ref.shape[1] // BLK_DEV
    for i, out_ref in enumerate(outs):
        out_ref[...] = jnp.zeros_like(out_ref)
        for j in range(BLK_DEV):
            here = pl.ds(j * block, block)
            add_product(out_ref, v_ref[:, here], kept[2 * i][here, :], kept[2 * i + 1][here, :])


def factor_inverse(gram, w=8):
    k = gram.shape[0]
    rows = lax.broadcasted_iota(jnp.int32, (k, k), 0)
    cols = lax.broadcasted_iota(jnp.int32, (k, k), 1)
    aug = jnp.concatenate([gram, (rows == cols).astype(f32)], 1)
    tall, wide = 8, 2 * k
    a = [aug[t * tall : (t + 1) * tall, :] for t in range(k // tall)]
    sub = lax.broadcasted_iota(jnp.int32, (tall, wide), 0)
    spread = lambda x: jnp.broadcast_to(x, (tall, wide))
    for start in range(0, k, w):
        t, s = start // tall, start % tall
        r = [spread(a[t][s + i : s + i + 1, :]) for i in range(w)]
        d = [[spread(a[t][s + i : s + i + 1, start + j : start + j + 1]) if j >= i else None for j in range(w)] for i in range(w)]
        later = range(t if s + w < tall else t + 1, len(a))
        c = {u: [spread(a[u][:, start + i : start + i + 1]) for i in range(w)] for u in later}
        l = [[None] * w for _ in range(w)]
        inv = [None] * w
        for i in range(w):
            p = d[i][i]
            for m in range(i):
                p = p - l[i][m] * l[i][m]
            inv[i] = lax.rsqrt(p)
            for j in range(i + 1, w):
                q = d[i][j]
                for m in range(i):
                    q = q - l[i][m] * l[j][m]
                l[j][i] = q * inv[i]
        for i in range(w):
            for m in range(i):
                r[i] = r[i] - l[i][m] * r[m]
            r[i] = r[i] * inv[i]
        for u in later:
            x = c[u]
            for i in range(w):
                for m in range(i):
                    x[i] = x[i] - l[i][m] * x[m]
                x[i] = x[i] * inv[i]
            new = a[u]
            for i in range(w):
                new = new - x[i] * r[i]
            a[u] = new if u > t else jnp.where(sub < s + w, a[u], new)
        for i in range(w):
            a[t] = jnp.where(sub == s + i, r[i], a[t])
    return jnp.concatenate(a, 0)[:, k:]


def factor_kernel(*refs):
    inv_ref = refs[-1]
    inv_ref[...] = factor_inverse(take_gram(refs[:-1]))


def exact(a, b):
    return lax.dot_general(a, b, NN, precision=lax.Precision.HIGHEST, preferred_element_type=f32)


def image_kernel(members, total, inv_ref, *refs):
    pieces, image_ref, gram_ref = refs[:members], refs[members], refs[members + 1]
    gather_into(image_ref, pieces, members)
    image_ref[...] = exact(inv_ref[...], image_ref[...])
    put_gram(gram_ref, image_ref[...], total)


def last_kernel(image_ref, *refs):
    out_ref = refs[-1]
    out_ref[...] = exact(factor_inverse(take_gram(refs[:-1])), image_ref[...])


VM = pl.BlockSpec(memory_space=pltpu.VMEM)
SM = pl.BlockSpec(memory_space=pltpu.SMEM)
HB = pl.BlockSpec(memory_space=pltpu.HBM)


def call(body, specs, outs, name, limit=16, flops=10**9, scratch=()):
    return pl.pallas_call(
        body,
        in_specs=specs,
        out_specs=[VM] * len(outs),
        scratch_shapes=scratch,
        out_shape=[jax.ShapeDtypeStruct(s, t) for s, t in outs],
        compiler_params=pltpu.CompilerParams(vmem_limit_bytes=limit * MB),
        cost_estimate=pl.CostEstimate(flops=flops, bytes_accessed=MB, transcendentals=0),
        name=name,
    )


def shifted(x, axis, by):
    n = lax.axis_size(axis)
    return lax.ppermute(x, axis, [(i, (i + by) % n) for i in range(n)])


def crossed(x):
    n = lax.axis_size("rows")
    return lax.ppermute(x, "rows", [(i, (i + 2 * (i % 2) - 1) % n) for i in range(n)])


def swapped(x):
    return lax.ppermute(x, "rows", [(i, i ^ 1) for i in range(lax.axis_size("rows"))])


NEAR = 8


def far_sets():
    groups, members = lax.axis_size("rows"), lax.axis_size("sub")
    return [[g * members + m for g in range(low, groups, NEAR)] for low in range(NEAR) for m in range(members)]


def exchanged(x, sets):
    return lax.all_to_all(x, ("rows", "sub"), 0, 0, axis_index_groups=sets)


def sum_kernel(gram_ref, out_ref):
    packed = gram_ref[0]
    for n in range(1, gram_ref.shape[0]):
        packed = packed + gram_ref[n]
    out_ref[...] = packed


MASKS = (1, 2, 6, 8, 16, 48)


def pair_sums(total):
    groups = lax.axis_size("rows")
    for mask in MASKS:
        other = lax.ppermute(total, "rows", [(i, i ^ mask) for i in range(groups)])
        if mask == MASKS[-1]:
            return [total, other]
        total = total + other


RING = (4, 2, 6)


def row_sums(gram):
    (total,) = call(sum_kernel, [VM], [(gram.shape[1:], f32)], "sum_z", flops=10**6)(exchanged(gram, far_sets()))
    total = total + swapped(total)
    groups = lax.axis_size("rows")
    return [total] + [lax.ppermute(total, "rows", [(i, i ^ mask) for i in range(groups)]) for mask in RING]


def tie(x, *others):
    return lax.optimization_barrier((x, *others))[0]


def on_device(embeddings, start_vectors, pairs):
    members = lax.axis_size("sub")
    groups = lax.axis_size("rows")
    rows, width = embeddings.shape
    k = start_vectors.shape[1]
    quarter = rows // members
    total = rows * groups
    vt = start_vectors.T
    pairs = pairs.T
    part = ((k, quarter), f32)
    kept = [((rows, quarter), bf16)] * 2
    (mine,) = call(
        cut_kernel, [HB, SM], [((quarter + NOTE, width), f32)], "cut", flops=10**6, scratch=[pltpu.SemaphoreType.DMA])(
        pltpu.with_memory_space_constraint(embeddings, pltpu.HBM), pairs)
    cross = crossed(mine)
    sib = swapped(mine)

    def make(side, message, name):
        acc, *t = call(
            functools.partial(tiles_kernel, members, side), [VM, VM, VM, SM], [part] + kept, name, flops=5 * 10**9,
            scratch=[pltpu.VMEM((quarter, width), bf16)] * 2)(embeddings, vt, message, pairs)
        return acc, t

    acc, own_t = make(OWN, mine, "own_tiles")
    sib_acc, sib_t = make(SIB, sib, "sib_tiles")
    cross_acc, cross_t = make(CROSS, tie(cross, sib_acc), "cross_tiles")
    acc = (acc + swapped(sib_acc)) + crossed(cross_acc)
    pieces = [acc] + [shifted(acc, "sub", s) for s in range(1, members)]
    whole = ((k, rows), f32)
    copies = ((groups // NEAR, k // 2, 2 * k), f32)
    image, gram = call(functools.partial(join_kernel, members, total), [VM] * members, [whole, (copies[0][1:], f32)], "join")(*pieces)
    sib_acc, cross_acc = call(second_kernel, [VM] * 5, [part] * 2, "second_far")(image, *sib_t, *cross_t)
    (acc2,) = call(second_kernel, [VM] * 3, [part], "second_own")(image, *own_t)
    terms = pair_sums(gram)
    acc2 = (acc2 + swapped(sib_acc)) + crossed(cross_acc)
    pieces = [acc2] + [shifted(acc2, "sub", s) for s in range(1, members)]
    (inv,) = call(factor_kernel, [VM] * len(terms), [((k, k), f32)], "factor")(*terms)
    image, gram = call(functools.partial(image_kernel, members, total), [VM] * (1 + members), [whole, copies], "image")(inv, *pieces)
    terms = row_sums(gram)
    (out,) = call(last_kernel, [VM] * (1 + len(terms)), [whole], "last")(image, *terms)
    return out.T


def solution(mesh):
    return jax.shard_map(
        on_device,
        mesh=mesh,
        in_specs=(P("rows", None), P("rows", None), P("rows", None)),
        out_specs=P("rows", None),
        check_vma=False,
    )
```

```python
import functools
import jax
import jax.numpy as jnp
from jax import lax
from jax.experimental import pallas as pl
from jax.experimental.pallas import tpu as pltpu
from jax.sharding import PartitionSpec as P

BLK_DEV = 2
OWN, SIB, CROSS = 0, 1, -1
NOTE = 8
MB = 1024 * 1024
LOG2E = 1.4426950408889634
SCALE = LOG2E / 64.0

f32 = jnp.float32
bf16 = jnp.bfloat16
NN = (((1,), (0,)), ((), ()))
NT = (((1,), (1,)), ((), ()))


def dot(a, b, dims):
    return lax.dot_general(a, b, dims, preferred_element_type=f32)


def split2(x):
    hi = x.astype(bf16)
    return hi, (x - hi.astype(f32)).astype(bf16)


def split3(x):
    hi = x.astype(bf16)
    rest = x - hi.astype(f32)
    mid = rest.astype(bf16)
    return hi, mid, (rest - mid.astype(f32)).astype(bf16)


def listed(pairs_ref, row_block, col_block):
    hit = jnp.int32(0)
    for slot in range(pairs_ref.shape[1]):
        same = (pairs_ref[0, slot] == row_block) & (pairs_ref[1, slot] == col_block)
        hit = hit | same.astype(jnp.int32)
    return hit > 0


def place():
    group = lax.axis_index("rows")
    member = lax.axis_index("sub")
    return group, member


def want(pairs_ref, note_ref, members, side, j):
    group, member = place()
    mine = group * BLK_DEV + j
    other = (group + side * (1 - 2 * (group & 1))) * BLK_DEV + (member * BLK_DEV) // members
    low, high = jnp.minimum(mine, other), jnp.maximum(mine, other)
    slot = lax.broadcasted_iota(jnp.int32, (1, note_ref.shape[1]), 1) < pairs_ref.shape[1]
    same = slot & (note_ref[0:1, :] == low.astype(f32)) & (note_ref[1:2, :] == high.astype(f32))
    return listed(pairs_ref, low, high) | (jnp.max(same.astype(f32)) > 0.5)


def add_product(acc_ref, v, eh, el):
    vh, vm, vl = split3(v)
    k = vh.shape[0]
    one = dot(jnp.concatenate([vh, vm, vl], 0), eh, NN)
    two = dot(jnp.concatenate([vh, vm], 0), el, NN)
    acc_ref[...] += (one[:k] + two[:k]) + (one[k : 2 * k] + two[k:] + one[2 * k :])


def cut_kernel(x_ref, pairs_ref, out_ref, list_ref, sems):
    _, member = place()
    quarter = out_ref.shape[0] - NOTE
    source = x_ref.at[pl.ds(pl.multiple_of(member * quarter, quarter), quarter)]
    copies = [
        pltpu.make_async_copy(source, out_ref.at[pl.ds(0, quarter)], sems.at[0]),
        pltpu.make_async_copy(pairs_ref, list_ref, sems.at[1]),
    ]
    for copy in copies:
        copy.start()
    copies[1].wait()
    count, slots = list_ref.shape
    out_ref[quarter:, :] = jnp.zeros((NOTE, out_ref.shape[1]), f32)
    out_ref[quarter : quarter + count, :slots] = list_ref[...].astype(f32)
    copies[0].wait()


def tiles_kernel(members, side, x_ref, v_ref, message_ref, pairs_ref, acc_ref, eh_ref, el_ref, xah_ref, xal_ref, chunk=256):
    quarter = message_ref.shape[0] - NOTE
    block = x_ref.shape[0] // BLK_DEV
    xa = message_ref[:quarter, :]
    ones = jnp.ones((8, xa.shape[1]), f32)
    na = lax.dot_general(ones, xa * xa, NT, precision=lax.Precision.HIGHEST, preferred_element_type=f32)[0:1, :] * SCALE
    xah_ref[...], xal_ref[...] = split2(xa * (2.0 * SCALE))
    acc_ref[...] = jnp.zeros_like(acc_ref)
    for j in range(BLK_DEV):
        hit = want(pairs_ref, message_ref.at[quarter:], members, side, j)
        all_rows = pl.ds(j * block, block)

        @pl.when(hit)
        def _():
            xah, xal = xah_ref[...], xal_ref[...]
            for c in range(block // chunk):
                here = pl.ds(j * block + c * chunk, chunk)
                x = x_ref[here, :]
                nb = jnp.sum(x * x, axis=1, keepdims=True) * SCALE
                xh, xl = split2(x)
                d = dot(xh, xah, NT) + (dot(xh, xal, NT) + dot(xl, xah, NT))
                e = jnp.exp2(jnp.minimum(d - nb - na, 0.0))
                eh_ref[here, :], el_ref[here, :] = split2(e)
            add_product(acc_ref, v_ref[:, all_rows], eh_ref[all_rows, :], el_ref[all_rows, :])

        @pl.when(jnp.logical_not(hit))
        def _():
            eh_ref[all_rows, :] = jnp.zeros((block, quarter), bf16)
            el_ref[all_rows, :] = jnp.zeros((block, quarter), bf16)


def gram_sum(vh, vm, vl):
    s = jnp.concatenate([vh, vm, vl], 0)
    k = vh.shape[0]
    p = dot(s, s, NT)
    r = p[:k] + (p[k : 2 * k] + p[2 * k :])
    return r[:, :k] + (r[:, k : 2 * k] + r[:, 2 * k :])


def gather_into(full_ref, pieces, members):
    _, member = place()
    quarter = full_ref.shape[1] // members
    for piece, other in zip(pieces, (0, 3)):
        for near in range(2):
            q = member ^ (other ^ near)
            full_ref[:, pl.ds(pl.multiple_of(q * quarter, quarter), quarter)] = piece[:, near * quarter : (near + 1) * quarter]


def put_gram(gram_ref, image, total):
    gram = gram_sum(*split3(image)) / total
    half = gram.shape[0] // 2
    packed = jnp.concatenate([gram[:half], gram[half:]], 1)
    if len(gram_ref.shape) == 2:
        gram_ref[...] = packed
        return
    for n in range(gram_ref.shape[0]):
        gram_ref[n] = packed


def take_gram(terms):
    packed = terms[0][...] + terms[1][...]
    if len(terms) > 2:
        packed = packed + (terms[2][...] + terms[3][...])
    k = packed.shape[1] // 2
    return jnp.concatenate([packed[:, :k], packed[:, k:]], 0)


def join_kernel(members, total, *refs):
    pieces, full_ref, gram_ref = refs[:2], refs[2], refs[3]
    gather_into(full_ref, pieces, members)
    put_gram(gram_ref, full_ref[...], total)


def second_kernel(v_ref, *refs):
    n = len(refs) // 3
    kept, outs = refs[: 2 * n], refs[2 * n :]
    block = v_ref.shape[1] // BLK_DEV
    for i, out_ref in enumerate(outs):
        out_ref[...] = jnp.zeros_like(out_ref)
        for j in range(BLK_DEV):
            here = pl.ds(j * block, block)
            add_product(out_ref, v_ref[:, here], kept[2 * i][here, :], kept[2 * i + 1][here, :])


def factor_inverse(gram, w=8):
    k = gram.shape[0]
    rows = lax.broadcasted_iota(jnp.int32, (k, k), 0)
    cols = lax.broadcasted_iota(jnp.int32, (k, k), 1)
    aug = jnp.concatenate([gram, (rows == cols).astype(f32)], 1)
    tall, wide = 8, 2 * k
    a = [aug[t * tall : (t + 1) * tall, :] for t in range(k // tall)]
    sub = lax.broadcasted_iota(jnp.int32, (tall, wide), 0)
    spread = lambda x: jnp.broadcast_to(x, (tall, wide))
    for start in range(0, k, w):
        t, s = start // tall, start % tall
        r = [spread(a[t][s + i : s + i + 1, :]) for i in range(w)]
        d = [[spread(a[t][s + i : s + i + 1, start + j : start + j + 1]) if j >= i else None for j in range(w)] for i in range(w)]
        later = range(t if s + w < tall else t + 1, len(a))
        c = {u: [spread(a[u][:, start + i : start + i + 1]) for i in range(w)] for u in later}
        l = [[None] * w for _ in range(w)]
        inv = [None] * w
        for i in range(w):
            p = d[i][i]
            for m in range(i):
                p = p - l[i][m] * l[i][m]
            inv[i] = lax.rsqrt(p)
            for j in range(i + 1, w):
                q = d[i][j]
                for m in range(i):
                    q = q - l[i][m] * l[j][m]
                l[j][i] = q * inv[i]
        for i in range(w):
            for m in range(i):
                r[i] = r[i] - l[i][m] * r[m]
            r[i] = r[i] * inv[i]
        for u in later:
            x = c[u]
            for i in range(w):
                for m in range(i):
                    x[i] = x[i] - l[i][m] * x[m]
                x[i] = x[i] * inv[i]
            new = a[u]
            for i in range(w):
                new = new - x[i] * r[i]
            a[u] = new if u > t else jnp.where(sub < s + w, a[u], new)
        for i in range(w):
            a[t] = jnp.where(sub == s + i, r[i], a[t])
    return jnp.concatenate(a, 0)[:, k:]


def factor_kernel(*refs):
    inv_ref = refs[-1]
    inv_ref[...] = factor_inverse(take_gram(refs[:-1]))


def exact(a, b):
    return lax.dot_general(a, b, NN, precision=lax.Precision.HIGHEST, preferred_element_type=f32)


def image_kernel(members, total, inv_ref, *refs):
    pieces, image_ref, gram_ref = refs[:2], refs[2], refs[3]
    gather_into(image_ref, pieces, members)
    image_ref[...] = exact(inv_ref[...], image_ref[...])
    put_gram(gram_ref, image_ref[...], total)


def last_kernel(image_ref, *refs):
    out_ref = refs[-1]
    out_ref[...] = exact(factor_inverse(take_gram(refs[:-1])), image_ref[...])


VM = pl.BlockSpec(memory_space=pltpu.VMEM)
SM = pl.BlockSpec(memory_space=pltpu.SMEM)
HB = pl.BlockSpec(memory_space=pltpu.HBM)


def call(body, specs, outs, name, limit=16, flops=10**9, scratch=()):
    return pl.pallas_call(
        body,
        in_specs=specs,
        out_specs=[VM] * len(outs),
        scratch_shapes=scratch,
        out_shape=[jax.ShapeDtypeStruct(s, t) for s, t in outs],
        compiler_params=pltpu.CompilerParams(vmem_limit_bytes=limit * MB),
        cost_estimate=pl.CostEstimate(flops=flops, bytes_accessed=MB, transcendentals=0),
        name=name,
    )


def gathered(x, *after):
    swap = lambda y, mask: lax.ppermute(y, "sub", [(i, i ^ mask) for i in range(lax.axis_size("sub"))])
    near = swap(x, 1)
    if after:
        near = tie(near, *after)
    both = jnp.concatenate([x, near], 1)
    return both, swap(both, 3)


def crossed(x):
    n = lax.axis_size("rows")
    return lax.ppermute(x, "rows", [(i, (i + 2 * (i % 2) - 1) % n) for i in range(n)])


def swapped(x):
    return lax.ppermute(x, "rows", [(i, i ^ 1) for i in range(lax.axis_size("rows"))])


NEAR = 8


def far_sets():
    groups, members = lax.axis_size("rows"), lax.axis_size("sub")
    return [[g * members + m for g in range(low, groups, NEAR)] for low in range(NEAR) for m in range(members)]


def exchanged(x, sets):
    return lax.all_to_all(x, ("rows", "sub"), 0, 0, axis_index_groups=sets)


def sum_kernel(gram_ref, out_ref):
    packed = gram_ref[0]
    for n in range(1, gram_ref.shape[0]):
        packed = packed + gram_ref[n]
    out_ref[...] = packed


MASKS = (1, 2, 6, 8, 16, 48)


def pair_sums(total):
    groups = lax.axis_size("rows")
    sums = [total]
    for mask in MASKS:
        other = lax.ppermute(sums[-1], "rows", [(i, i ^ mask) for i in range(groups)])
        sums.append(other if mask == MASKS[-1] else sums[-1] + other)
    return sums


RING = (4, 2, 6)


def row_sums(gram):
    (total,) = call(sum_kernel, [VM], [(gram.shape[1:], f32)], "sum_z", flops=10**6)(exchanged(gram, far_sets()))
    total = total + swapped(total)
    groups = lax.axis_size("rows")
    return [total] + [lax.ppermute(total, "rows", [(i, i ^ mask) for i in range(groups)]) for mask in RING]


def tie(x, *others):
    return lax.optimization_barrier((x, *others))[0]


def on_device(embeddings, start_vectors, pairs):
    members = lax.axis_size("sub")
    groups = lax.axis_size("rows")
    rows, width = embeddings.shape
    k = start_vectors.shape[1]
    quarter = rows // members
    total = rows * groups
    vt = start_vectors.T
    pairs = pairs.T
    part = ((k, quarter), f32)
    kept = [((rows, quarter), bf16)] * 2
    (mine,) = call(
        cut_kernel, [HB, HB], [((quarter + NOTE, width), f32)], "cut", flops=10**6,
        scratch=[pltpu.VMEM(pairs.shape, jnp.int32), pltpu.SemaphoreType.DMA((2,))])(
        *(pltpu.with_memory_space_constraint(a, pltpu.HBM) for a in (embeddings, pairs)))
    cross = crossed(mine)
    sib = swapped(mine)

    def make(side, message, name):
        acc, *t = call(
            functools.partial(tiles_kernel, members, side), [VM, VM, VM, SM], [part] + kept, name, flops=5 * 10**9,
            scratch=[pltpu.VMEM((quarter, width), bf16)] * 2)(embeddings, vt, message, pairs)
        return acc, t

    acc, own_t = make(OWN, mine, "own_tiles")
    sib_acc, sib_t = make(SIB, sib, "sib_tiles")
    cross_acc, cross_t = make(CROSS, tie(cross, sib_acc), "cross_tiles")
    acc = (acc + swapped(sib_acc)) + crossed(cross_acc)
    pieces = gathered(acc)
    whole = ((k, rows), f32)
    copies = ((groups // NEAR, k // 2, 2 * k), f32)
    image, gram = call(functools.partial(join_kernel, members, total), [VM] * 2, [whole, (copies[0][1:], f32)], "join")(*pieces)
    sums = pair_sums(gram)
    terms = sums[-2:]
    sib_acc, cross_acc = call(second_kernel, [VM] * 5, [part] * 2, "second_far")(tie(image, sums[1]), *sib_t, *cross_t)
    (acc2,) = call(second_kernel, [VM] * 3, [part], "second_own")(tie(image, sums[2]), *own_t)
    acc2 = (acc2 + swapped(sib_acc)) + crossed(cross_acc)
    pieces = gathered(tie(acc2, sums[3]), sums[4])
    (inv,) = call(factor_kernel, [VM] * len(terms), [((k, k), f32)], "factor")(*terms)
    image, gram = call(functools.partial(image_kernel, members, total), [VM] * 3, [whole, copies], "image")(inv, *pieces)
    terms = row_sums(gram)
    (out,) = call(last_kernel, [VM] * (1 + len(terms)), [whole], "last")(image, *terms)
    return out.T


def solution(mesh):
    return jax.shard_map(
        on_device,
        mesh=mesh,
        in_specs=(P("rows", None), P("rows", None), P("rows", None)),
        out_specs=P("rows", None),
        check_vma=False,
    )
```

```python
import functools
import jax
import jax.numpy as jnp
from jax import lax
from jax.experimental import pallas as pl
from jax.experimental.pallas import tpu as pltpu
from jax.sharding import PartitionSpec as P

BLK_DEV = 2
OWN, SIB, CROSS = 0, 1, -1
NOTE = 8
MB = 1024 * 1024
LOG2E = 1.4426950408889634
SCALE = LOG2E / 64.0

f32 = jnp.float32
bf16 = jnp.bfloat16
NN = (((1,), (0,)), ((), ()))
NT = (((1,), (1,)), ((), ()))


def dot(a, b, dims):
    return lax.dot_general(a, b, dims, preferred_element_type=f32)


def split2(x):
    hi = x.astype(bf16)
    return hi, (x - hi.astype(f32)).astype(bf16)


def split3(x):
    hi = x.astype(bf16)
    rest = x - hi.astype(f32)
    mid = rest.astype(bf16)
    return hi, mid, (rest - mid.astype(f32)).astype(bf16)


def listed(pairs_ref, row_block, col_block):
    hit = jnp.int32(0)
    for slot in range(pairs_ref.shape[1]):
        same = (pairs_ref[0, slot] == row_block) & (pairs_ref[1, slot] == col_block)
        hit = hit | same.astype(jnp.int32)
    return hit > 0


def place():
    group = lax.axis_index("rows")
    member = lax.axis_index("sub")
    return group, member


def want(pairs_ref, note_ref, members, side, j):
    group, member = place()
    mine = group * BLK_DEV + j
    other = (group + side * (1 - 2 * (group & 1))) * BLK_DEV + (member * BLK_DEV) // members
    low, high = jnp.minimum(mine, other), jnp.maximum(mine, other)
    slot = lax.broadcasted_iota(jnp.int32, (1, note_ref.shape[1]), 1) < pairs_ref.shape[1]
    same = slot & (note_ref[0:1, :] == low.astype(f32)) & (note_ref[1:2, :] == high.astype(f32))
    return listed(pairs_ref, low, high) | (jnp.max(same.astype(f32)) > 0.5)


def add_product(acc_ref, v, eh, el):
    vh, vm, vl = split3(v)
    k = vh.shape[0]
    one = dot(jnp.concatenate([vh, vm, vl], 0), eh, NN)
    two = dot(jnp.concatenate([vh, vm], 0), el, NN)
    acc_ref[...] += (one[:k] + two[:k]) + (one[k : 2 * k] + two[k:] + one[2 * k :])


def cut_kernel(x_ref, pairs_ref, out_ref, list_ref, sems):
    _, member = place()
    quarter = out_ref.shape[0] - NOTE
    source = x_ref.at[pl.ds(pl.multiple_of(member * quarter, quarter), quarter)]
    copies = [
        pltpu.make_async_copy(source, out_ref.at[pl.ds(0, quarter)], sems.at[0]),
        pltpu.make_async_copy(pairs_ref, list_ref, sems.at[1]),
    ]
    for copy in copies:
        copy.start()
    copies[1].wait()
    count, slots = list_ref.shape
    out_ref[quarter:, :] = jnp.zeros((NOTE, out_ref.shape[1]), f32)
    out_ref[quarter : quarter + count, :slots] = list_ref[...].astype(f32)
    copies[0].wait()


def tiles_kernel(members, side, x_ref, v_ref, message_ref, pairs_ref, acc_ref, eh_ref, el_ref, xah_ref, xal_ref, chunk=256):
    quarter = message_ref.shape[0] - NOTE
    block = x_ref.shape[0] // BLK_DEV
    xa = message_ref[:quarter, :]
    ones = jnp.ones((8, xa.shape[1]), f32)
    na = lax.dot_general(ones, xa * xa, NT, precision=lax.Precision.HIGHEST, preferred_element_type=f32)[0:1, :] * SCALE
    xah_ref[...], xal_ref[...] = split2(xa * (2.0 * SCALE))
    acc_ref[...] = jnp.zeros_like(acc_ref)
    for j in range(BLK_DEV):
        hit = want(pairs_ref, message_ref.at[quarter:], members, side, j)
        all_rows = pl.ds(j * block, block)

        @pl.when(hit)
        def _():
            xah, xal = xah_ref[...], xal_ref[...]
            for c in range(block // chunk):
                here = pl.ds(j * block + c * chunk, chunk)
                x = x_ref[here, :]
                nb = jnp.sum(x * x, axis=1, keepdims=True) * SCALE
                xh, xl = split2(x)
                d = dot(xh, xah, NT) + (dot(xh, xal, NT) + dot(xl, xah, NT))
                e = jnp.exp2(jnp.minimum(d - nb - na, 0.0))
                eh_ref[here, :], el_ref[here, :] = split2(e)
            add_product(acc_ref, v_ref[:, all_rows], eh_ref[all_rows, :], el_ref[all_rows, :])

        @pl.when(jnp.logical_not(hit))
        def _():
            eh_ref[all_rows, :] = jnp.zeros((block, quarter), bf16)
            el_ref[all_rows, :] = jnp.zeros((block, quarter), bf16)


def gram_sum(vh, vm, vl):
    s = jnp.concatenate([vh, vm, vl], 0)
    k = vh.shape[0]
    p = dot(s, s, NT)
    r = p[:k] + (p[k : 2 * k] + p[2 * k :])
    return r[:, :k] + (r[:, k : 2 * k] + r[:, 2 * k :])


def gather_into(full_ref, pieces, members):
    _, member = place()
    quarter = pieces[0].shape[1]
    for k, piece in enumerate(pieces):
        q = lax.rem(member - k + members, members)
        full_ref[:, pl.ds(pl.multiple_of(q * quarter, quarter), quarter)] = piece[...]


def put_gram(gram_ref, image, total):
    gram = gram_sum(*split3(image)) / total
    half = gram.shape[0] // 2
    packed = jnp.concatenate([gram[:half], gram[half:]], 1)
    if len(gram_ref.shape) == 2:
        gram_ref[...] = packed
        return
    for n in range(gram_ref.shape[0]):
        gram_ref[n] = packed


def take_gram(terms):
    packed = terms[0][...] + terms[1][...]
    if len(terms) > 2:
        packed = packed + (terms[2][...] + terms[3][...])
    k = packed.shape[1] // 2
    return jnp.concatenate([packed[:, :k], packed[:, k:]], 0)


def join_kernel(members, total, *refs):
    pieces, full_ref, gram_ref = refs[:members], refs[members], refs[members + 1]
    gather_into(full_ref, pieces, members)
    put_gram(gram_ref, full_ref[...], total)


def second_kernel(v_ref, *refs):
    n = len(refs) // 3
    kept, outs = refs[: 2 * n], refs[2 * n :]
    block = v_ref.shape[1] // BLK_DEV
    for i, out_ref in enumerate(outs):
        out_ref[...] = jnp.zeros_like(out_ref)
        for j in range(BLK_DEV):
            here = pl.ds(j * block, block)
            add_product(out_ref, v_ref[:, here], kept[2 * i][here, :], kept[2 * i + 1][here, :])


def factor_inverse(gram, w=8):
    k = gram.shape[0]
    rows = lax.broadcasted_iota(jnp.int32, (k, k), 0)
    cols = lax.broadcasted_iota(jnp.int32, (k, k), 1)
    aug = jnp.concatenate([gram, (rows == cols).astype(f32)], 1)
    tall, wide = 8, 2 * k
    a = [aug[t * tall : (t + 1) * tall, :] for t in range(k // tall)]
    sub = lax.broadcasted_iota(jnp.int32, (tall, wide), 0)
    spread = lambda x: jnp.broadcast_to(x, (tall, wide))
    for start in range(0, k, w):
        t, s = start // tall, start % tall
        r = [spread(a[t][s + i : s + i + 1, :]) for i in range(w)]
        d = [[spread(a[t][s + i : s + i + 1, start + j : start + j + 1]) if j >= i else None for j in range(w)] for i in range(w)]
        later = range(t if s + w < tall else t + 1, len(a))
        c = {u: [spread(a[u][:, start + i : start + i + 1]) for i in range(w)] for u in later}
        l = [[None] * w for _ in range(w)]
        inv = [None] * w
        for i in range(w):
            p = d[i][i]
            for m in range(i):
                p = p - l[i][m] * l[i][m]
            inv[i] = lax.rsqrt(p)
            for j in range(i + 1, w):
                q = d[i][j]
                for m in range(i):
                    q = q - l[i][m] * l[j][m]
                l[j][i] = q * inv[i]
        for i in range(w):
            for m in range(i):
                r[i] = r[i] - l[i][m] * r[m]
            r[i] = r[i] * inv[i]
        for u in later:
            x = c[u]
            for i in range(w):
                for m in range(i):
                    x[i] = x[i] - l[i][m] * x[m]
                x[i] = x[i] * inv[i]
            new = a[u]
            for i in range(w):
                new = new - x[i] * r[i]
            a[u] = new if u > t else jnp.where(sub < s + w, a[u], new)
        for i in range(w):
            a[t] = jnp.where(sub == s + i, r[i], a[t])
    return jnp.concatenate(a, 0)[:, k:]


def factor_kernel(*refs):
    inv_ref = refs[-1]
    inv_ref[...] = factor_inverse(take_gram(refs[:-1]))


def exact(a, b):
    return lax.dot_general(a, b, NN, precision=lax.Precision.HIGHEST, preferred_element_type=f32)


def image_kernel(members, total, inv_ref, *refs):
    pieces, image_ref, gram_ref = refs[:members], refs[members], refs[members + 1]
    gather_into(image_ref, pieces, members)
    image_ref[...] = exact(inv_ref[...], image_ref[...])
    put_gram(gram_ref, image_ref[...], total)


def last_kernel(image_ref, *refs):
    out_ref = refs[-1]
    out_ref[...] = exact(factor_inverse(take_gram(refs[:-1])), image_ref[...])


VM = pl.BlockSpec(memory_space=pltpu.VMEM)
SM = pl.BlockSpec(memory_space=pltpu.SMEM)
HB = pl.BlockSpec(memory_space=pltpu.HBM)


def call(body, specs, outs, name, limit=16, flops=10**9, scratch=()):
    return pl.pallas_call(
        body,
        in_specs=specs,
        out_specs=[VM] * len(outs),
        scratch_shapes=scratch,
        out_shape=[jax.ShapeDtypeStruct(s, t) for s, t in outs],
        compiler_params=pltpu.CompilerParams(vmem_limit_bytes=limit * MB),
        cost_estimate=pl.CostEstimate(flops=flops, bytes_accessed=MB, transcendentals=0),
        name=name,
    )


def shifted(x, axis, by):
    n = lax.axis_size(axis)
    return lax.ppermute(x, axis, [(i, (i + by) % n) for i in range(n)])


def crossed(x):
    n = lax.axis_size("rows")
    return lax.ppermute(x, "rows", [(i, (i + 2 * (i % 2) - 1) % n) for i in range(n)])


def swapped(x):
    return lax.ppermute(x, "rows", [(i, i ^ 1) for i in range(lax.axis_size("rows"))])


NEAR = 8


def far_sets():
    groups, members = lax.axis_size("rows"), lax.axis_size("sub")
    return [[g * members + m for g in range(low, groups, NEAR)] for low in range(NEAR) for m in range(members)]


def exchanged(x, sets):
    return lax.all_to_all(x, ("rows", "sub"), 0, 0, axis_index_groups=sets)


def sum_kernel(gram_ref, out_ref):
    packed = gram_ref[0]
    for n in range(1, gram_ref.shape[0]):
        packed = packed + gram_ref[n]
    out_ref[...] = packed


MASKS = (1, 2, 6, 8, 16, 48)


def pair_sums(total):
    groups = lax.axis_size("rows")
    for mask in MASKS:
        other = lax.ppermute(total, "rows", [(i, i ^ mask) for i in range(groups)])
        if mask == MASKS[-1]:
            return [total, other]
        total = total + other


RING = (4, 2, 6)


def row_sums(gram):
    (total,) = call(sum_kernel, [VM], [(gram.shape[1:], f32)], "sum_z", flops=10**6)(exchanged(gram, far_sets()))
    total = total + swapped(total)
    groups = lax.axis_size("rows")
    return [total] + [lax.ppermute(total, "rows", [(i, i ^ mask) for i in range(groups)]) for mask in RING]


def tie(x, *others):
    return lax.optimization_barrier((x, *others))[0]


def on_device(embeddings, start_vectors, pairs):
    members = lax.axis_size("sub")
    groups = lax.axis_size("rows")
    rows, width = embeddings.shape
    k = start_vectors.shape[1]
    quarter = rows // members
    total = rows * groups
    vt = start_vectors.T
    pairs = pairs.T
    part = ((k, quarter), f32)
    kept = [((rows, quarter), bf16)] * 2
    (mine,) = call(
        cut_kernel, [HB, HB], [((quarter + NOTE, width), f32)], "cut", flops=10**6,
        scratch=[pltpu.VMEM(pairs.shape, jnp.int32), pltpu.SemaphoreType.DMA((2,))])(
        *(pltpu.with_memory_space_constraint(a, pltpu.HBM) for a in (embeddings, pairs)))
    cross = crossed(mine)
    sib = swapped(mine)

    def make(side, message, name):
        acc, *t = call(
            functools.partial(tiles_kernel, members, side), [VM, VM, VM, SM], [part] + kept, name, flops=5 * 10**9,
            scratch=[pltpu.VMEM((quarter, width), bf16)] * 2)(embeddings, vt, message, pairs)
        return acc, t

    acc, own_t = make(OWN, mine, "own_tiles")
    sib_acc, sib_t = make(SIB, sib, "sib_tiles")
    cross_acc, cross_t = make(CROSS, tie(cross, sib_acc), "cross_tiles")
    acc = (acc + swapped(sib_acc)) + crossed(cross_acc)
    pieces = [acc] + [shifted(acc, "sub", s) for s in range(1, members)]
    whole = ((k, rows), f32)
    copies = ((groups // NEAR, k // 2, 2 * k), f32)
    image, gram = call(functools.partial(join_kernel, members, total), [VM] * members, [whole, (copies[0][1:], f32)], "join")(*pieces)
    sib_acc, cross_acc = call(second_kernel, [VM] * 5, [part] * 2, "second_far")(image, *sib_t, *cross_t)
    (acc2,) = call(second_kernel, [VM] * 3, [part], "second_own")(image, *own_t)
    terms = pair_sums(gram)
    acc2 = (acc2 + swapped(sib_acc)) + crossed(cross_acc)
    pieces = [acc2] + [shifted(acc2, "sub", s) for s in range(1, members)]
    (inv,) = call(factor_kernel, [VM] * len(terms), [((k, k), f32)], "factor")(*terms)
    image, gram = call(functools.partial(image_kernel, members, total), [VM] * (1 + members), [whole, copies], "image")(inv, *pieces)
    terms = row_sums(gram)
    (out,) = call(last_kernel, [VM] * (1 + len(terms)), [whole], "last")(image, *terms)
    return out.T


def solution(mesh):
    return jax.shard_map(
        on_device,
        mesh=mesh,
        in_specs=(P("rows", None), P("rows", None), P("rows", None)),
        out_specs=P("rows", None),
        check_vma=False,
    )
```

```python
import functools
import jax
import jax.numpy as jnp
from jax import lax
from jax.experimental import pallas as pl
from jax.experimental.pallas import tpu as pltpu
from jax.sharding import PartitionSpec as P

BLK_DEV = 2
OWN, SIB, CROSS = 0, 1, -1
NOTE = 8
MB = 1024 * 1024
LOG2E = 1.4426950408889634
SCALE = LOG2E / 64.0

f32 = jnp.float32
bf16 = jnp.bfloat16
NN = (((1,), (0,)), ((), ()))
NT = (((1,), (1,)), ((), ()))


def dot(a, b, dims):
    return lax.dot_general(a, b, dims, preferred_element_type=f32)


def split2(x):
    hi = x.astype(bf16)
    return hi, (x - hi.astype(f32)).astype(bf16)


def split3(x):
    hi = x.astype(bf16)
    rest = x - hi.astype(f32)
    mid = rest.astype(bf16)
    return hi, mid, (rest - mid.astype(f32)).astype(bf16)


def listed(pairs_ref, row_block, col_block):
    hit = jnp.int32(0)
    for slot in range(pairs_ref.shape[1]):
        same = (pairs_ref[0, slot] == row_block) & (pairs_ref[1, slot] == col_block)
        hit = hit | same.astype(jnp.int32)
    return hit > 0


def place():
    group = lax.axis_index("rows")
    member = lax.axis_index("sub")
    return group, member


def want(pairs_ref, note_ref, members, side, j):
    group, member = place()
    mine = group * BLK_DEV + j
    other = (group + side * (1 - 2 * (group & 1))) * BLK_DEV + (member * BLK_DEV) // members
    low, high = jnp.minimum(mine, other), jnp.maximum(mine, other)
    slot = lax.broadcasted_iota(jnp.int32, (1, note_ref.shape[1]), 1) < pairs_ref.shape[1]
    same = slot & (note_ref[0:1, :] == low.astype(f32)) & (note_ref[1:2, :] == high.astype(f32))
    return listed(pairs_ref, low, high) | (jnp.max(same.astype(f32)) > 0.5)


def add_product(acc_ref, v, eh, el):
    vh, vm, vl = split3(v)
    k = vh.shape[0]
    one = dot(jnp.concatenate([vh, vm, vl], 0), eh, NN)
    two = dot(jnp.concatenate([vh, vm], 0), el, NN)
    acc_ref[...] += (one[:k] + two[:k]) + (one[k : 2 * k] + two[k:] + one[2 * k :])


def cut_kernel(x_ref, pairs_ref, out_ref, list_ref, sems):
    _, member = place()
    quarter = out_ref.shape[0] - NOTE
    source = x_ref.at[pl.ds(pl.multiple_of(member * quarter, quarter), quarter)]
    copies = [
        pltpu.make_async_copy(source, out_ref.at[pl.ds(0, quarter)], sems.at[0]),
        pltpu.make_async_copy(pairs_ref, list_ref, sems.at[1]),
    ]
    for copy in copies:
        copy.start()
    copies[1].wait()
    count, slots = list_ref.shape
    out_ref[quarter:, :] = jnp.zeros((NOTE, out_ref.shape[1]), f32)
    out_ref[quarter : quarter + count, :slots] = list_ref[...].astype(f32)
    copies[0].wait()


def tiles_kernel(members, side, x_ref, v_ref, message_ref, pairs_ref, acc_ref, eh_ref, el_ref, xah_ref, xal_ref, chunk=256):
    quarter = message_ref.shape[0] - NOTE
    block = x_ref.shape[0] // BLK_DEV
    xa = message_ref[:quarter, :]
    ones = jnp.ones((8, xa.shape[1]), f32)
    na = lax.dot_general(ones, xa * xa, NT, precision=lax.Precision.HIGHEST, preferred_element_type=f32)[0:1, :] * SCALE
    xah_ref[...], xal_ref[...] = split2(xa * (2.0 * SCALE))
    acc_ref[...] = jnp.zeros_like(acc_ref)
    for j in range(BLK_DEV):
        hit = want(pairs_ref, message_ref.at[quarter:], members, side, j)
        all_rows = pl.ds(j * block, block)

        @pl.when(hit)
        def _():
            xah, xal = xah_ref[...], xal_ref[...]
            for c in range(block // chunk):
                here = pl.ds(j * block + c * chunk, chunk)
                x = x_ref[here, :]
                nb = jnp.sum(x * x, axis=1, keepdims=True) * SCALE
                xh, xl = split2(x)
                d = dot(xh, xah, NT) + (dot(xh, xal, NT) + dot(xl, xah, NT))
                e = jnp.exp2(jnp.minimum(d - nb - na, 0.0))
                eh_ref[here, :], el_ref[here, :] = split2(e)
            add_product(acc_ref, v_ref[:, all_rows], eh_ref[all_rows, :], el_ref[all_rows, :])

        @pl.when(jnp.logical_not(hit))
        def _():
            eh_ref[all_rows, :] = jnp.zeros((block, quarter), bf16)
            el_ref[all_rows, :] = jnp.zeros((block, quarter), bf16)


def gram_sum(vh, vm, vl):
    s = jnp.concatenate([vh, vm, vl], 0)
    k = vh.shape[0]
    p = dot(s, s, NT)
    r = p[:k] + (p[k : 2 * k] + p[2 * k :])
    return r[:, :k] + (r[:, k : 2 * k] + r[:, 2 * k :])


def gather_into(full_ref, pieces, members):
    _, member = place()
    quarter = pieces[0].shape[1]
    for k, piece in enumerate(pieces):
        q = lax.rem(member - k + members, members)
        full_ref[:, pl.ds(pl.multiple_of(q * quarter, quarter), quarter)] = piece[...]


def put_gram(gram_ref, image, total):
    gram = gram_sum(*split3(image)) / total
    half = gram.shape[0] // 2
    packed = jnp.concatenate([gram[:half], gram[half:]], 1)
    if len(gram_ref.shape) == 2:
        gram_ref[...] = packed
        return
    for n in range(gram_ref.shape[0]):
        gram_ref[n] = packed


def take_gram(terms):
    packed = terms[0][...] + terms[1][...]
    if len(terms) > 2:
        packed = packed + (terms[2][...] + terms[3][...])
    k = packed.shape[1] // 2
    return jnp.concatenate([packed[:, :k], packed[:, k:]], 0)


def join_kernel(members, total, *refs):
    pieces, full_ref, gram_ref = refs[:members], refs[members], refs[members + 1]
    gather_into(full_ref, pieces, members)
    put_gram(gram_ref, full_ref[...], total)


def second_kernel(v_ref, *refs):
    n = len(refs) // 3
    kept, outs = refs[: 2 * n], refs[2 * n :]
    block = v_ref.shape[1] // BLK_DEV
    for i, out_ref in enumerate(outs):
        out_ref[...] = jnp.zeros_like(out_ref)
        for j in range(BLK_DEV):
            here = pl.ds(j * block, block)
            add_product(out_ref, v_ref[:, here], kept[2 * i][here, :], kept[2 * i + 1][here, :])


def factor_inverse(gram, w=8):
    k = gram.shape[0]
    rows = lax.broadcasted_iota(jnp.int32, (k, k), 0)
    cols = lax.broadcasted_iota(jnp.int32, (k, k), 1)
    aug = jnp.concatenate([gram, (rows == cols).astype(f32)], 1)
    tall, wide = 8, 2 * k
    a = [aug[t * tall : (t + 1) * tall, :] for t in range(k // tall)]
    sub = lax.broadcasted_iota(jnp.int32, (tall, wide), 0)
    spread = lambda x: jnp.broadcast_to(x, (tall, wide))
    for start in range(0, k, w):
        t, s = start // tall, start % tall
        r = [spread(a[t][s + i : s + i + 1, :]) for i in range(w)]
        d = [[spread(a[t][s + i : s + i + 1, start + j : start + j + 1]) if j >= i else None for j in range(w)] for i in range(w)]
        later = range(t if s + w < tall else t + 1, len(a))
        c = {u: [spread(a[u][:, start + i : start + i + 1]) for i in range(w)] for u in later}
        l = [[None] * w for _ in range(w)]
        inv = [None] * w
        for i in range(w):
            p = d[i][i]
            for m in range(i):
                p = p - l[i][m] * l[i][m]
            inv[i] = lax.rsqrt(p)
            for j in range(i + 1, w):
                q = d[i][j]
                for m in range(i):
                    q = q - l[i][m] * l[j][m]
                l[j][i] = q * inv[i]
        for i in range(w):
            for m in range(i):
                r[i] = r[i] - l[i][m] * r[m]
            r[i] = r[i] * inv[i]
        for u in later:
            x = c[u]
            for i in range(w):
                for m in range(i):
                    x[i] = x[i] - l[i][m] * x[m]
                x[i] = x[i] * inv[i]
            new = a[u]
            for i in range(w):
                new = new - x[i] * r[i]
            a[u] = new if u > t else jnp.where(sub < s + w, a[u], new)
        for i in range(w):
            a[t] = jnp.where(sub == s + i, r[i], a[t])
    return jnp.concatenate(a, 0)[:, k:]


def factor_kernel(*refs):
    inv_ref = refs[-1]
    inv_ref[...] = factor_inverse(take_gram(refs[:-1]))


def exact(a, b):
    return lax.dot_general(a, b, NN, precision=lax.Precision.HIGHEST, preferred_element_type=f32)


def image_kernel(members, total, inv_ref, *refs):
    pieces, image_ref, gram_ref = refs[:members], refs[members], refs[members + 1]
    gather_into(image_ref, pieces, members)
    image_ref[...] = exact(inv_ref[...], image_ref[...])
    put_gram(gram_ref, image_ref[...], total)


def last_kernel(image_ref, *refs):
    out_ref = refs[-1]
    out_ref[...] = exact(factor_inverse(take_gram(refs[:-1])), image_ref[...])


VM = pl.BlockSpec(memory_space=pltpu.VMEM)
SM = pl.BlockSpec(memory_space=pltpu.SMEM)
HB = pl.BlockSpec(memory_space=pltpu.HBM)


def call(body, specs, outs, name, limit=16, flops=10**9, scratch=()):
    return pl.pallas_call(
        body,
        in_specs=specs,
        out_specs=[VM] * len(outs),
        scratch_shapes=scratch,
        out_shape=[jax.ShapeDtypeStruct(s, t) for s, t in outs],
        compiler_params=pltpu.CompilerParams(vmem_limit_bytes=limit * MB),
        cost_estimate=pl.CostEstimate(flops=flops, bytes_accessed=MB, transcendentals=0),
        name=name,
    )


def shifted(x, axis, by):
    n = lax.axis_size(axis)
    return lax.ppermute(x, axis, [(i, (i + by) % n) for i in range(n)])


def crossed(x):
    n = lax.axis_size("rows")
    return lax.ppermute(x, "rows", [(i, (i + 2 * (i % 2) - 1) % n) for i in range(n)])


def swapped(x):
    return lax.ppermute(x, "rows", [(i, i ^ 1) for i in range(lax.axis_size("rows"))])


NEAR = 8


def far_sets():
    groups, members = lax.axis_size("rows"), lax.axis_size("sub")
    return [[g * members + m for g in range(low, groups, NEAR)] for low in range(NEAR) for m in range(members)]


def exchanged(x, sets):
    return lax.all_to_all(x, ("rows", "sub"), 0, 0, axis_index_groups=sets)


def sum_kernel(gram_ref, out_ref):
    packed = gram_ref[0]
    for n in range(1, gram_ref.shape[0]):
        packed = packed + gram_ref[n]
    out_ref[...] = packed


MASKS = (1, 2, 6, 8, 16, 48)


def pair_sums(total):
    groups = lax.axis_size("rows")
    sums = [total]
    for mask in MASKS:
        other = lax.ppermute(sums[-1], "rows", [(i, i ^ mask) for i in range(groups)])
        sums.append(other if mask == MASKS[-1] else sums[-1] + other)
    return sums


RING = (4, 2, 6)


def row_sums(gram):
    (total,) = call(sum_kernel, [VM], [(gram.shape[1:], f32)], "sum_z", flops=10**6)(exchanged(gram, far_sets()))
    total = total + swapped(total)
    groups = lax.axis_size("rows")
    return [total] + [lax.ppermute(total, "rows", [(i, i ^ mask) for i in range(groups)]) for mask in RING]


def tie(x, *others):
    return lax.optimization_barrier((x, *others))[0]


def on_device(embeddings, start_vectors, pairs):
    members = lax.axis_size("sub")
    groups = lax.axis_size("rows")
    rows, width = embeddings.shape
    k = start_vectors.shape[1]
    quarter = rows // members
    total = rows * groups
    vt = start_vectors.T
    pairs = pairs.T
    part = ((k, quarter), f32)
    kept = [((rows, quarter), bf16)] * 2
    (mine,) = call(
        cut_kernel, [HB, HB], [((quarter + NOTE, width), f32)], "cut", flops=10**6,
        scratch=[pltpu.VMEM(pairs.shape, jnp.int32), pltpu.SemaphoreType.DMA((2,))])(
        *(pltpu.with_memory_space_constraint(a, pltpu.HBM) for a in (embeddings, pairs)))
    cross = crossed(mine)
    sib = swapped(mine)

    def make(side, message, name):
        acc, *t = call(
            functools.partial(tiles_kernel, members, side), [VM, VM, VM, SM], [part] + kept, name, flops=5 * 10**9,
            scratch=[pltpu.VMEM((quarter, width), bf16)] * 2)(embeddings, vt, message, pairs)
        return acc, t

    acc, own_t = make(OWN, mine, "own_tiles")
    sib_acc, sib_t = make(SIB, sib, "sib_tiles")
    cross_acc, cross_t = make(CROSS, tie(cross, sib_acc), "cross_tiles")
    acc = (acc + swapped(sib_acc)) + crossed(cross_acc)
    pieces = [acc] + [shifted(acc, "sub", s) for s in range(1, members)]
    whole = ((k, rows), f32)
    copies = ((groups // NEAR, k // 2, 2 * k), f32)
    image, gram = call(functools.partial(join_kernel, members, total), [VM] * members, [whole, (copies[0][1:], f32)], "join")(*pieces)
    sums = pair_sums(gram)
    terms = sums[-2:]
    sib_acc, cross_acc = call(second_kernel, [VM] * 5, [part] * 2, "second_far")(tie(image, sums[1]), *sib_t, *cross_t)
    (acc2,) = call(second_kernel, [VM] * 3, [part], "second_own")(tie(image, sums[2]), *own_t)
    acc2 = (acc2 + swapped(tie(sib_acc, sums[2]))) + crossed(tie(cross_acc, sums[2]))
    pieces = [acc2] + [shifted(acc2, "sub", s) for s in range(1, members)]
    (inv,) = call(factor_kernel, [VM] * len(terms), [((k, k), f32)], "factor")(*terms)
    image, gram = call(functools.partial(image_kernel, members, total), [VM] * (1 + members), [whole, copies], "image")(inv, *pieces)
    terms = row_sums(gram)
    (out,) = call(last_kernel, [VM] * (1 + len(terms)), [whole], "last")(image, *terms)
    return out.T


def solution(mesh):
    return jax.shard_map(
        on_device,
        mesh=mesh,
        in_specs=(P("rows", None), P("rows", None), P("rows", None)),
        out_specs=P("rows", None),
        check_vma=False,
    )
```

```python
import functools
import jax
import jax.numpy as jnp
from jax import lax
from jax.experimental import pallas as pl
from jax.experimental.pallas import tpu as pltpu
from jax.sharding import PartitionSpec as P

BLK_DEV = 2
OWN, SIB, CROSS = 0, 1, -1
NOTE = 8
MB = 1024 * 1024
LOG2E = 1.4426950408889634
SCALE = LOG2E / 64.0

f32 = jnp.float32
bf16 = jnp.bfloat16
NN = (((1,), (0,)), ((), ()))
NT = (((1,), (1,)), ((), ()))


def dot(a, b, dims):
    return lax.dot_general(a, b, dims, preferred_element_type=f32)


def split2(x):
    hi = x.astype(bf16)
    return hi, (x - hi.astype(f32)).astype(bf16)


def split3(x):
    hi = x.astype(bf16)
    rest = x - hi.astype(f32)
    mid = rest.astype(bf16)
    return hi, mid, (rest - mid.astype(f32)).astype(bf16)


def listed(pairs_ref, row_block, col_block):
    hit = jnp.int32(0)
    for slot in range(pairs_ref.shape[1]):
        same = (pairs_ref[0, slot] == row_block) & (pairs_ref[1, slot] == col_block)
        hit = hit | same.astype(jnp.int32)
    return hit > 0


def place():
    group = lax.axis_index("rows")
    member = lax.axis_index("sub")
    return group, member


def want(pairs_ref, note_ref, members, side, j):
    group, member = place()
    mine = group * BLK_DEV + j
    other = (group + side * (1 - 2 * (group & 1))) * BLK_DEV + (member * BLK_DEV) // members
    low, high = jnp.minimum(mine, other), jnp.maximum(mine, other)
    slot = lax.broadcasted_iota(jnp.int32, (1, note_ref.shape[1]), 1) < pairs_ref.shape[1]
    same = slot & (note_ref[0:1, :] == low.astype(f32)) & (note_ref[1:2, :] == high.astype(f32))
    return listed(pairs_ref, low, high) | (jnp.max(same.astype(f32)) > 0.5)


def add_product(acc_ref, v, eh, el):
    vh, vm, vl = split3(v)
    k = vh.shape[0]
    one = dot(jnp.concatenate([vh, vm, vl], 0), eh, NN)
    two = dot(jnp.concatenate([vh, vm], 0), el, NN)
    acc_ref[...] += (one[:k] + two[:k]) + (one[k : 2 * k] + two[k:] + one[2 * k :])


def cut_kernel(x_ref, pairs_ref, out_ref, list_ref, sems):
    _, member = place()
    quarter = out_ref.shape[0] - NOTE
    source = x_ref.at[pl.ds(pl.multiple_of(member * quarter, quarter), quarter)]
    copies = [
        pltpu.make_async_copy(source, out_ref.at[pl.ds(0, quarter)], sems.at[0]),
        pltpu.make_async_copy(pairs_ref, list_ref, sems.at[1]),
    ]
    for copy in copies:
        copy.start()
    copies[1].wait()
    count, slots = list_ref.shape
    out_ref[quarter:, :] = jnp.zeros((NOTE, out_ref.shape[1]), f32)
    out_ref[quarter : quarter + count, :slots] = list_ref[...].astype(f32)
    copies[0].wait()


def tiles_kernel(members, side, x_ref, v_ref, message_ref, pairs_ref, acc_ref, eh_ref, el_ref, xah_ref, xal_ref, chunk=256):
    quarter = message_ref.shape[0] - NOTE
    block = x_ref.shape[0] // BLK_DEV
    xa = message_ref[:quarter, :]
    ones = jnp.ones((8, xa.shape[1]), f32)
    na = lax.dot_general(ones, xa * xa, NT, precision=lax.Precision.HIGHEST, preferred_element_type=f32)[0:1, :] * SCALE
    xah_ref[...], xal_ref[...] = split2(xa * (2.0 * SCALE))
    acc_ref[...] = jnp.zeros_like(acc_ref)
    for j in range(BLK_DEV):
        hit = want(pairs_ref, message_ref.at[quarter:], members, side, j)
        all_rows = pl.ds(j * block, block)

        @pl.when(hit)
        def _():
            xah, xal = xah_ref[...], xal_ref[...]
            for c in range(block // chunk):
                here = pl.ds(j * block + c * chunk, chunk)
                x = x_ref[here, :]
                nb = jnp.sum(x * x, axis=1, keepdims=True) * SCALE
                xh, xl = split2(x)
                d = dot(xh, xah, NT) + (dot(xh, xal, NT) + dot(xl, xah, NT))
                e = jnp.exp2(jnp.minimum(d - nb - na, 0.0))
                eh_ref[here, :], el_ref[here, :] = split2(e)
            add_product(acc_ref, v_ref[:, all_rows], eh_ref[all_rows, :], el_ref[all_rows, :])

        @pl.when(jnp.logical_not(hit))
        def _():
            eh_ref[all_rows, :] = jnp.zeros((block, quarter), bf16)
            el_ref[all_rows, :] = jnp.zeros((block, quarter), bf16)


def gram_sum(vh, vm, vl):
    s = jnp.concatenate([vh, vm, vl], 0)
    k = vh.shape[0]
    p = dot(s, s, NT)
    r = p[:k] + (p[k : 2 * k] + p[2 * k :])
    return r[:, :k] + (r[:, k : 2 * k] + r[:, 2 * k :])


def gather_into(full_ref, pieces, members):
    _, member = place()
    quarter = pieces[0].shape[1]
    for k, piece in enumerate(pieces):
        q = lax.rem(member - k + members, members)
        full_ref[:, pl.ds(pl.multiple_of(q * quarter, quarter), quarter)] = piece[...]


def put_gram(gram_ref, image, total):
    gram = gram_sum(*split3(image)) / total
    half = gram.shape[0] // 2
    gram_ref[...] = jnp.concatenate([gram[:half], gram[half:]], 1)


def take_gram(terms):
    packed = terms[0]
    for term in terms[1:]:
        packed = packed + term
    k = packed.shape[1] // 2
    return jnp.concatenate([packed[:, :k], packed[:, k:]], 0)


def join_kernel(members, total, *refs):
    pieces, full_ref, gram_ref = refs[:members], refs[members], refs[members + 1]
    gather_into(full_ref, pieces, members)
    put_gram(gram_ref, full_ref[...], total)


def second_kernel(v_ref, *refs):
    n = len(refs) // 3
    kept, outs = refs[: 2 * n], refs[2 * n :]
    block = v_ref.shape[1] // BLK_DEV
    for i, out_ref in enumerate(outs):
        out_ref[...] = jnp.zeros_like(out_ref)
        for j in range(BLK_DEV):
            here = pl.ds(j * block, block)
            add_product(out_ref, v_ref[:, here], kept[2 * i][here, :], kept[2 * i + 1][here, :])


def factor_inverse(gram, w=8):
    k = gram.shape[0]
    rows = lax.broadcasted_iota(jnp.int32, (k, k), 0)
    cols = lax.broadcasted_iota(jnp.int32, (k, k), 1)
    aug = jnp.concatenate([gram, (rows == cols).astype(f32)], 1)
    tall, wide = 8, 2 * k
    a = [aug[t * tall : (t + 1) * tall, :] for t in range(k // tall)]
    sub = lax.broadcasted_iota(jnp.int32, (tall, wide), 0)
    spread = lambda x: jnp.broadcast_to(x, (tall, wide))
    for start in range(0, k, w):
        t, s = start // tall, start % tall
        r = [spread(a[t][s + i : s + i + 1, :]) for i in range(w)]
        d = [[spread(a[t][s + i : s + i + 1, start + j : start + j + 1]) if j >= i else None for j in range(w)] for i in range(w)]
        later = range(t if s + w < tall else t + 1, len(a))
        c = {u: [spread(a[u][:, start + i : start + i + 1]) for i in range(w)] for u in later}
        l = [[None] * w for _ in range(w)]
        inv = [None] * w
        for i in range(w):
            p = d[i][i]
            for m in range(i):
                p = p - l[i][m] * l[i][m]
            inv[i] = lax.rsqrt(p)
            for j in range(i + 1, w):
                q = d[i][j]
                for m in range(i):
                    q = q - l[i][m] * l[j][m]
                l[j][i] = q * inv[i]
        for i in range(w):
            for m in range(i):
                r[i] = r[i] - l[i][m] * r[m]
            r[i] = r[i] * inv[i]
        for u in later:
            x = c[u]
            for i in range(w):
                for m in range(i):
                    x[i] = x[i] - l[i][m] * x[m]
                x[i] = x[i] * inv[i]
            new = a[u]
            for i in range(w):
                new = new - x[i] * r[i]
            a[u] = new if u > t else jnp.where(sub < s + w, a[u], new)
        for i in range(w):
            a[t] = jnp.where(sub == s + i, r[i], a[t])
    return jnp.concatenate(a, 0)[:, k:]


def factor_kernel(*refs):
    inv_ref = refs[-1]
    inv_ref[...] = factor_inverse(take_gram([ref[...] for ref in refs[:-1]]))


def exact(a, b):
    return lax.dot_general(a, b, NN, precision=lax.Precision.HIGHEST, preferred_element_type=f32)


def image_kernel(members, total, inv_ref, *refs):
    pieces, image_ref, gram_ref = refs[:members], refs[members], refs[members + 1]
    gather_into(image_ref, pieces, members)
    image_ref[...] = exact(inv_ref[...], image_ref[...])
    put_gram(gram_ref, image_ref[...], total)


def last_kernel(image_ref, gram_ref, out_ref):
    gram = take_gram([gram_ref[n] for n in range(gram_ref.shape[0])])
    out_ref[...] = exact(factor_inverse(gram), image_ref[...])


VM = pl.BlockSpec(memory_space=pltpu.VMEM)
SM = pl.BlockSpec(memory_space=pltpu.SMEM)
HB = pl.BlockSpec(memory_space=pltpu.HBM)


def call(body, specs, outs, name, limit=16, flops=10**9, scratch=()):
    return pl.pallas_call(
        body,
        in_specs=specs,
        out_specs=[VM] * len(outs),
        scratch_shapes=scratch,
        out_shape=[jax.ShapeDtypeStruct(s, t) for s, t in outs],
        compiler_params=pltpu.CompilerParams(vmem_limit_bytes=limit * MB),
        cost_estimate=pl.CostEstimate(flops=flops, bytes_accessed=MB, transcendentals=0),
        name=name,
    )


def shifted(x, axis, by):
    n = lax.axis_size(axis)
    return lax.ppermute(x, axis, [(i, (i + by) % n) for i in range(n)])


def crossed(x):
    n = lax.axis_size("rows")
    return lax.ppermute(x, "rows", [(i, (i + 2 * (i % 2) - 1) % n) for i in range(n)])


def swapped(x):
    return lax.ppermute(x, "rows", [(i, i ^ 1) for i in range(lax.axis_size("rows"))])


NEAR = 8


def far_sets():
    groups, members = lax.axis_size("rows"), lax.axis_size("sub")
    return [[g * members + m for g in range(low, groups, NEAR)] for low in range(NEAR) for m in range(members)]


def exchanged(x, sets):
    return lax.all_to_all(x, ("rows", "sub"), 0, 0, axis_index_groups=sets)


def spread_kernel(me_ref, opposite_ref, left_ref, right_ref, out_ref):
    packed = (me_ref[...] + opposite_ref[...]) + (left_ref[...] + right_ref[...])
    for n in range(out_ref.shape[0]):
        out_ref[n] = packed


MASKS = (1, 2, 6, 8, 16, 48)


def pair_sums(total):
    groups = lax.axis_size("rows")
    sums = [total]
    for mask in MASKS:
        other = lax.ppermute(sums[-1], "rows", [(i, i ^ mask) for i in range(groups)])
        sums.append(other if mask == MASKS[-1] else sums[-1] + other)
    return sums


RING = (4, 2, 6)


def row_sums(gram):
    groups = lax.axis_size("rows")
    total = gram + swapped(gram)
    terms = [total] + [lax.ppermute(total, "rows", [(i, i ^ mask) for i in range(groups)]) for mask in RING]
    (spread,) = call(spread_kernel, [VM] * len(terms), [((groups // NEAR, *gram.shape), f32)], "sum_x", flops=10**6)(*terms)
    return exchanged(spread, far_sets())


def tie(x, *others):
    return lax.optimization_barrier((x, *others))[0]


def on_device(embeddings, start_vectors, pairs):
    members = lax.axis_size("sub")
    groups = lax.axis_size("rows")
    rows, width = embeddings.shape
    k = start_vectors.shape[1]
    quarter = rows // members
    total = rows * groups
    vt = start_vectors.T
    pairs = pairs.T
    part = ((k, quarter), f32)
    kept = [((rows, quarter), bf16)] * 2
    (mine,) = call(
        cut_kernel, [HB, HB], [((quarter + NOTE, width), f32)], "cut", flops=10**6,
        scratch=[pltpu.VMEM(pairs.shape, jnp.int32), pltpu.SemaphoreType.DMA((2,))])(
        *(pltpu.with_memory_space_constraint(a, pltpu.HBM) for a in (embeddings, pairs)))
    cross = crossed(mine)
    sib = swapped(mine)

    def make(side, message, name):
        acc, *t = call(
            functools.partial(tiles_kernel, members, side), [VM, VM, VM, SM], [part] + kept, name, flops=5 * 10**9,
            scratch=[pltpu.VMEM((quarter, width), bf16)] * 2)(embeddings, vt, message, pairs)
        return acc, t

    acc, own_t = make(OWN, mine, "own_tiles")
    sib_acc, sib_t = make(SIB, sib, "sib_tiles")
    cross_acc, cross_t = make(CROSS, tie(cross, sib_acc), "cross_tiles")
    acc = (acc + swapped(sib_acc)) + crossed(cross_acc)
    pieces = [acc] + [shifted(acc, "sub", s) for s in range(1, members)]
    whole = ((k, rows), f32)
    packed = ((k // 2, 2 * k), f32)
    image, gram = call(functools.partial(join_kernel, members, total), [VM] * members, [whole, packed], "join")(*pieces)
    sums = pair_sums(gram)
    terms = sums[-2:]
    sib_acc, cross_acc = call(second_kernel, [VM] * 5, [part] * 2, "second_far")(tie(image, sums[1]), *sib_t, *cross_t)
    (acc2,) = call(second_kernel, [VM] * 3, [part], "second_own")(tie(image, sums[2]), *own_t)
    acc2 = (acc2 + swapped(tie(sib_acc, sums[2]))) + crossed(tie(cross_acc, sums[2]))
    pieces = [acc2] + [shifted(acc2, "sub", s) for s in range(1, members)]
    (inv,) = call(factor_kernel, [VM] * len(terms), [((k, k), f32)], "factor")(*terms)
    image, gram = call(functools.partial(image_kernel, members, total), [VM] * (1 + members), [whole, packed], "image")(inv, *pieces)
    (out,) = call(last_kernel, [VM, VM], [whole], "last")(image, row_sums(gram))
    return out.T


def solution(mesh):
    return jax.shard_map(
        on_device,
        mesh=mesh,
        in_specs=(P("rows", None), P("rows", None), P("rows", None)),
        out_specs=P("rows", None),
        check_vma=False,
    )
```

```python
import functools
import jax
import jax.numpy as jnp
from jax import lax
from jax.experimental import pallas as pl
from jax.experimental.pallas import tpu as pltpu
from jax.sharding import PartitionSpec as P

BLK_DEV = 2
OWN, SIB, CROSS = 0, 1, -1
NOTE = 8
MB = 1024 * 1024
LOG2E = 1.4426950408889634
SCALE = LOG2E / 64.0

f32 = jnp.float32
bf16 = jnp.bfloat16
NN = (((1,), (0,)), ((), ()))
NT = (((1,), (1,)), ((), ()))


def dot(a, b, dims):
    return lax.dot_general(a, b, dims, preferred_element_type=f32)


def split2(x):
    hi = x.astype(bf16)
    return hi, (x - hi.astype(f32)).astype(bf16)


def split3(x):
    hi = x.astype(bf16)
    rest = x - hi.astype(f32)
    mid = rest.astype(bf16)
    return hi, mid, (rest - mid.astype(f32)).astype(bf16)


def listed(pairs_ref, row_block, col_block):
    hit = jnp.int32(0)
    for slot in range(pairs_ref.shape[1]):
        same = (pairs_ref[0, slot] == row_block) & (pairs_ref[1, slot] == col_block)
        hit = hit | same.astype(jnp.int32)
    return hit > 0


def place():
    group = lax.axis_index("rows")
    member = lax.axis_index("sub")
    return group, member


def want(pairs_ref, note_ref, members, side, j):
    group, member = place()
    mine = group * BLK_DEV + j
    other = (group + side * (1 - 2 * (group & 1))) * BLK_DEV + (member * BLK_DEV) // members
    low, high = jnp.minimum(mine, other), jnp.maximum(mine, other)
    slot = lax.broadcasted_iota(jnp.int32, (1, note_ref.shape[1]), 1) < pairs_ref.shape[1]
    same = slot & (note_ref[0:1, :] == low.astype(f32)) & (note_ref[1:2, :] == high.astype(f32))
    return listed(pairs_ref, low, high) | (jnp.max(same.astype(f32)) > 0.5)


def add_product(acc_ref, v, eh, el):
    vh, vm, vl = split3(v)
    k = vh.shape[0]
    one = dot(jnp.concatenate([vh, vm, vl], 0), eh, NN)
    two = dot(jnp.concatenate([vh, vm], 0), el, NN)
    acc_ref[...] += (one[:k] + two[:k]) + (one[k : 2 * k] + two[k:] + one[2 * k :])


def cut_kernel(x_ref, pairs_ref, out_ref, list_ref, sems):
    _, member = place()
    quarter = out_ref.shape[0] - NOTE
    source = x_ref.at[pl.ds(pl.multiple_of(member * quarter, quarter), quarter)]
    copies = [
        pltpu.make_async_copy(source, out_ref.at[pl.ds(0, quarter)], sems.at[0]),
        pltpu.make_async_copy(pairs_ref, list_ref, sems.at[1]),
    ]
    for copy in copies:
        copy.start()
    copies[1].wait()
    count, slots = list_ref.shape
    out_ref[quarter:, :] = jnp.zeros((NOTE, out_ref.shape[1]), f32)
    out_ref[quarter : quarter + count, :slots] = list_ref[...].astype(f32)
    copies[0].wait()


def tiles_kernel(members, side, blocks, x_ref, v_ref, message_ref, pairs_ref, acc_ref, eh_ref, el_ref, xah_ref, xal_ref, chunk=256):
    quarter = message_ref.shape[0] - NOTE
    block = x_ref.shape[0] // BLK_DEV
    xa = message_ref[:quarter, :]
    ones = jnp.ones((8, xa.shape[1]), f32)
    na = lax.dot_general(ones, xa * xa, NT, precision=lax.Precision.HIGHEST, preferred_element_type=f32)[0:1, :] * SCALE
    xah_ref[...], xal_ref[...] = split2(xa * (2.0 * SCALE))
    acc_ref[...] = jnp.zeros_like(acc_ref)
    for i, j in enumerate(blocks):
        hit = want(pairs_ref, message_ref.at[quarter:], members, side, j)
        all_rows = pl.ds(i * block, block)
        v_rows = pl.ds(j * block, block)

        @pl.when(hit)
        def _():
            xah, xal = xah_ref[...], xal_ref[...]
            for c in range(block // chunk):
                here = pl.ds(i * block + c * chunk, chunk)
                x = x_ref[pl.ds(j * block + c * chunk, chunk), :]
                nb = jnp.sum(x * x, axis=1, keepdims=True) * SCALE
                xh, xl = split2(x)
                d = dot(xh, xah, NT) + (dot(xh, xal, NT) + dot(xl, xah, NT))
                e = jnp.exp2(jnp.minimum(d - nb - na, 0.0))
                eh_ref[here, :], el_ref[here, :] = split2(e)
            add_product(acc_ref, v_ref[:, v_rows], eh_ref[all_rows, :], el_ref[all_rows, :])

        @pl.when(jnp.logical_not(hit))
        def _():
            eh_ref[all_rows, :] = jnp.zeros((block, quarter), bf16)
            el_ref[all_rows, :] = jnp.zeros((block, quarter), bf16)


def gram_sum(vh, vm, vl):
    s = jnp.concatenate([vh, vm, vl], 0)
    k = vh.shape[0]
    p = dot(s, s, NT)
    r = p[:k] + (p[k : 2 * k] + p[2 * k :])
    return r[:, :k] + (r[:, k : 2 * k] + r[:, 2 * k :])


def gather_into(full_ref, pieces, members):
    _, member = place()
    quarter = pieces[0].shape[1]
    for k, piece in enumerate(pieces):
        q = lax.rem(member - k + members, members)
        full_ref[:, pl.ds(pl.multiple_of(q * quarter, quarter), quarter)] = piece[...]


def put_gram(gram_ref, image, total):
    gram = gram_sum(*split3(image)) / total
    half = gram.shape[0] // 2
    gram_ref[...] = jnp.concatenate([gram[:half], gram[half:]], 1)


def take_gram(terms):
    packed = terms[0]
    for term in terms[1:]:
        packed = packed + term
    k = packed.shape[1] // 2
    return jnp.concatenate([packed[:, :k], packed[:, k:]], 0)


def join_kernel(members, total, *refs):
    pieces, full_ref, gram_ref = refs[:members], refs[members], refs[members + 1]
    gather_into(full_ref, pieces, members)
    put_gram(gram_ref, full_ref[...], total)


def second_kernel(v_ref, *refs):
    n = len(refs) // 3
    kept, outs = refs[: 2 * n], refs[2 * n :]
    block = v_ref.shape[1] // BLK_DEV
    for i, out_ref in enumerate(outs):
        out_ref[...] = jnp.zeros_like(out_ref)
        for j in range(BLK_DEV):
            here = pl.ds(j * block, block)
            add_product(out_ref, v_ref[:, here], kept[2 * i][here, :], kept[2 * i + 1][here, :])


def second_own_kernel(v_ref, *refs):
    kept, out_ref = refs[:-1], refs[-1]
    out_ref[...] = jnp.zeros_like(out_ref)
    block = kept[0].shape[0]
    for j in range(len(kept) // 2):
        add_product(out_ref, v_ref[:, pl.ds(j * block, block)], kept[2 * j][...], kept[2 * j + 1][...])


def factor_inverse(gram, w=8):
    k = gram.shape[0]
    rows = lax.broadcasted_iota(jnp.int32, (k, k), 0)
    cols = lax.broadcasted_iota(jnp.int32, (k, k), 1)
    aug = jnp.concatenate([gram, (rows == cols).astype(f32)], 1)
    tall, wide = 8, 2 * k
    a = [aug[t * tall : (t + 1) * tall, :] for t in range(k // tall)]
    sub = lax.broadcasted_iota(jnp.int32, (tall, wide), 0)
    spread = lambda x: jnp.broadcast_to(x, (tall, wide))
    for start in range(0, k, w):
        t, s = start // tall, start % tall
        r = [spread(a[t][s + i : s + i + 1, :]) for i in range(w)]
        d = [[spread(a[t][s + i : s + i + 1, start + j : start + j + 1]) if j >= i else None for j in range(w)] for i in range(w)]
        later = range(t if s + w < tall else t + 1, len(a))
        c = {u: [spread(a[u][:, start + i : start + i + 1]) for i in range(w)] for u in later}
        l = [[None] * w for _ in range(w)]
        inv = [None] * w
        for i in range(w):
            p = d[i][i]
            for m in range(i):
                p = p - l[i][m] * l[i][m]
            inv[i] = lax.rsqrt(p)
            for j in range(i + 1, w):
                q = d[i][j]
                for m in range(i):
                    q = q - l[i][m] * l[j][m]
                l[j][i] = q * inv[i]
        for i in range(w):
            for m in range(i):
                r[i] = r[i] - l[i][m] * r[m]
            r[i] = r[i] * inv[i]
        for u in later:
            x = c[u]
            for i in range(w):
                for m in range(i):
                    x[i] = x[i] - l[i][m] * x[m]
                x[i] = x[i] * inv[i]
            new = a[u]
            for i in range(w):
                new = new - x[i] * r[i]
            a[u] = new if u > t else jnp.where(sub < s + w, a[u], new)
        for i in range(w):
            a[t] = jnp.where(sub == s + i, r[i], a[t])
    return jnp.concatenate(a, 0)[:, k:]


def factor_kernel(*refs):
    inv_ref = refs[-1]
    inv_ref[...] = factor_inverse(take_gram([ref[...] for ref in refs[:-1]]))


def exact(a, b):
    return lax.dot_general(a, b, NN, precision=lax.Precision.HIGHEST, preferred_element_type=f32)


def image_kernel(members, total, inv_ref, *refs):
    pieces, image_ref, gram_ref = refs[:members], refs[members], refs[members + 1]
    gather_into(image_ref, pieces, members)
    image_ref[...] = exact(inv_ref[...], image_ref[...])
    put_gram(gram_ref, image_ref[...], total)


def last_kernel(image_ref, gram_ref, out_ref):
    gram = take_gram([gram_ref[n] for n in range(gram_ref.shape[0])])
    out_ref[...] = exact(factor_inverse(gram), image_ref[...])


VM = pl.BlockSpec(memory_space=pltpu.VMEM)
SM = pl.BlockSpec(memory_space=pltpu.SMEM)
HB = pl.BlockSpec(memory_space=pltpu.HBM)


def call(body, specs, outs, name, limit=16, flops=10**9, scratch=()):
    return pl.pallas_call(
        body,
        in_specs=specs,
        out_specs=[VM] * len(outs),
        scratch_shapes=scratch,
        out_shape=[jax.ShapeDtypeStruct(s, t) for s, t in outs],
        compiler_params=pltpu.CompilerParams(vmem_limit_bytes=limit * MB),
        cost_estimate=pl.CostEstimate(flops=flops, bytes_accessed=MB, transcendentals=0),
        name=name,
    )


def shifted(x, axis, by):
    n = lax.axis_size(axis)
    return lax.ppermute(x, axis, [(i, (i + by) % n) for i in range(n)])


def crossed(x):
    n = lax.axis_size("rows")
    return lax.ppermute(x, "rows", [(i, (i + 2 * (i % 2) - 1) % n) for i in range(n)])


def swapped(x):
    return lax.ppermute(x, "rows", [(i, i ^ 1) for i in range(lax.axis_size("rows"))])


NEAR = 8


def far_sets():
    groups, members = lax.axis_size("rows"), lax.axis_size("sub")
    return [[g * members + m for g in range(low, groups, NEAR)] for low in range(NEAR) for m in range(members)]


def exchanged(x, sets):
    return lax.all_to_all(x, ("rows", "sub"), 0, 0, axis_index_groups=sets)


def spread_kernel(me_ref, opposite_ref, left_ref, right_ref, out_ref):
    packed = (me_ref[...] + opposite_ref[...]) + (left_ref[...] + right_ref[...])
    for n in range(out_ref.shape[0]):
        out_ref[n] = packed


MASKS = (1, 2, 6, 8, 16, 48)


def pair_sums(total):
    groups = lax.axis_size("rows")
    sums = [total]
    for mask in MASKS:
        other = lax.ppermute(sums[-1], "rows", [(i, i ^ mask) for i in range(groups)])
        sums.append(other if mask == MASKS[-1] else sums[-1] + other)
    return sums


RING = (4, 2, 6)


def row_sums(gram):
    groups = lax.axis_size("rows")
    total = gram + swapped(gram)
    terms = [total] + [lax.ppermute(total, "rows", [(i, i ^ mask) for i in range(groups)]) for mask in RING]
    (spread,) = call(spread_kernel, [VM] * len(terms), [((groups // NEAR, *gram.shape), f32)], "sum_x", flops=10**6)(*terms)
    return exchanged(spread, far_sets())


def tie(x, *others):
    return lax.optimization_barrier((x, *others))[0]


def on_device(embeddings, start_vectors, pairs):
    members = lax.axis_size("sub")
    groups = lax.axis_size("rows")
    rows, width = embeddings.shape
    k = start_vectors.shape[1]
    quarter = rows // members
    total = rows * groups
    vt = start_vectors.T
    pairs = pairs.T
    part = ((k, quarter), f32)
    (mine,) = call(
        cut_kernel, [HB, HB], [((quarter + NOTE, width), f32)], "cut", flops=10**6,
        scratch=[pltpu.VMEM(pairs.shape, jnp.int32), pltpu.SemaphoreType.DMA((2,))])(
        *(pltpu.with_memory_space_constraint(a, pltpu.HBM) for a in (embeddings, pairs)))
    cross = crossed(mine)
    sib = swapped(mine)

    every = tuple(range(BLK_DEV))

    def make(side, message, name, blocks=every):
        kept = [((rows * len(blocks) // BLK_DEV, quarter), bf16)] * 2
        acc, *t = call(
            functools.partial(tiles_kernel, members, side, blocks), [VM, VM, VM, SM], [part] + kept, name, flops=5 * 10**9,
            scratch=[pltpu.VMEM((quarter, width), bf16)] * 2)(embeddings, vt, message, pairs)
        return acc, t

    sib_acc, sib_t = make(SIB, sib, "sib_tiles")
    acc, own_t = make(OWN, tie(mine, sib_acc), "own_tiles", every[:1])
    cross_acc, cross_t = make(CROSS, tie(cross, acc), "cross_tiles")
    more, t = make(OWN, mine, "own_tiles", every[1:])
    acc = acc + more
    own_t += t
    acc = (acc + swapped(sib_acc)) + crossed(cross_acc)
    pieces = [acc] + [shifted(acc, "sub", s) for s in range(1, members)]
    whole = ((k, rows), f32)
    packed = ((k // 2, 2 * k), f32)
    image, gram = call(functools.partial(join_kernel, members, total), [VM] * members, [whole, packed], "join")(*pieces)
    sums = pair_sums(gram)
    terms = sums[-2:]
    sib_acc, cross_acc = call(second_kernel, [VM] * 5, [part] * 2, "second_far")(tie(image, sums[1]), *sib_t, *cross_t)
    (acc2,) = call(second_own_kernel, [VM] * 5, [part], "second_own")(tie(image, sums[2]), *own_t)
    acc2 = (acc2 + swapped(tie(sib_acc, sums[2]))) + crossed(tie(cross_acc, sums[2]))
    pieces = [acc2] + [shifted(acc2, "sub", s) for s in range(1, members)]
    (inv,) = call(factor_kernel, [VM] * len(terms), [((k, k), f32)], "factor")(*terms)
    image, gram = call(functools.partial(image_kernel, members, total), [VM] * (1 + members), [whole, packed], "image")(inv, *pieces)
    (out,) = call(last_kernel, [VM, VM], [whole], "last")(image, row_sums(gram))
    return out.T


def solution(mesh):
    return jax.shard_map(
        on_device,
        mesh=mesh,
        in_specs=(P("rows", None), P("rows", None), P("rows", None)),
        out_specs=P("rows", None),
        check_vma=False,
    )
```
